32 devices in a mesh: dp: 8 (over z, core), tensor: 4 (over y, x).
Axes of the slice: x: 2, y: 2, z: 4, core: 2. Of those that a mesh axis runs over, the one named last changes fastest.
Arguments:
- inputs: bfloat16 [8192, 2048], P(('dp', 'tensor')), may hold values from -6 to 6
- cotangent: bfloat16 [8192, 2048], P(('dp', 'tensor')), may hold values from -6 to 6
- lengths: int32 [8], P('dp'), may hold values from 256 to 1024, as said below
- norm_gain: float32 [2048], replicated, may hold values from 0.1 to 1.9
- w_query: float32 [2048, 2048], P('dp', 'tensor'), may hold values from -0.125 to 0.125
- w_key: float32 [2048, 2048], P('dp', 'tensor'), may hold values from -0.125 to 0.125
- w_value: float32 [2048, 2048], P('dp', 'tensor'), may hold values from -0.125 to 0.125
- w_gate_out: float32 [2048, 2048], P('dp', 'tensor'), may hold values from -0.125 to 0.125
- w_beta: float32 [2048, 16], P('dp', 'tensor'), may hold values from -0.125 to 0.125
- conv_weight: float32 [3, 4, 2048], P(None, None, 'tensor'), may hold values from -3 to 3
- out_norm_gain: float32 [128], replicated, may hold values from 0.1 to 1.9
- w_output: float32 [2048, 2048], P('tensor', 'dp'), may hold values from -0.125 to 0.125
- ffn_norm_gain: float32 [2048], replicated, may hold values from 0.1 to 1.9
- w_gate: float32 [2048, 5632], P('dp', 'tensor'), may hold values from -0.125 to 0.125
- w_up: float32 [2048, 5632], P('dp', 'tensor'), may hold values from -0.125 to 0.125
- w_down: float32 [5632, 2048], P('tensor', 'dp'), may hold values from -0.078125 to 0.078125
Outputs:
- output: bfloat16 [8192, 2048], P(('dp', 'tensor'))
- input_grad: float32 [8192, 2048], P(('dp', 'tensor'))
- norm_gain_grad: float32 [2048], replicated
- w_query_grad: float32 [2048, 2048], P('dp', 'tensor')
- w_key_grad: float32 [2048, 2048], P('dp', 'tensor')
- w_value_grad: float32 [2048, 2048], P('dp', 'tensor')
- w_gate_out_grad: float32 [2048, 2048], P('dp', 'tensor')
- w_beta_grad: float32 [2048, 16], P('dp', 'tensor')
- conv_weight_grad: float32 [3, 4, 2048], P(None, None, 'tensor')
- out_norm_gain_grad: float32 [128], replicated
- w_output_grad: float32 [2048, 2048], P('tensor', 'dp')
- ffn_norm_gain_grad: float32 [2048], replicated
- w_gate_grad: float32 [2048, 5632], P('dp', 'tensor')
- w_up_grad: float32 [2048, 5632], P('dp', 'tensor')
- w_down_grad: float32 [5632, 2048], P('tensor', 'dp')
The draws below stay inside these ranges and needn't reach their ends.
Inputs may be any that keep to these rules, and one draw needn't show every extreme that they name: `lengths`: each entry is the number of valid tokens at the start of its sequence of 1024 slots; the rest is padding. In every draw some sequence is full.
All inputs are finite; a program needn't handle non-finite values.
Results may differ from the reference program's by a relative error of at most 0.02.
Values may be sent and summed in bfloat16 or wider, within the bound.
A program may use at most 320 MiB of HBM per device.

```python
import jax
import jax.numpy as jnp
from jax import lax

D = 2048
H = 16
DK = 128
FF = 5632
CONV = 4
GROUP = 64
SEQ = 1024
SEQS = 8
TOKENS = 8192


def draw_lengths(key, part):
    key = jax.random.fold_in(key, 11)
    first_key, second_key = jax.random.split(key)
    drawn = jax.random.randint(first_key, (SEQS,), SEQ // 4, SEQ + 1)
    chosen = jax.random.randint(second_key, (), 0, SEQS)
    return jnp.where(jnp.arange(SEQS) == chosen, SEQ, drawn).astype(jnp.int32)


def strengthened(values, rng, source, target, parts, factor):
    owner, partner = [(jnp.arange(values.shape[axis_at]) // (values.shape[axis_at] // parts)).reshape([-1 if axis == axis_at else 1 for axis in range(values.ndim)]) for axis_at in (source, target)]
    chosen = jax.random.permutation(rng, parts)[partner]
    strong = (owner == chosen) | (owner == (partner + parts // 2) % parts)
    return jnp.where(strong, factor * values, values)


def levels(key, extent, cuts, least, largest):
    loudness = 1.0
    for dim, parts in cuts:
        heights = jax.random.uniform(jax.random.fold_in(jax.random.fold_in(key, 6), dim), (parts,), jnp.float32, least / len(cuts), largest / len(cuts))
        loudness = loudness * jnp.repeat(jnp.exp(heights), extent[dim] // parts).reshape((-1,) + (1,) * (len(extent) - 1 - dim))
    return loudness


def bell_draw(key, shape, spread, bound, cuts=(), kind=jnp.bfloat16):
    values = spread * jax.random.normal(key, shape, jnp.float32)
    if cuts:
        values = values * levels(key, shape, cuts, -0.22, 0.18)
    return jnp.clip(values, -bound, bound).astype(kind)


def gaussian_with(stream_key, shape, spread, reach, cuts, heavy, held_as=jnp.bfloat16):
    values = spread * jax.random.normal(stream_key, shape, jnp.float32)
    if cuts:
        values = values * levels(stream_key, shape, cuts, -0.22, 0.18)
    return jnp.clip(strengthened(values, jax.random.fold_in(stream_key, 3), *heavy), -reach, reach).astype(held_as)


def setup_inputs(seed: int = 0) -> dict:
    key_list = jax.random.split(jax.random.key(seed), 17)
    return {
        "inputs": bell_draw(key_list[0], (TOKENS, D), 1.0, 6.0, ((0, 32),)),
        "cotangent": gaussian_with(key_list[1], (TOKENS, D), 1.0, 6.0, ((0, 32),), (0, 1, 32, 2.75)),
        "lengths": draw_lengths(jax.random.fold_in(key_list[16], 71), 0),
        "norm_gain": jnp.clip(1.0 + 0.18 * jax.random.normal(key_list[3], (D,), jnp.float32), 0.1, 1.9),
        "w_query": bell_draw(key_list[4], (D, D), D ** -0.5, 0.125, ((0, 8), (1, 4)), jnp.float32),
        "w_key": bell_draw(key_list[5], (D, D), D ** -0.5, 0.125, ((0, 8), (1, 4)), jnp.float32),
        "w_value": bell_draw(key_list[6], (D, D), D ** -0.5, 0.125, ((0, 8), (1, 4)), jnp.float32),
        "w_gate_out": bell_draw(key_list[7], (D, D), D ** -0.5, 0.125, ((0, 8), (1, 4)), jnp.float32),
        "w_beta": bell_draw(key_list[8], (D, H), D ** -0.5, 0.125, ((0, 8), (1, 4)), jnp.float32),
        "conv_weight": bell_draw(key_list[9], (3, CONV, D), CONV ** -0.5, 3.0, ((2, 4),), jnp.float32),
        "out_norm_gain": jnp.clip(1.0 + 0.18 * jax.random.normal(key_list[10], (DK,), jnp.float32), 0.1, 1.9),
        "w_output": bell_draw(key_list[11], (D, D), D ** -0.5, 0.125, ((0, 4), (1, 8)), jnp.float32),
        "ffn_norm_gain": jnp.clip(1.0 + 0.18 * jax.random.normal(key_list[12], (D,), jnp.float32), 0.1, 1.9),
        "w_gate": bell_draw(key_list[13], (D, FF), D ** -0.5, 0.125, ((0, 8), (1, 4)), jnp.float32),
        "w_up": bell_draw(key_list[14], (D, FF), D ** -0.5, 0.125, ((0, 8), (1, 4)), jnp.float32),
        "w_down": bell_draw(key_list[15], (FF, D), FF ** -0.5, 0.078125, ((0, 4), (1, 8)), jnp.float32),
    }


norm_epsilon = 1e-06
head_epsilon = 1e-05
highest_precision = lax.Precision.HIGHEST

@jax.custom_vjp
def low(v):
    return lax.optimization_barrier(v.astype(jnp.bfloat16)).astype(jnp.float32)

@jax.custom_vjp
def low_back(v):
    return v

def low_keep(v):
    return (low(v), None)

def low_pass(kept, grad):
    return (grad,)

def back_keep(v):
    return (v, None)

def back_low(kept, grad):
    return (low(grad),)
low.defvjp(low_keep, low_pass)
low_back.defvjp(back_keep, back_low)

def rms_norm(values, gain):
    return values * lax.rsqrt(lax.optimization_barrier(jnp.mean(values * values, axis=-1, keepdims=True)) + norm_epsilon) * gain

def short_conv(signal, taps):
    width = taps.shape[0]
    length = signal.shape[0]
    padded = jnp.pad(signal, ((width - 1, 0), (0, 0)))
    total = taps[0] * padded[0:length]
    for offset in range(1, width):
        total = total + taps[offset] * padded[offset:offset + length]
    return total

def unit_rows(values):
    return values * lax.rsqrt(lax.optimization_barrier(jnp.sum(values * values, axis=-1, keepdims=True)) + norm_epsilon)

def delta_rule(query, keys, values, beta):
    length, heads, head_size = query.shape
    blocks = length // GROUP

    def to_blocks(array):
        return array.reshape(blocks, GROUP, heads, array.shape[-1]).transpose(0, 2, 1, 3)
    query_blocks = to_blocks(query)
    key_blocks = to_blocks(keys)
    value_blocks = to_blocks(values)
    beta_blocks = beta.reshape(blocks, GROUP, heads).transpose(0, 2, 1)
    strict_lower = jnp.tril(jnp.ones((GROUP, GROUP), jnp.float32), -1)
    with_diagonal = jnp.tril(jnp.ones((GROUP, GROUP), jnp.float32))
    identity = jnp.eye(GROUP, dtype=jnp.float32)

    def block_step(state, block):
        query_block, key_block, value_block, beta_block = block
        gram = jnp.einsum('hcd,hed->hce', key_block, key_block, precision=highest_precision)
        system = identity + gram * beta_block[:, :, None] * strict_lower
        stacked = jnp.concatenate([key_block * beta_block[:, :, None], value_block * beta_block[:, :, None]], axis=-1)
        solved = lax.linalg.triangular_solve(system, stacked, left_side=True, lower=True, unit_diagonal=True)
        weights_part = solved[..., :head_size]
        update_part = solved[..., head_size:]
        fresh = update_part - jnp.einsum('hcd,hde->hce', weights_part, state, precision=highest_precision)
        scores = jnp.einsum('hcd,hed->hce', query_block, key_block, precision=highest_precision) * with_diagonal
        result = jnp.einsum('hcd,hde->hce', query_block, state, precision=highest_precision)
        result = result + jnp.einsum('hce,hef->hcf', scores, fresh, precision=highest_precision)
        state = state + jnp.einsum('hcd,hce->hde', key_block, fresh, precision=highest_precision)
        return (state, result)
    start_state = jnp.zeros((heads, head_size, head_size), jnp.float32)
    end_state, results = lax.scan(jax.checkpoint(block_step), start_state, (query_blocks, key_blocks, value_blocks, beta_blocks))
    return results.transpose(0, 2, 1, 3).reshape(length, heads, head_size)

def mix_sequence(q_pre, k_pre, v_pre, gate_pre, beta_pre, conv_taps, head_gain):
    length, width = q_pre.shape
    head_size = head_gain.shape[0]
    heads = width // head_size
    query = jax.nn.silu(short_conv(q_pre, conv_taps[0])).reshape(length, heads, head_size)
    keys = jax.nn.silu(short_conv(k_pre, conv_taps[1])).reshape(length, heads, head_size)
    values = jax.nn.silu(short_conv(v_pre, conv_taps[2])).reshape(length, heads, head_size)
    query = unit_rows(query) * head_size ** (-0.5)
    keys = unit_rows(keys)
    beta = jax.nn.sigmoid(beta_pre)
    mixed = delta_rule(query, keys, values, beta)
    normed = mixed * lax.rsqrt(lax.optimization_barrier(jnp.mean(mixed * mixed, axis=-1, keepdims=True)) + head_epsilon) * head_gain
    gated = normed * jax.nn.silu(gate_pre.reshape(length, heads, head_size))
    return gated.reshape(length, width)

def matmul(left, right):
    return jnp.dot(left, right, precision=highest_precision)

def layer(features, params, mask):
    norm_gain, w_query, w_key, w_value, w_gate_out, w_beta, conv_weight, out_norm_gain, w_output, ffn_norm_gain, w_gate, w_up, w_down = params
    normed = low(rms_norm(features, norm_gain))
    q_pre = low_back(matmul(normed, low(w_query)))
    k_pre = low_back(matmul(normed, low(w_key)))
    v_pre = low_back(matmul(normed, low(w_value)))
    gate_pre = low_back(matmul(normed, low(w_gate_out)))
    beta_pre = low_back(matmul(normed, low(w_beta)))
    mixed = mix_sequence(q_pre, k_pre, v_pre, gate_pre, beta_pre, conv_weight, out_norm_gain)
    branch = low_back(matmul(low(mixed), low(w_output)))
    resid = features + branch
    normed2 = low(rms_norm(resid, ffn_norm_gain))
    gate = low_back(matmul(normed2, low(w_gate)))
    up_part = low_back(matmul(normed2, low(w_up)))
    middle = low(jax.nn.silu(gate) * up_part)
    result = resid + low_back(matmul(middle, low(w_down)))
    return result * mask[:, None]

def reference(inputs, cotangent, lengths, norm_gain, w_query, w_key, w_value, w_gate_out, w_beta, conv_weight, out_norm_gain, w_output, ffn_norm_gain, w_gate, w_up, w_down):
    params = (norm_gain, w_query, w_key, w_value, w_gate_out, w_beta, conv_weight, out_norm_gain, w_output, ffn_norm_gain, w_gate, w_up, w_down)
    count = inputs.shape[0] // SEQ
    width = inputs.shape[1]
    seq_inputs = inputs.astype(jnp.float32).reshape(count, SEQ, width)
    seq_cotangent = cotangent.astype(jnp.float32).reshape(count, SEQ, width)
    positions = jnp.arange(SEQ, dtype=jnp.int32)

    def one_sequence(totals, item):
        features, seq_grad, length = item
        mask = (positions < length).astype(jnp.float32)

        def forward(feat, prm):
            return layer(feat, prm, mask)
        result, pull = jax.vjp(forward, features, params)
        feat_grad, param_grads = pull(seq_grad)
        totals = jax.tree.map(jnp.add, totals, param_grads)
        return (totals, (result, feat_grad))
    start = jax.tree.map(jnp.zeros_like, params)
    grads, (results, feat_grads) = lax.scan(one_sequence, start, (seq_inputs, seq_cotangent, lengths))
    output = results.reshape(count * SEQ, width).astype(jnp.bfloat16)
    input_grad = feat_grads.reshape(count * SEQ, width)
    return (output, input_grad, grads[0], grads[1], grads[2], grads[3], grads[4], grads[5], grads[6], grads[7], grads[8], grads[9], grads[10], grads[11], grads[12])
```

```python
import functools
import jax
import jax.numpy as jnp
from jax import lax
from jax.experimental import pallas as pl
from jax.experimental.pallas import tpu as pltpu
from jax.sharding import PartitionSpec as P

norm_epsilon = 1e-06
head_epsilon = 1e-05
HEAD = 128
CHUNK = 128
STEP = 256
TAPS = 4
BETA_PAD = 128
VMEM_LIMIT = 56 * 1024 * 1024
f32 = jnp.float32
bf16 = jnp.bfloat16


def mm(a, b):
    return lax.dot_general(a, b, (((1,), (0,)), ((), ())), preferred_element_type=f32)


def mm_nt(a, b):
    return lax.dot_general(a, b, (((1,), (1,)), ((), ())), preferred_element_type=f32)


def mm_tn(a, b):
    return lax.dot_general(a, b, (((0,), (0,)), ((), ())), preferred_element_type=f32)


def chunk_indices():
    row = lax.broadcasted_iota(jnp.int32, (CHUNK, CHUNK), 0)
    col = lax.broadcasted_iota(jnp.int32, (CHUNK, CHUNK), 1)
    return row, col


def unit_lower_inverses(stricts, row, col):
    apart = row ^ col
    inverses = [jnp.where(row == col, 1.0, jnp.where(apart == 1, -strict, 0.0)) for strict in stricts]
    span = 2
    while span < CHUNK:
        here = (apart >= span) & (apart < 2 * span)
        lows = [inverse.astype(bf16) for inverse in inverses]
        firsts = [mm(low, jnp.where(here, strict, 0.0).astype(bf16)).astype(bf16) for low, strict in zip(lows, stricts)]
        inverses = [inverse - mm(first, low) for inverse, first, low in zip(inverses, firsts, lows)]
        span *= 2
    return [inverse.astype(bf16) for inverse in inverses]


def silu_parts(conv):
    sig = jax.nn.sigmoid(conv)
    return conv * sig, sig


def forward_kernel(
    heads, pre_ref, taps_ref, gain_ref, z_ref, conv_ref, mixed_ref, inv_ref, state_ref, hist, state
):
    step = pl.program_id(0)
    width = heads * HEAD
    rows = pre_ref.shape[0]

    @pl.when(step == 0)
    def _():
        hist[0:8, :] = jnp.zeros((8, 3 * width), f32)
        state[...] = jnp.zeros_like(state)

    @pl.when(step > 0)
    def _():
        hist[0:8, :] = hist[rows : rows + 8, :]

    hist[8 : 8 + rows, :] = pre_ref[:, 0 : 3 * width].astype(f32)
    row, col = chunk_indices()
    beta_all = jax.nn.sigmoid(pre_ref[:, 4 * width : 4 * width + BETA_PAD].astype(f32))
    work = []
    for head in range(heads):
        parts = []
        for kind in range(3):
            lanes = slice(kind * width + head * HEAD, kind * width + (head + 1) * HEAD)
            total = taps_ref[kind * TAPS : kind * TAPS + 1, head * HEAD : (head + 1) * HEAD] * hist[5 : 5 + rows, lanes]
            for tap in range(1, TAPS):
                total = total + taps_ref[
                    kind * TAPS + tap : kind * TAPS + tap + 1, head * HEAD : (head + 1) * HEAD
                ] * hist[5 + tap : 5 + tap + rows, lanes]
            conv_ref[:, lanes] = total
            act, _ = silu_parts(total)
            if kind < 2:
                act = act * lax.rsqrt(jnp.sum(act * act, axis=-1, keepdims=True) + norm_epsilon)
            if kind == 0:
                act = act * HEAD ** (-0.5)
            parts.append(act)
        beta = beta_all[:, head : head + 1]
        for part in range(rows // CHUNK):
            here = slice(part * CHUNK, (part + 1) * CHUNK)
            query, key, value = (p[here] for p in parts)
            query_low, key_low = query.astype(bf16), key.astype(bf16)
            b = beta[here]
            stacked = jnp.concatenate([(b * key).astype(bf16), (b * value).astype(bf16)], axis=1)
            strict = jnp.where(row > col, b * mm_nt(key_low, key_low), 0.0)
            scores = jnp.where(row >= col, mm_nt(query_low, key_low), 0.0).astype(bf16)
            work.append((head, part, query_low, key_low, stacked, scores, strict))
    inverses = unit_lower_inverses([item[-1] for item in work], row, col)
    solved_all = {}
    for (head, part, query_low, key_low, stacked, scores, _), inverse in zip(work, inverses):
        inv_ref[head, part] = inverse
        solved_all[part, head] = (query_low, key_low, scores, mm(inverse, stacked))
    states = [state[head] for head in range(heads)]
    for part in range(rows // CHUNK):
        here = slice(part * CHUNK, (part + 1) * CHUNK)
        enters = [enter.astype(bf16) for enter in states]
        items = [solved_all[part, head] for head in range(heads)]
        freshes = [
            (solved[:, HEAD:] - mm(solved[:, :HEAD].astype(bf16), enter)).astype(bf16)
            for (_, _, _, solved), enter in zip(items, enters)
        ]
        states = [old + mm_tn(key_low, fresh) for old, (_, key_low, _, _), fresh in zip(states, items, freshes)]
        for head in range(heads):
            lanes = slice(head * HEAD, (head + 1) * HEAD)
            query_low, _, scores, _ = items[head]
            state_ref[head, part] = enters[head]
            mixed = mm(query_low, enters[head]) + mm(scores, freshes[head])
            mixed_ref[here, lanes] = mixed
            gate = pre_ref[here, 3 * width + head * HEAD : 3 * width + (head + 1) * HEAD].astype(f32)
            gate_act, _ = silu_parts(gate)
            normed = mixed * lax.rsqrt(jnp.mean(mixed * mixed, axis=-1, keepdims=True) + head_epsilon)
            z_ref[here, lanes] = (normed * gain_ref[...] * gate_act).astype(bf16)
    for head in range(heads):
        state[head] = states[head]


def mixer_forward(pre, taps, gain, heads):
    length, total = pre.shape
    width = heads * HEAD
    steps, parts = length // STEP, STEP // CHUNK
    return pl.pallas_call(
        functools.partial(forward_kernel, heads),
        grid=(steps,),
        in_specs=[
            pl.BlockSpec((STEP, total), lambda i: (i, 0)),
            pl.BlockSpec((3 * TAPS, width), lambda i: (0, 0)),
            pl.BlockSpec((1, HEAD), lambda i: (0, 0)),
        ],
        out_specs=[
            pl.BlockSpec((STEP, width), lambda i: (i, 0)),
            pl.BlockSpec((STEP, 3 * width), lambda i: (i, 0)),
            pl.BlockSpec((STEP, width), lambda i: (i, 0)),
            pl.BlockSpec((heads, parts, CHUNK, CHUNK), lambda i: (0, i, 0, 0)),
            pl.BlockSpec((heads, parts, HEAD, HEAD), lambda i: (0, i, 0, 0)),
        ],
        out_shape=[
            jax.ShapeDtypeStruct((length, width), bf16),
            jax.ShapeDtypeStruct((length, 3 * width), f32),
            jax.ShapeDtypeStruct((length, width), f32),
            jax.ShapeDtypeStruct((heads, steps * parts, CHUNK, CHUNK), bf16),
            jax.ShapeDtypeStruct((heads, steps * parts, HEAD, HEAD), bf16),
        ],
        scratch_shapes=[
            pltpu.VMEM((STEP + 8, 3 * width), f32),
            pltpu.VMEM((heads, HEAD, HEAD), f32),
        ],
        compiler_params=pltpu.CompilerParams(
            dimension_semantics=("arbitrary",), vmem_limit_bytes=VMEM_LIMIT
        ),
        cost_estimate=pl.CostEstimate(
            flops=2 * length * width * HEAD * 60, bytes_accessed=length * (total * 4 + width * 24), transcendentals=length * width * 8
        ),
    )(pre, taps, gain)


def backward_kernel(
    heads,
    pre_ref,
    conv_ref,
    mixed_ref,
    dz_ref,
    inv_ref,
    state_ref,
    taps_ref,
    gain_ref,
    dpre_ref,
    dtaps_ref,
    dgain_ref,
    later,
    dstate,
):
    step = pl.program_id(0)
    width = heads * HEAD
    rows = pre_ref.shape[0]
    count = rows // CHUNK

    @pl.when(step == 0)
    def _():
        later[rows : rows + 8, :] = jnp.zeros((8, 3 * width), f32)
        dstate[...] = jnp.zeros_like(dstate)
        dtaps_ref[...] = jnp.zeros_like(dtaps_ref)
        dgain_ref[...] = jnp.zeros_like(dgain_ref)

    @pl.when(step > 0)
    def _():
        later[rows : rows + 8, :] = later[0:8, :]

    row, col = chunk_indices()
    beta_all = jax.nn.sigmoid(pre_ref[:, 4 * width : 4 * width + BETA_PAD].astype(f32))
    beta_lane = lax.broadcasted_iota(jnp.int32, (CHUNK, BETA_PAD), 1)
    dbeta_all = [jnp.zeros((CHUNK, BETA_PAD), f32) for _ in range(count)]
    dgain = jnp.zeros((1, HEAD), f32)
    gain = gain_ref[...]
    every = [(part, head) for part in reversed(range(count)) for head in range(heads)]

    def of(ref, kind, at):
        part, head = at
        lanes = slice(kind * width + head * HEAD, kind * width + (head + 1) * HEAD)
        return ref[part * CHUNK : (part + 1) * CHUNK, lanes].astype(f32)

    betas = {(part, head): beta_all[part * CHUNK : (part + 1) * CHUNK, head : head + 1] for part, head in every}
    unit_queries, keys, query_lows, key_lows, scales, stacks = {}, {}, {}, {}, {}, {}
    for at in every:
        acts = [silu_parts(of(conv_ref, kind, at))[0] for kind in range(3)]
        scales[at] = [lax.rsqrt(jnp.sum(act * act, axis=-1, keepdims=True) + norm_epsilon) for act in acts[:2]]
        unit_queries[at], keys[at] = acts[0] * scales[at][0], acts[1] * scales[at][1]
        query_lows[at] = (unit_queries[at] * HEAD ** (-0.5)).astype(bf16)
        key_lows[at] = keys[at].astype(bf16)
        stacks[at] = jnp.concatenate([(betas[at] * keys[at]).astype(bf16), (betas[at] * acts[2]).astype(bf16)], axis=1)
    solved = {at: mm(inv_ref[at[1], at[0]], stacks[at]) for at in every}
    scores = {at: jnp.where(row >= col, mm_nt(query_lows[at], key_lows[at]), 0.0).astype(bf16) for at in every}
    weights = {at: solved[at][:, :HEAD].astype(bf16) for at in every}
    outs = {}
    for at in every:
        part, head = at
        here = slice(part * CHUNK, (part + 1) * CHUNK)
        gate = of(pre_ref, 3, at)
        gate_act, gate_sig = silu_parts(gate)
        mixed, dz = of(mixed_ref, 0, at), of(dz_ref, 0, at)
        root = lax.rsqrt(jnp.mean(mixed * mixed, axis=-1, keepdims=True) + head_epsilon)
        normed = mixed * root
        dgate = dz * normed * gain * (gate_sig * (1.0 + gate * (1.0 - gate_sig)))
        dpre_ref[here, 3 * width + head * HEAD : 3 * width + (head + 1) * HEAD] = dgate.astype(bf16)
        dgained = dz * gate_act
        dgain = dgain + jnp.sum(dgained * normed, axis=0, keepdims=True)
        dnormed = dgained * gain
        dmixed = root * (dnormed - normed * jnp.mean(dnormed * normed, axis=-1, keepdims=True))
        outs[at] = dmixed.astype(bf16)
    enters = {(part, head): state_ref[head, part] for part, head in every}
    fresh = {at: (solved[at][:, HEAD:] - mm(weights[at], enters[at])).astype(bf16) for at in every}
    within = {at: mm_tn(scores[at], outs[at]) for at in every}
    across = {at: mm_tn(query_lows[at], outs[at]) for at in every}
    leavings, dfresh = {}, {}
    states = [dstate[head] for head in range(heads)]
    for part in reversed(range(count)):
        for head in range(heads):
            leavings[part, head] = states[head].astype(bf16)
        for head in range(heads):
            at = (part, head)
            dfresh[at] = (within[at] + mm(key_lows[at], leavings[at])).astype(bf16)
        for head in range(heads):
            at = (part, head)
            states[head] = states[head] + across[at] - mm_tn(weights[at], dfresh[at])
    for head in range(heads):
        dstate[head] = states[head]
    dscores = {at: jnp.where(row >= col, mm_nt(outs[at], fresh[at]), 0.0).astype(bf16) for at in every}
    dweights = {at: (-mm_nt(dfresh[at], enters[at])).astype(bf16) for at in every}
    dxys = {
        at: mm_tn(inv_ref[at[1], at[0]], jnp.concatenate([dweights[at], dfresh[at]], axis=1)) for at in every
    }
    dqueries = {at: mm_nt(outs[at], enters[at]) + mm(dscores[at], key_lows[at]) for at in every}
    dkeys = {at: mm_tn(dscores[at], query_lows[at]) + mm_nt(fresh[at], leavings[at]) for at in every}
    dsystems = {
        at: jnp.where(row > col, -mm_nt(dxys[at].astype(bf16), solved[at].astype(bf16)), 0.0) for at in every
    }
    dsystem_lows = {at: dsystems[at].astype(bf16) for at in every}
    firsts = {at: mm(dsystem_lows[at], key_lows[at]) for at in every}
    seconds = {at: mm_tn(dsystem_lows[at], stacks[at][:, :HEAD]) for at in every}
    grams = {at: mm_nt(key_lows[at], key_lows[at]) for at in every}
    for at in every:
        part, head = at
        beta, dx, dy, key = betas[at], dxys[at][:, :HEAD], dxys[at][:, HEAD:], keys[at]
        dkey = dkeys[at] + beta * (firsts[at] + dx) + seconds[at]
        convs = [of(conv_ref, kind, at) for kind in range(3)]
        sigs = [jax.nn.sigmoid(conv) for conv in convs]
        dbeta = jnp.sum(dsystems[at] * grams[at] + dx * key + dy * (convs[2] * sigs[2]), axis=-1, keepdims=True)
        dbeta = dbeta * beta * (1.0 - beta)
        dbeta_all[part] = jnp.where(beta_lane == head, dbeta, dbeta_all[part])
        unit_query, dquery = unit_queries[at], dqueries[at] * HEAD ** (-0.5)
        dquery = scales[at][0] * (dquery - unit_query * jnp.sum(unit_query * dquery, axis=-1, keepdims=True))
        dkey = scales[at][1] * (dkey - key * jnp.sum(key * dkey, axis=-1, keepdims=True))
        for kind, grad in enumerate((dquery, dkey, beta * dy)):
            dconv = grad * (sigs[kind] * (1.0 + convs[kind] * (1.0 - sigs[kind])))
            lanes = slice(kind * width + head * HEAD, kind * width + (head + 1) * HEAD)
            later[part * CHUNK : (part + 1) * CHUNK, lanes] = dconv
    for part in range(count):
        dpre_ref[part * CHUNK : (part + 1) * CHUNK, 4 * width : 4 * width + BETA_PAD] = dbeta_all[part].astype(bf16)
    dgain_ref[...] += dgain
    for kind in range(3):
        for head in range(heads):
            lanes = slice(kind * width + head * HEAD, kind * width + (head + 1) * HEAD)
            source = pre_ref[:, lanes].astype(f32)
            total = jnp.zeros((rows, HEAD), f32)
            for tap in range(TAPS):
                at = kind * TAPS + tap
                shifted = later[TAPS - 1 - tap : TAPS - 1 - tap + rows, lanes]
                total = total + taps_ref[at : at + 1, head * HEAD : (head + 1) * HEAD] * shifted
                dtaps_ref[at : at + 1, head * HEAD : (head + 1) * HEAD] += jnp.sum(
                    source * shifted, axis=0, keepdims=True
                )
            dpre_ref[:, lanes] = total.astype(bf16)


def mixer_backward(pre, conv, mixed, dz, inverse, states, taps, gain, heads):
    length, total = pre.shape
    width = heads * HEAD
    steps, parts = length // STEP, STEP // CHUNK
    return pl.pallas_call(
        functools.partial(backward_kernel, heads),
        grid=(steps,),
        in_specs=[
            pl.BlockSpec((STEP, total), lambda i: (steps - 1 - i, 0)),
            pl.BlockSpec((STEP, 3 * width), lambda i: (steps - 1 - i, 0)),
            pl.BlockSpec((STEP, width), lambda i: (steps - 1 - i, 0)),
            pl.BlockSpec((STEP, width), lambda i: (steps - 1 - i, 0)),
            pl.BlockSpec((heads, parts, CHUNK, CHUNK), lambda i: (0, steps - 1 - i, 0, 0)),
            pl.BlockSpec((heads, parts, HEAD, HEAD), lambda i: (0, steps - 1 - i, 0, 0)),
            pl.BlockSpec((3 * TAPS, width), lambda i: (0, 0)),
            pl.BlockSpec((1, HEAD), lambda i: (0, 0)),
        ],
        out_specs=[
            pl.BlockSpec((STEP, total), lambda i: (steps - 1 - i, 0)),
            pl.BlockSpec((3 * TAPS, width), lambda i: (0, 0)),
            pl.BlockSpec((1, HEAD), lambda i: (0, 0)),
        ],
        out_shape=[
            jax.ShapeDtypeStruct((length, total), bf16),
            jax.ShapeDtypeStruct((3 * TAPS, width), f32),
            jax.ShapeDtypeStruct((1, HEAD), f32),
        ],
        scratch_shapes=[
            pltpu.VMEM((STEP + 8, 3 * width), f32),
            pltpu.VMEM((heads, HEAD, HEAD), f32),
        ],
        compiler_params=pltpu.CompilerParams(
            dimension_semantics=("arbitrary",), vmem_limit_bytes=VMEM_LIMIT
        ),
        cost_estimate=pl.CostEstimate(
            flops=2 * length * width * HEAD * 120, bytes_accessed=length * (total * 6 + width * 24), transcendentals=length * width * 8
        ),
    )(pre, conv, mixed, dz, inverse, states, taps, gain)


MESH = pl.DeviceIdType.MESH
TILE = 16
LANES = 128
LARGE_LIMIT = 60 * 1024 * 1024


def remote(source, target, send, receive, **where):
    return pltpu.make_async_remote_copy(
        src_ref=source,
        dst_ref=target,
        send_sem=send,
        recv_sem=receive,
        device_id=where,
        device_id_type=MESH,
    )


def when(condition, action):
    pl.when(condition)(action)


def greet(**where):
    pl.semaphore_signal(
        pltpu.get_barrier_semaphore(), inc=1, device_id=where, device_id_type=MESH
    )


def wait_greetings(count):
    pl.semaphore_wait(pltpu.get_barrier_semaphore(), count)


def plane():
    me = lax.axis_index("tensor")
    across = me + 1 - 2 * lax.rem(me, 2)
    along = lax.rem(me + 2, 4)
    return me, across, along


def chip_and_core():
    index = lax.axis_index("dp")
    return index // 2, lax.rem(index, 2)


def greet_line(chips):
    chip, core = chip_and_core()
    greet(dp=chip * 2 + 1 - core)
    when(chip > 0, lambda: greet(dp=(chip - 1) * 2 + core))
    when(chip < chips - 1, lambda: greet(dp=(chip + 1) * 2 + core))
    return 1 + jnp.where(chip > 0, 1, 0) + jnp.where(chip < chips - 1, 1, 0)


class PlaneGather:
    def __init__(self, own, full, send, receive):
        self.own, self.full, self.send, self.receive = own, full, send, receive
        self.me, self.across, self.along = plane()
        self.far = lax.rem(self.across + 2, 4)
        self.rows = own.shape[0]
        self.half = self.rows // 2

    def slot(self, block, half):
        start = pl.multiple_of(block * self.rows + half * self.half, self.half)
        return self.full.at[pl.ds(start, self.half)]

    def mine(self, half):
        return self.own.at[pl.ds(half * self.half, self.half)]

    def out(self, half, kind):
        where = self.across if kind == 0 else self.along
        at = 2 * kind + half
        return remote(
            self.mine(half), self.slot(self.me, half), self.send.at[at], self.receive.at[at], tensor=where
        )

    def arriving(self, half, kind):
        block = self.across if kind == 0 else self.along
        at = 2 * kind + half
        view = self.slot(block, half)
        return remote(view, view, self.send.at[at], self.receive.at[at], tensor=block)

    def passing(self, kind):
        view = self.slot(self.across if kind == 0 else self.along, kind)
        where = self.along if kind == 0 else self.across
        return remote(view, view, self.send.at[4 + kind], self.receive.at[4 + kind], tensor=where)

    def passed(self, kind):
        view = self.slot(self.far, kind)
        where = self.along if kind == 0 else self.across
        return remote(view, view, self.send.at[4 + kind], self.receive.at[4 + kind], tensor=where)

    def start(self, half):
        for kind in (half, 1 - half):
            self.out(half, kind).start()

    def relay(self, kind):
        self.arriving(kind, kind).wait_recv()
        self.passing(kind).start()

    def finish(self):
        for kind in (0, 1):
            self.arriving(1 - kind, kind).wait_recv()
        for kind in (0, 1):
            self.passed(kind).wait_recv()
            self.passing(kind).wait_send()
            for half in (0, 1):
                self.out(half, kind).wait_send()


class PlaneScatter:
    def __init__(self, part, first, second, stage, send, receive):
        self.part, self.first, self.second, self.stage = part, first, second, stage
        self.send, self.receive = send, receive
        self.me, self.across, self.along = plane()
        self.far = lax.rem(self.across + 2, 4)
        self.rows = part.shape[0] // 4
        self.half = self.rows // 2

    def start_of(self, block, half):
        return pl.multiple_of(block * self.rows + half * self.half, self.half)

    def view(self, block, half):
        return self.part.at[pl.ds(self.start_of(block, half), self.half)]

    def out(self, kind, order):
        where = self.across if kind == 0 else self.along
        at = 2 * kind + order
        return remote(
            self.view(self.far if order == 0 else where, kind),
            self.first.at[at],
            self.send.at[at],
            self.receive.at[at],
            tensor=where,
        )

    def over(self, kind):
        where = self.along if kind == 0 else self.across
        return remote(
            self.stage.at[kind], self.second.at[kind], self.send.at[4 + kind], self.receive.at[4 + kind], tensor=where
        )

    def start_far(self):
        for kind in (0, 1):
            self.out(kind, 0).start()

    def start_near(self, kind):
        self.out(kind, 1).start()

    def relay(self, kind):
        self.out(kind, 0).wait_recv()
        block = self.along if kind == 0 else self.across
        start = self.start_of(block, kind)

        def add(index, carry):
            at = pl.multiple_of(index * TILE, TILE)
            mine = self.part[pl.ds(pl.multiple_of(start + at, TILE), TILE), :].astype(f32)
            other = self.first[2 * kind, pl.ds(at, TILE), :].astype(f32)
            self.stage[kind, pl.ds(at, TILE), :] = (mine + other).astype(bf16)
            return carry

        lax.fori_loop(0, self.half // TILE, add, 0)
        self.over(kind).start()

    def ready(self, kind):
        self.out(kind, 1).wait_recv()
        self.over(kind).wait_recv()

    def tile(self, kind, at):
        start = self.start_of(self.me, kind)
        mine = self.part[pl.ds(pl.multiple_of(start + at, TILE), TILE), :].astype(f32)
        near = self.first[2 * kind + 1, pl.ds(at, TILE), :].astype(f32)
        return mine + near + self.second[kind, pl.ds(at, TILE), :].astype(f32)

    def finish(self):
        for kind in (0, 1):
            for order in (0, 1):
                self.out(kind, order).wait_send()
            self.over(kind).wait_send()


def plane_scatter_scratch(rows, columns):
    half = rows // 2
    return [
        pltpu.VMEM((4, half, columns), bf16),
        pltpu.VMEM((2, half, columns), bf16),
        pltpu.VMEM((2, half, columns), bf16),
        pltpu.SemaphoreType.DMA((6,)),
        pltpu.SemaphoreType.DMA((6,)),
    ]


def pieces_of(arrays, size):
    found = []
    for index, array in enumerate(arrays):
        rows, columns = array.shape[-2:]
        count = max(1, min(rows // 64, round(rows * columns / size)))
        while rows % count or (rows // count) % 16:
            count -= 1
        for piece in range(count):
            found.append((index, piece * (rows // count), rows // count))
    return found


PIECE = 64 * 2176


class LineGather:
    def __init__(self, chips, owns, fulls, sems):
        self.chips, self.owns, self.fulls = chips, owns, fulls
        self.pieces = pieces_of(owns, PIECE)
        self.right_send, self.right_receive, self.left_send, self.left_receive = sems[:4]
        self.core_send, self.core_receive, self.local = sems[4:]
        self.chip, self.core = chip_and_core()

    @staticmethod
    def scratch(chips, pieces, arrays):
        return [pltpu.SemaphoreType.DMA((chips, pieces)) for _ in range(6)] + [pltpu.SemaphoreType.DMA((arrays,))]

    def slot(self, piece, chip, core):
        index, start, rows = self.pieces[piece]
        return self.fulls[index].at[chip * 2 + core, pl.ds(start, rows)]

    def source(self, piece, away):
        index, start, rows = self.pieces[piece]
        return self.owns[index].at[pl.ds(start, rows)]

    def right(self, piece, away, chip):
        slot = self.slot(piece, chip, self.core)
        source = self.source(piece, 0) if away == 0 else slot
        to = (self.chip + 1) * 2 + self.core
        return remote(source, slot, self.right_send.at[away, piece], self.right_receive.at[away, piece], dp=to)

    def left(self, piece, away, chip):
        slot = self.slot(piece, chip, self.core)
        source = self.source(piece, 0) if away == 0 else slot
        to = (self.chip - 1) * 2 + self.core
        return remote(source, slot, self.left_send.at[away, piece], self.left_receive.at[away, piece], dp=to)

    def trade(self, piece, chip, own):
        slot = self.slot(piece, chip, self.core)
        source = self.source(piece, 0) if own else slot
        to = self.chip * 2 + 1 - self.core
        return remote(source, slot, self.core_send.at[chip, piece], self.core_receive.at[chip, piece], dp=to)

    def keep(self, index):
        return pltpu.make_async_copy(
            self.owns[index], self.fulls[index].at[self.chip * 2 + self.core], self.local.at[index]
        )

    def start(self):
        for piece in range(len(self.pieces)):
            when(self.chip < self.chips - 1, lambda: self.right(piece, 0, self.chip).start())
            when(self.chip > 0, lambda: self.left(piece, 0, self.chip).start())
        for piece in range(len(self.pieces)):
            self.trade(piece, self.chip, True).start()
        for index in range(len(self.owns)):
            self.keep(index).start()

    def step(self, away):
        for piece in range(len(self.pieces)):

            def from_left():
                chip = self.chip - away
                self.right(piece, away - 1, chip).wait_recv()
                if away < self.chips - 1:
                    when(self.chip < self.chips - 1, lambda: self.right(piece, away, chip).start())
                self.trade(piece, chip, False).start()

            def from_right():
                chip = self.chip + away
                self.left(piece, away - 1, chip).wait_recv()
                if away < self.chips - 1:
                    when(self.chip > 0, lambda: self.left(piece, away, chip).start())
                self.trade(piece, chip, False).start()

            when(self.chip >= away, from_left)
            when(self.chip + away < self.chips, from_right)

    def finish(self):
        for index in range(len(self.owns)):
            self.keep(index).wait()
        for piece in range(len(self.pieces)):
            for away in range(self.chips - 1):
                when(
                    (self.chip < self.chips - 1) & (self.chip >= away),
                    lambda: self.right(piece, away, self.chip - away).wait_send(),
                )
                when(
                    (self.chip > 0) & (self.chip + away < self.chips),
                    lambda: self.left(piece, away, self.chip + away).wait_send(),
                )
            for chip in range(self.chips):
                trade = remote(
                    self.slot(piece, chip, self.core),
                    self.slot(piece, chip, 1 - self.core),
                    self.core_send.at[chip, piece],
                    self.core_receive.at[chip, piece],
                    dp=self.chip * 2 + 1 - self.core,
                )
                trade.wait_send()
                trade.wait_recv()


def first_gather_kernel(chips, *refs):
    w_query, w_key, w_value, w_gate_out, w_beta, w_output, inputs, cotangent, mask, gain = refs[:10]
    w_gate, w_up, w_down = refs[10:13]
    inner_full, output_full, normed_full, grad_full, gate_up, down, grad = refs[13:20]
    inner, output, normed, gate_wide, up_wide, down_wide = refs[20:26]
    sems = refs[26:]
    width, hidden = w_query.shape[1], w_gate.shape[1]
    line = LineGather(chips, [inner, output], [inner_full, output_full], sems[:7])
    rows = [PlaneGather(normed, normed_full, *sems[7:9]), PlaneGather(grad, grad_full, *sems[9:11])]
    local = sems[11]
    keeps = [
        pltpu.make_async_copy(
            own, full.at[pl.ds(pl.multiple_of(each.me * each.rows, each.rows), each.rows)], local.at[at]
        )
        for at, (own, full, each) in enumerate(((normed, normed_full, rows[0]), (grad, grad_full, rows[1])))
    ]
    loads = [
        pltpu.make_async_copy(source, target, local.at[2 + at])
        for at, (source, target) in enumerate(((w_gate, gate_wide), (w_up, up_wide), (w_down, down_wide)))
    ]
    greetings = greet_line(chips)
    greet(tensor=rows[0].across)
    greet(tensor=rows[0].along)
    for kind, weight in enumerate((w_query, w_key, w_value, w_gate_out)):
        inner[:, kind * width : (kind + 1) * width] = weight[...].astype(bf16)
    inner[:, 4 * width :] = jnp.zeros((inner.shape[0], BETA_PAD), bf16)
    inner[:, 4 * width : 4 * width + w_beta.shape[1]] = w_beta[...].astype(bf16)
    output[...] = jnp.transpose(w_output[...]).astype(bf16)
    wait_greetings(2 + greetings)
    line.start()
    for load in loads:
        load.start()

    def norm(index, carry):
        here = pl.ds(pl.multiple_of(index * TILE, TILE), TILE)
        value = inputs[here, :].astype(f32)
        scale = lax.rsqrt(jnp.mean(value * value, axis=-1, keepdims=True) + norm_epsilon)
        normed[here, :] = (value * scale * gain[...]).astype(bf16)
        grad[here, :] = (cotangent[here, :].astype(f32) * mask[here, :]).astype(bf16)
        return carry

    lax.fori_loop(0, inputs.shape[0] // TILE, norm, 0)
    for each in rows:
        each.start(0)
        each.start(1)
    for keep in keeps:
        keep.start()
    for load in loads:
        load.wait()
    for kind, wide in enumerate((gate_wide, up_wide)):
        for tile in range(hidden // LANES):
            to = (2 * tile + kind) * LANES
            gate_up[:, to : to + LANES] = wide[:, tile * LANES : (tile + 1) * LANES].astype(bf16)
    down[...] = jnp.transpose(down_wide[...]).astype(bf16)
    rows[0].relay(0)
    rows[0].relay(1)
    line.step(1)
    rows[1].relay(0)
    rows[1].relay(1)
    for away in range(2, chips):
        line.step(away)
    for each in rows:
        each.finish()
    for keep in keeps:
        keep.wait()
    line.finish()


def ffn_kernel(normed, weight, middle, slopes):
    def block(index, carry):
        here = pl.ds(pl.multiple_of(index * 512, 512), 512)
        both = mm(normed[here, :], weight[...])
        gate, up_part = both[:, :LANES], both[:, LANES:]
        act, sig = silu_parts(gate)
        middle[here, :] = (act * up_part).astype(bf16)
        slopes[here, :LANES] = (up_part * sig * (1.0 + gate * (1.0 - sig))).astype(bf16)
        slopes[here, LANES:] = act.astype(bf16)
        return carry

    lax.fori_loop(0, normed.shape[0] // 512, block, 0, unroll=True)


def ffn(normed, gate_up):
    length, model = normed.shape
    hidden = gate_up.shape[1] // 2
    return pl.pallas_call(
        ffn_kernel,
        grid=(hidden // LANES,),
        in_specs=[
            pl.BlockSpec((length, model), lambda i: (0, 0)),
            pl.BlockSpec((model, 2 * LANES), lambda i: (0, i)),
        ],
        out_specs=[
            pl.BlockSpec((length, LANES), lambda i: (0, i)),
            pl.BlockSpec((length, 2 * LANES), lambda i: (0, i)),
        ],
        out_shape=[
            jax.ShapeDtypeStruct((length, hidden), bf16),
            jax.ShapeDtypeStruct((length, 2 * hidden), bf16),
        ],
        compiler_params=pltpu.CompilerParams(
            dimension_semantics=("arbitrary",), vmem_limit_bytes=VMEM_LIMIT
        ),
        cost_estimate=pl.CostEstimate(
            flops=4 * length * model * hidden, bytes_accessed=2 * (length * model + 2 * model * hidden), transcendentals=length * hidden
        ),
    )(normed, gate_up)


def ffn_backward_kernel(grad, weight, slopes, grad_both):
    grad_middle = mm(grad[...], weight[...])
    for tile in range(weight.shape[1] // LANES):
        part = grad_middle[:, tile * LANES : (tile + 1) * LANES]
        for kind in range(2):
            lanes = slice((2 * tile + kind) * LANES, (2 * tile + kind + 1) * LANES)
            grad_both[:, lanes] = (part * slopes[:, lanes].astype(f32)).astype(bf16)


def ffn_backward(grad, down, slopes):
    length, model = grad.shape
    hidden = down.shape[1]
    block = 512
    return pl.pallas_call(
        ffn_backward_kernel,
        grid=(length // block,),
        in_specs=[
            pl.BlockSpec((block, model), lambda i: (i, 0)),
            pl.BlockSpec((model, hidden), lambda i: (0, 0)),
            pl.BlockSpec((block, 2 * hidden), lambda i: (i, 0)),
        ],
        out_specs=pl.BlockSpec((block, 2 * hidden), lambda i: (i, 0)),
        out_shape=jax.ShapeDtypeStruct((length, 2 * hidden), bf16),
        compiler_params=pltpu.CompilerParams(
            dimension_semantics=("arbitrary",), vmem_limit_bytes=VMEM_LIMIT
        ),
        cost_estimate=pl.CostEstimate(
            flops=2 * length * model * hidden, bytes_accessed=2 * (length * model + model * hidden + 4 * length * hidden), transcendentals=0
        ),
    )(grad, down, slopes)


def finish_kernel(count, *refs):
    both, down = refs[:2]
    sources, gate_out, up_out, down_out = refs[2 : 2 + count], *refs[2 + count : 5 + count]
    targets, held, sems = refs[5 + count : 5 + 2 * count], refs[5 + 2 * count : 5 + 3 * count], refs[-1]
    loads = [
        pltpu.make_async_copy(source, here, sems.at[0, at]) for at, (source, here) in enumerate(zip(sources, held))
    ]
    stores = [
        pltpu.make_async_copy(here, target, sems.at[1, at]) for at, (here, target) in enumerate(zip(held, targets))
    ]
    for load in loads:
        load.start()
    for tile in range(gate_out.shape[1] // LANES):
        lanes = slice(tile * LANES, (tile + 1) * LANES)
        gate_out[:, lanes] = both[:, 2 * tile * LANES : (2 * tile + 1) * LANES].astype(f32)
        up_out[:, lanes] = both[:, (2 * tile + 1) * LANES : (2 * tile + 2) * LANES].astype(f32)
    for load, store in zip(loads, stores):
        load.wait()
        store.start()
    for tile in range(gate_out.shape[1] // LANES):
        lanes = slice(tile * LANES, (tile + 1) * LANES)
        down_out[lanes, :] = jnp.transpose(down[:, lanes].astype(f32))
    for store in stores:
        store.wait()


def finish(both, down, arrays):
    slab, hidden = down.shape
    return pl.pallas_call(
        functools.partial(finish_kernel, len(arrays)),
        in_specs=in_vmem(2) + anywhere(len(arrays)),
        out_specs=in_vmem(3) + anywhere(len(arrays)),
        out_shape=[
            jax.ShapeDtypeStruct((slab, hidden), f32),
            jax.ShapeDtypeStruct((slab, hidden), f32),
            jax.ShapeDtypeStruct((hidden, slab), f32),
        ]
        + [jax.ShapeDtypeStruct(array.shape, array.dtype) for array in arrays],
        scratch_shapes=[pltpu.VMEM(array.shape, array.dtype) for array in arrays]
        + [pltpu.SemaphoreType.DMA((2, len(arrays)))],
        compiler_params=pltpu.CompilerParams(vmem_limit_bytes=VMEM_LIMIT),
        cost_estimate=pl.CostEstimate(flops=0, bytes_accessed=40 * slab * hidden, transcendentals=0),
    )(both, down, *arrays)


def plain_ffn(normed, gate_up):
    gate, up_part = jnp.split(jnp.dot(normed, gate_up, preferred_element_type=f32), 2, axis=1)
    act, sig = silu_parts(gate)
    slopes = jnp.concatenate([up_part * sig * (1.0 + gate * (1.0 - sig)), act], axis=1)
    return (act * up_part).astype(bf16), slopes.astype(bf16)


def plain_ffn_backward(grad, down, slopes):
    grad_middle = jnp.dot(grad, down, preferred_element_type=f32)
    return (jnp.concatenate([grad_middle, grad_middle], axis=1) * slopes.astype(f32)).astype(bf16)


def plain_finish(both, down, arrays):
    gate, up_part = jnp.split(both.astype(f32), 2, axis=1)
    return gate, up_part, down.astype(f32).T, *arrays


def anywhere(count):
    return [pl.BlockSpec(memory_space=pl.ANY)] * count


def in_vmem(count):
    return [pl.BlockSpec(memory_space=pltpu.VMEM)] * count


def first_gather(w_query, w_key, w_value, w_gate_out, w_beta, w_output, inputs, cotangent, mask, gain, w_gate, w_up, w_down):
    shards = lax.axis_size("dp")
    rows, model = inputs.shape
    slab, width = w_query.shape
    hidden = w_gate.shape[1]
    inner = jax.ShapeDtypeStruct((slab, 4 * width + BETA_PAD), bf16)
    output = jax.ShapeDtypeStruct((slab, width), bf16)
    pieces = len(pieces_of([inner, output], PIECE))
    return pl.pallas_call(
        functools.partial(first_gather_kernel, shards // 2),
        in_specs=in_vmem(10) + anywhere(3),
        out_specs=anywhere(4) + in_vmem(3),
        out_shape=[
            jax.ShapeDtypeStruct((shards, *inner.shape), bf16),
            jax.ShapeDtypeStruct((shards, *output.shape), bf16),
            jax.ShapeDtypeStruct((4 * rows, model), bf16),
            jax.ShapeDtypeStruct((4 * rows, model), bf16),
            jax.ShapeDtypeStruct((slab, 2 * hidden), bf16),
            jax.ShapeDtypeStruct((slab, hidden), bf16),
            jax.ShapeDtypeStruct((rows, model), bf16),
        ],
        scratch_shapes=[
            pltpu.VMEM(inner.shape, bf16),
            pltpu.VMEM(output.shape, bf16),
            pltpu.VMEM((rows, model), bf16),
            pltpu.VMEM((slab, hidden), f32),
            pltpu.VMEM((slab, hidden), f32),
            pltpu.VMEM((hidden, slab), f32),
        ]
        + LineGather.scratch(shards // 2, pieces, 2)
        + [pltpu.SemaphoreType.DMA((6,)) for _ in range(4)]
        + [pltpu.SemaphoreType.DMA((5,))],
        compiler_params=pltpu.CompilerParams(
            collective_id=1, has_side_effects=True, vmem_limit_bytes=VMEM_LIMIT
        ),
        cost_estimate=pl.CostEstimate(flops=80_000_000_000, bytes_accessed=20_000_000, transcendentals=0),
    )(w_query, w_key, w_value, w_gate_out, w_beta, w_output, inputs, cotangent, mask, gain, w_gate, w_up, w_down)


def branch_kernel(z, weight, inputs, gain, resid, full, part, first, second, stage, low, s_send, s_recv, g_send, g_recv, local):
    scatter = PlaneScatter(part, first, second, stage, s_send, s_recv)
    gather = PlaneGather(low, full, g_send, g_recv)
    rows = scatter.rows
    slab = weight.shape[1]
    greet(tensor=scatter.across)
    greet(tensor=scatter.along)

    def compute(block):
        here = pl.ds(scatter.start_of(block, 0), rows)

        def column(index, carry):
            part[here, pl.ds(pl.multiple_of(index * slab, slab), slab)] = mm_nt(z[here, :], weight[index]).astype(bf16)
            return carry

        lax.fori_loop(0, weight.shape[0], column, 0)

    compute(scatter.far)
    wait_greetings(2)
    scatter.start_far()
    compute(scatter.across)
    scatter.start_near(0)
    compute(scatter.along)
    scatter.start_near(1)
    compute(scatter.me)
    scatter.relay(0)
    scatter.relay(1)
    for half in (0, 1):
        scatter.ready(half)

        def norm(index, carry):
            at = pl.multiple_of(index * TILE, TILE)
            here = pl.ds(pl.multiple_of(half * scatter.half + at, TILE), TILE)
            value = inputs[here, :].astype(f32) + scatter.tile(half, at)
            resid[here, :] = value
            scale = lax.rsqrt(jnp.mean(value * value, axis=-1, keepdims=True) + norm_epsilon)
            low[here, :] = (value * scale * gain[...]).astype(bf16)
            return carry

        lax.fori_loop(0, scatter.half // TILE, norm, 0)
        gather.start(half)
    keep = pltpu.make_async_copy(low, full.at[pl.ds(pl.multiple_of(gather.me * rows, rows), rows)], local.at[0])
    keep.start()
    gather.relay(0)
    gather.relay(1)
    scatter.finish()
    gather.finish()
    keep.wait()


def branch_and_norm(z, weight, inputs, gain):
    rows, model = inputs.shape
    return pl.pallas_call(
        branch_kernel,
        in_specs=in_vmem(4),
        out_specs=in_vmem(1) + anywhere(1),
        out_shape=[
            jax.ShapeDtypeStruct((rows, model), f32),
            jax.ShapeDtypeStruct((4 * rows, model), bf16),
        ],
        scratch_shapes=[pltpu.VMEM((4 * rows, model), bf16)]
        + plane_scatter_scratch(rows, model)[:3]
        + [pltpu.VMEM((rows, model), bf16)]
        + [pltpu.SemaphoreType.DMA((6,)) for _ in range(4)]
        + [pltpu.SemaphoreType.DMA((1,))],
        compiler_params=pltpu.CompilerParams(
            collective_id=2, has_side_effects=True, vmem_limit_bytes=VMEM_LIMIT
        ),
        cost_estimate=pl.CostEstimate(flops=50_000_000_000, bytes_accessed=20_000_000, transcendentals=0),
    )(z, weight, inputs, gain)


def norm_backward(value, grad, gain):
    scale = lax.rsqrt(jnp.mean(value * value, axis=-1, keepdims=True) + norm_epsilon)
    normed = value * scale
    inner = grad * gain
    return scale * (inner - normed * jnp.mean(inner * normed, axis=-1, keepdims=True)), grad * normed


class LineScatter:
    def __init__(self, chips, parts, stages, trades, arrived, sems):
        self.chips, self.parts, self.stages, self.trades, self.arrived = chips, parts, stages, trades, arrived
        self.pieces = pieces_of(parts, PIECE)
        self.right_send, self.right_receive, self.left_send, self.left_receive = sems[:4]
        self.core_send, self.core_receive, self.local = sems[4:]
        self.chip, self.core = chip_and_core()

    @staticmethod
    def scratch(chips, arrays):
        shapes = [array.shape[-2:] for array in arrays]
        pieces = len(pieces_of(arrays, PIECE))
        return (
            [pltpu.VMEM((chips, *shape), bf16) for shape in shapes]
            + [pltpu.VMEM((chips, *shape), bf16) for shape in shapes]
            + [pltpu.VMEM((chips + 1, *shape), bf16) for shape in shapes]
            + [pltpu.SemaphoreType.DMA((chips, pieces)) for _ in range(6)]
            + [pltpu.SemaphoreType.DMA((len(arrays), chips))]
        )

    def order(self):
        order = []
        for step in range(self.chips // 2):
            order += [self.chips - 1 - step, step]
        return order

    def trade(self, piece, dest):
        index, start, rows = self.pieces[piece]
        return remote(
            self.parts[index].at[dest * 2 + 1 - self.core, pl.ds(start, rows)],
            self.trades[index].at[dest, pl.ds(start, rows)],
            self.core_send.at[dest, piece],
            self.core_receive.at[dest, piece],
            dp=self.chip * 2 + 1 - self.core,
        )

    def load(self, index, dest):
        return pltpu.make_async_copy(
            self.parts[index].at[dest * 2 + self.core], self.stages[index].at[dest], self.local.at[index, dest]
        )

    def right(self, piece, dest):
        index, start, rows = self.pieces[piece]
        here = pl.ds(start, rows)
        return remote(
            self.stages[index].at[dest, here],
            self.arrived[index].at[dest, here],
            self.right_send.at[dest, piece],
            self.right_receive.at[dest, piece],
            dp=(self.chip + 1) * 2 + self.core,
        )

    def left_slot(self, dest, chip):
        return jnp.where(dest == chip, self.chips, dest)

    def left(self, piece, dest):
        index, start, rows = self.pieces[piece]
        here = pl.ds(start, rows)
        return remote(
            self.stages[index].at[dest, here],
            self.arrived[index].at[self.left_slot(dest, self.chip - 1), here],
            self.left_send.at[dest, piece],
            self.left_receive.at[dest, piece],
            dp=(self.chip - 1) * 2 + self.core,
        )

    def start(self):
        for dest in self.order():
            for index in range(len(self.parts)):
                self.load(index, dest).start()
            for piece in range(len(self.pieces)):
                self.trade(piece, dest).start()

    def add(self, piece, dest, slots, put=None):
        index, start, rows = self.pieces[piece]

        def tile(at, carry):
            here = pl.ds(pl.multiple_of(start + at * TILE, TILE), TILE)
            total = self.stages[index][dest, here, :].astype(f32) + self.trades[index][dest, here, :].astype(f32)
            for slot in slots:
                total = total + self.arrived[index][slot, here, :].astype(f32)
            if put is None:
                self.stages[index][dest, here, :] = total.astype(bf16)
            else:
                put[index](here, total)
            return carry

        lax.fori_loop(0, rows // TILE, tile, 0)

    def first_of(self, piece):
        return piece == 0 or self.pieces[piece - 1][0] != self.pieces[piece][0]

    def receive(self, piece, dest):
        if self.first_of(piece):
            self.load(self.pieces[piece][0], dest).wait()
        self.trade(piece, dest).wait_recv()

    def step(self, step, ends):
        to_right, to_left = self.chips - 1 - step, step

        def send_right(piece):
            self.receive(piece, to_right)
            if not ends:
                self.right(piece, to_right).wait_recv()
            self.add(piece, to_right, [] if ends else [to_right])
            self.right(piece, to_right).start()

        def send_left(piece):
            self.receive(piece, to_left)
            if not ends:
                self.left(piece, to_left).wait_recv()
            self.add(piece, to_left, [] if ends else [to_left])
            self.left(piece, to_left).start()

        count = len(self.pieces)
        if ends:
            when(self.chip == 0, lambda: [send_right(piece) for piece in range(count)] and None)
            when(self.chip == self.chips - 1, lambda: [send_left(piece) for piece in range(count)] and None)
            return
        inner_right = (self.chip > 0) & (to_right > self.chip)
        inner_left = (self.chip < self.chips - 1) & (to_left < self.chip)
        low = self.chip < self.chips // 2
        lead = 2
        for at in range(count + lead):
            early, late = at, at - lead
            if early < count:
                when(low & inner_right, functools.partial(send_right, early))
                when(jnp.logical_not(low) & inner_left, functools.partial(send_left, early))
            if late >= 0:
                when(low & inner_left, functools.partial(send_left, late))
                when(jnp.logical_not(low) & inner_right, functools.partial(send_right, late))

    def keep(self, outs, pieces):
        me = self.chip
        for piece in pieces:
            self.receive(piece, me)
            when(me > 0, lambda: self.right(piece, me).wait_recv())
            when(me < self.chips - 1, lambda: self.left(piece, me).wait_recv())
            when((me > 0) & (me < self.chips - 1), lambda: self.add(piece, me, [me, self.chips], outs))
            when(me == 0, lambda: self.add(piece, me, [self.chips], outs))
            when(me == self.chips - 1, lambda: self.add(piece, me, [me], outs))

    def finish(self):
        for piece in range(len(self.pieces)):
            for dest in range(self.chips):
                self.trade(piece, dest).wait_send()
                when(dest > self.chip, lambda: self.right(piece, dest).wait_send())
                when(dest < self.chip, lambda: self.left(piece, dest).wait_send())


def resid_kernel(
    slab, grad_far, weight_far, resid, grad_out, gain, grad_resid, full, dgain,
    part, first, second, stage, low, s_send, s_recv, g_send, g_recv, local, grad_both, weight, load_sems
):
    scatter = PlaneScatter(part, first, second, stage, s_send, s_recv)
    gather = PlaneGather(low, full, g_send, g_recv)
    rows = scatter.rows
    greet(tensor=scatter.across)
    greet(tensor=scatter.along)

    slabs = weight.shape[0] // slab
    order = (scatter.far, scatter.across, scatter.along, scatter.me)

    def rows_load(at):
        here = pl.ds(scatter.start_of(order[at], 0), rows)
        return pltpu.make_async_copy(grad_far.at[here], grad_both.at[here], load_sems.at[slabs + at])

    def slab_load(index):
        here = pl.ds(pl.multiple_of(index * slab, slab), slab)
        return pltpu.make_async_copy(weight_far.at[here], weight.at[here], load_sems.at[index])

    rows_load(0).start()
    for index in range(slabs):
        slab_load(index).start()
    for at in range(1, 4):
        rows_load(at).start()

    def compute(at):
        here = pl.ds(scatter.start_of(order[at], 0), rows)
        rows_load(at).wait()

        def column(index, carry):
            lanes = pl.ds(pl.multiple_of(index * slab, slab), slab)
            if at == 0:
                slab_load(index).wait()
            part[here, lanes] = mm_nt(grad_both[here, :], weight[lanes, :]).astype(bf16)
            return carry

        lax.fori_loop(0, slabs, column, 0)

    compute(0)
    wait_greetings(2)
    scatter.start_far()
    compute(1)
    scatter.start_near(0)
    compute(2)
    scatter.start_near(1)
    compute(3)
    dgain[...] = jnp.zeros_like(dgain)
    scatter.relay(0)
    scatter.relay(1)
    for half in (0, 1):
        scatter.ready(half)

        def norm(index, carry):
            at = pl.multiple_of(index * TILE, TILE)
            here = pl.ds(pl.multiple_of(half * scatter.half + at, TILE), TILE)
            back, gain_part = norm_backward(resid[here, :], scatter.tile(half, at), gain[...])
            value = grad_out[here, :].astype(f32) + back
            grad_resid[here, :] = value
            low[here, :] = value.astype(bf16)
            dgain[...] += jnp.sum(gain_part, axis=0, keepdims=True)
            return carry

        lax.fori_loop(0, scatter.half // TILE, norm, 0)
        gather.start(half)
    keep = pltpu.make_async_copy(low, full.at[pl.ds(pl.multiple_of(gather.me * rows, rows), rows)], local.at[0])
    keep.start()
    gather.relay(0)
    gather.relay(1)
    scatter.finish()
    gather.finish()
    keep.wait()


def resid_backward(grad_both, weight, resid, grad_out, gain):
    rows, model = resid.shape
    return pl.pallas_call(
        functools.partial(resid_kernel, 256),
        in_specs=anywhere(2) + in_vmem(3),
        out_specs=in_vmem(1) + anywhere(1) + in_vmem(1),
        out_shape=[
            jax.ShapeDtypeStruct((rows, model), f32),
            jax.ShapeDtypeStruct((4 * rows, model), bf16),
            jax.ShapeDtypeStruct((1, model), f32),
        ],
        scratch_shapes=[pltpu.VMEM((4 * rows, model), bf16)]
        + plane_scatter_scratch(rows, model)[:3]
        + [pltpu.VMEM((rows, model), bf16)]
        + [pltpu.SemaphoreType.DMA((6,)) for _ in range(4)]
        + [
            pltpu.SemaphoreType.DMA((1,)),
            pltpu.VMEM(grad_both.shape, bf16),
            pltpu.VMEM(weight.shape, bf16),
            pltpu.SemaphoreType.DMA((model // 256 + 4,)),
        ],
        compiler_params=pltpu.CompilerParams(
            collective_id=3, has_side_effects=True, vmem_limit_bytes=VMEM_LIMIT
        ),
        cost_estimate=pl.CostEstimate(flops=60_000_000_000, bytes_accessed=30_000_000, transcendentals=0),
    )(grad_both, weight, resid, grad_out, gain)


SMALL = 512


def last_kernel(chips, *refs):
    inner_part, output_part, weight, inner, dpre_far, middle_far, inputs_far, grad_resid_far, resid_far = refs[:9]
    mask, first_gain, ffn_dgain, head_dgain, dtaps = refs[9:14]
    query_out, key_out, value_out, gate_out, beta_out, output_out, input_grad, out = refs[14:22]
    first_out, ffn_out, head_out, taps_out = refs[22:26]
    refs = refs[26:]
    line = LineScatter(chips, [inner_part, output_part], refs[:2], refs[2:4], refs[4:6], refs[6:13])
    grad = PlaneScatter(*refs[13:19])
    ffn = PlaneScatter(*refs[19:25])
    turned, small, near, lined, dgain, small_send, small_receive, inner_slabs, down_slabs, slab_sems = refs[25:35]
    dpre, middle, inputs, grad_resid, resid, load_sems = refs[35:41]
    chip, core = line.chip, line.core
    slab = inner_part.shape[1]
    shards = 2 * chips
    sibling = chip * 2 + 1 - core
    greet(tensor=grad.across)
    greet(tensor=grad.along)
    greet(dp=sibling)
    for other in range(1, chips):
        greet(dp=lax.rem(chip + other, chips) * 2 + core)

    def stream(at, source, buffers, kind):
        return pltpu.make_async_copy(source.at[at], buffers.at[lax.rem(at, 2)], slab_sems.at[kind, lax.rem(at, 2)])

    def product(left, source, buffers, target, kind):
        def column(index, carry):
            when(index < shards - 1, lambda: stream(index + 1, source, buffers, kind).start())
            stream(index, source, buffers, kind).wait()
            lanes = pl.ds(pl.multiple_of(index * slab, slab), slab)
            target[:, lanes] = mm_nt(left[...], buffers[lax.rem(index, 2)]).astype(bf16)
            return carry

        lax.fori_loop(0, shards, column, 0)

    loads = [
        pltpu.make_async_copy(source, target, load_sems.at[at])
        for at, (source, target) in enumerate(
            (
                (dpre_far, dpre),
                (middle_far, middle),
                (inputs_far, inputs),
                (grad_resid_far, grad_resid),
                (resid_far, resid),
            )
        )
    ]
    wait_greetings(2 + chips)
    line.start()
    for load in loads[:2]:
        load.start()
    stream(0, inner, inner_slabs, 0).start()
    stream(0, weight, down_slabs, 1).start()
    for load in loads[2:]:
        load.start()
    dgain[...] = jnp.zeros_like(dgain)
    small[...] = jnp.zeros_like(small)
    line.step(0, True)
    loads[0].wait()
    product(dpre, inner, inner_slabs, grad.part, 0)
    grad.start_far()
    grad.start_near(0)
    grad.start_near(1)
    line.step(1, True)
    line.step(0, False)
    loads[1].wait()
    product(middle, weight, down_slabs, ffn.part, 1)
    grad.relay(0)
    grad.relay(1)
    ffn.start_far()
    ffn.start_near(0)
    ffn.start_near(1)
    for step in range(2, chips - 1):
        line.step(step, True)
    for step in range(1, chips - 1):
        line.step(step, False)
    for load in loads[2:]:
        load.wait()
    for half in (0, 1):
        grad.ready(half)

        def norm(index, carry):
            at = pl.multiple_of(index * TILE, TILE)
            here = pl.ds(pl.multiple_of(half * grad.half + at, TILE), TILE)
            back, gain_part = norm_backward(inputs[here, :].astype(f32), grad.tile(half, at), first_gain[...])
            input_grad[here, :] = grad_resid[here, :] + back
            dgain[...] += jnp.sum(gain_part, axis=0, keepdims=True)
            return carry

        lax.fori_loop(0, grad.half // TILE, norm, 0)
    model = dgain.shape[1]
    count = model // SMALL
    for row in range(count):
        lanes = slice(row * SMALL, (row + 1) * SMALL)
        small[0, row : row + 1, :] = dgain[:, lanes]
        small[0, count + row : count + row + 1, :] = ffn_dgain[:, lanes]
    small[0, 2 * count : 2 * count + 1, 0:HEAD] = head_dgain[...]
    small[0, 16 : 16 + 3 * TAPS, :] = dtaps[...]

    def hop(at):
        where = (dict(tensor=grad.across), dict(tensor=grad.along), dict(dp=sibling))[at]
        return remote(small.at[at], near.at[at], small_send.at[at], small_receive.at[at], **where)

    def hopped(at):
        hop(at).wait()
        if at < 2:
            small[at + 1, 0:16, :] = small[at, 0:16, :] + near[at, 0:16, :]
            small[at + 1, 16:32, :] = small[at, 16:32, :]
        else:
            small[3] = small[2] + near[2]

    def tell(other):
        to = lax.rem(chip + other, chips)
        return remote(
            small.at[3], lined.at[chip], small_send.at[2 + other], small_receive.at[2 + other], dp=to * 2 + core
        )

    def put_inner(here, total):
        width = query_out.shape[1]
        for kind, target in enumerate((query_out, key_out, value_out, gate_out)):
            target[here, :] = total[:, kind * width : (kind + 1) * width]
        beta_out[here, :] = total[:, 4 * width : 4 * width + beta_out.shape[1]]

    def put_output(here, total):
        turned[here, :] = total

    puts = [put_inner, put_output]
    hop(0).start()
    ffn.relay(0)
    ffn.relay(1)
    hopped(0)
    hop(1).start()
    pieces = len(line.pieces)
    line.keep(puts, range(0, pieces - 3))
    hopped(1)
    hop(2).start()
    for half in (0, 1):
        ffn.ready(half)

        def finish_rows(index, carry):
            at = pl.multiple_of(index * TILE, TILE)
            here = pl.ds(pl.multiple_of(half * ffn.half + at, TILE), TILE)
            out[here, :] = ((resid[here, :] + ffn.tile(half, at)) * mask[here, :]).astype(bf16)
            return carry

        lax.fori_loop(0, ffn.half // TILE, finish_rows, 0)
    hopped(2)
    lined[chip] = small[3]
    for other in range(1, chips):
        tell(other).start()
    line.keep(puts, range(pieces - 3, pieces))
    output_out[...] = jnp.transpose(turned[...])
    for other in range(1, chips):
        tell(other).wait()
    total = lined[0]
    for other in range(1, chips):
        total = total + lined[other]
    for row in range(count):
        lanes = slice(row * SMALL, (row + 1) * SMALL)
        first_out[:, lanes] = total[row : row + 1, :]
        ffn_out[:, lanes] = total[count + row : count + row + 1, :]
    head_out[...] = total[2 * count : 2 * count + 1, 0:HEAD]
    for kind in range(3):
        taps_out[kind] = total[16 + kind * TAPS : 16 + (kind + 1) * TAPS, :]
    grad.finish()
    ffn.finish()
    line.finish()


def last_scatter(
    inner_part, output_part, weight, inner, dpre, middle, inputs, grad_resid, resid, mask, gain, ffn_dgain, head_dgain, dtaps
):
    chips = lax.axis_size("dp") // 2
    rows, model = inputs.shape
    slab, width = output_part.shape[1:]
    arrays = [inner_part, output_part]
    shape = jax.ShapeDtypeStruct
    return pl.pallas_call(
        functools.partial(last_kernel, chips),
        in_specs=anywhere(9) + in_vmem(5),
        out_specs=in_vmem(12),
        out_shape=[shape((slab, width), f32)] * 4
        + [
            shape((slab, width // HEAD), f32),
            shape((width, slab), f32),
            shape((rows, model), f32),
            shape((rows, model), bf16),
            shape((1, model), f32),
            shape((1, model), f32),
            shape((1, HEAD), f32),
            shape((3, TAPS, dtaps.shape[1]), f32),
        ],
        scratch_shapes=LineScatter.scratch(chips, arrays)
        + [pltpu.VMEM((4 * rows, model), bf16)]
        + plane_scatter_scratch(rows, model)
        + [pltpu.VMEM((4 * rows, model), bf16)]
        + plane_scatter_scratch(rows, model)
        + [
            pltpu.VMEM((slab, width), f32),
            pltpu.VMEM((4, 32, SMALL), f32),
            pltpu.VMEM((3, 32, SMALL), f32),
            pltpu.VMEM((chips, 32, SMALL), f32),
            pltpu.VMEM((1, model), f32),
            pltpu.SemaphoreType.DMA((2 + chips,)),
            pltpu.SemaphoreType.DMA((2 + chips,)),
            pltpu.VMEM((2, *inner.shape[1:]), bf16),
            pltpu.VMEM((2, *weight.shape[1:]), bf16),
            pltpu.SemaphoreType.DMA((2, 2)),
            pltpu.VMEM(dpre.shape, bf16),
            pltpu.VMEM(middle.shape, bf16),
            pltpu.VMEM((rows, model), bf16),
            pltpu.VMEM((rows, model), f32),
            pltpu.VMEM((rows, model), f32),
            pltpu.SemaphoreType.DMA((5,)),
        ],
        compiler_params=pltpu.CompilerParams(
            collective_id=4, has_side_effects=True, vmem_limit_bytes=LARGE_LIMIT
        ),
        cost_estimate=pl.CostEstimate(flops=80_000_000_000, bytes_accessed=20_000_000, transcendentals=0),
    )(inner_part, output_part, weight, inner, dpre, middle, inputs, grad_resid, resid, mask, gain, ffn_dgain, head_dgain, dtaps)


def rms_norm(values, gain):
    return (
        values * lax.rsqrt(jnp.mean(values * values, axis=-1, keepdims=True) + norm_epsilon) * gain
    )


def gather(values, axis):
    return lax.all_gather(values, axis, axis=0, tiled=True)


def scatter(values, axis):
    return lax.psum_scatter(values, axis, scatter_dimension=0, tiled=True)


def plain_first_gather(
    w_query, w_key, w_value, w_gate_out, w_beta, w_output, inputs, cotangent, mask, gain, w_gate, w_up, w_down
):
    shards = lax.axis_size("dp")
    padded = jnp.pad(w_beta, ((0, 0), (0, BETA_PAD - w_beta.shape[1])))
    inner = jnp.concatenate([w_query, w_key, w_value, w_gate_out, padded], axis=1).astype(bf16)
    output = w_output.T.astype(bf16)
    grad = (cotangent.astype(f32) * mask).astype(bf16)
    return (
        gather(inner, "dp").reshape(shards, *inner.shape),
        gather(output, "dp").reshape(shards, *output.shape),
        gather(rms_norm(inputs.astype(f32), gain[0]).astype(bf16), "tensor"),
        gather(grad, "tensor"),
        jnp.concatenate([w_gate, w_up], axis=1).astype(bf16),
        w_down.T.astype(bf16),
        grad,
    )


def plain_branch_and_norm(z, weight, inputs, gain):
    branch = mm_nt(z, weight.reshape(-1, z.shape[1])).astype(bf16)
    resid = inputs.astype(f32) + scatter(branch, "tensor").astype(f32)
    return resid, gather(rms_norm(resid, gain[0]).astype(bf16), "tensor")


def plain_resid_backward(grad_both, weight, resid, grad_out, gain):
    part = mm_nt(grad_both, weight).astype(bf16)
    back, gain_part = norm_backward(resid, scatter(part, "tensor").astype(f32), gain)
    value = grad_out.astype(f32) + back
    return value, gather(value.astype(bf16), "tensor"), jnp.sum(gain_part, axis=0, keepdims=True)


def plain_last_scatter(
    inner_part, output_part, weight, inner, dpre, middle, inputs, grad_resid, resid, mask, gain, ffn_dgain, head_dgain, dtaps
):
    grad_part = mm_nt(dpre, inner.reshape(-1, inner.shape[2])).astype(bf16)
    inner, output = (
        scatter(part.reshape(-1, part.shape[-1]), "dp").astype(f32) for part in (inner_part, output_part)
    )
    width = output.shape[1]
    back, gain_part = norm_backward(inputs.astype(f32), scatter(grad_part, "tensor").astype(f32), gain)
    ffn_part = mm_nt(middle, weight.reshape(-1, weight.shape[2])).astype(bf16)
    out = ((resid + scatter(ffn_part, "tensor").astype(f32)) * mask).astype(bf16)
    gains = (jnp.sum(gain_part, axis=0, keepdims=True), ffn_dgain, head_dgain)
    return (
        *(inner[:, kind * width : (kind + 1) * width] for kind in range(4)),
        inner[:, 4 * width : 4 * width + width // HEAD],
        output.T,
        grad_resid + back,
        out,
        *lax.psum(gains, ("dp", "tensor")),
        lax.psum(dtaps, "dp").reshape(3, TAPS, -1),
    )


def body(
    inputs,
    cotangent,
    lengths,
    norm_gain,
    w_query,
    w_key,
    w_value,
    w_gate_out,
    w_beta,
    conv_weight,
    out_norm_gain,
    w_output,
    ffn_norm_gain,
    w_gate,
    w_up,
    w_down,
):
    tensor_count = lax.axis_size("tensor")
    shards = lax.axis_size("dp")
    kernels = tensor_count == 4 and shards == 8
    rows, model = inputs.shape
    length = rows * tensor_count
    width = w_query.shape[1]
    heads = width // HEAD
    hidden = w_gate.shape[1]
    slab = w_query.shape[0]
    taps = conv_weight.reshape(3 * TAPS, width)
    first_gain, head_gain = norm_gain.reshape(1, model), out_norm_gain.reshape(1, HEAD)
    ffn_gain = ffn_norm_gain.reshape(1, model)

    positions = lax.axis_index("tensor") * rows + jnp.arange(rows, dtype=jnp.int32)
    mask = (positions < lengths[0]).astype(f32)[:, None]
    inner, full_output, normed, grad_full, gate_up, down, grad_out = (
        first_gather if kernels else plain_first_gather
    )(w_query, w_key, w_value, w_gate_out, w_beta, w_output, inputs, cotangent, mask, first_gain, w_gate, w_up, w_down)
    gate_up = gather(gate_up, "dp")
    down = gather(down, "dp")

    pre = jnp.dot(normed, inner.reshape(model, -1), preferred_element_type=f32).astype(bf16)
    z, conv, mixed, inverse, states = mixer_forward(pre, taps, head_gain, heads)
    resid, normed2 = (branch_and_norm if kernels else plain_branch_and_norm)(z, full_output, inputs, ffn_gain)
    middle, slopes = (ffn if kernels else plain_ffn)(normed2, gate_up)
    down_part = mm_tn(grad_full, middle).astype(bf16)
    down, down_part = lax.optimization_barrier((down, down_part))
    down_total = scatter(down_part, "dp")
    grad_both = (ffn_backward if kernels else plain_ffn_backward)(grad_full, down, slopes)
    grad_both, both_part = lax.optimization_barrier((grad_both, mm_tn(normed2, grad_both).astype(bf16)))
    both_total = scatter(both_part, "dp")
    grad_resid, grad_resid_full, ffn_dgain = (resid_backward if kernels else plain_resid_backward)(
        grad_both, gate_up, resid, grad_out, ffn_gain
    )
    dz = jnp.dot(grad_resid_full, full_output.reshape(model, width), preferred_element_type=f32).astype(bf16)
    dpre, dtaps, head_dgain = mixer_backward(pre, conv, mixed, dz, inverse, states, taps, head_gain, heads)
    output_grad = mm_tn(grad_resid_full, z).astype(bf16).reshape(shards, slab, width)
    inner_grad = mm_tn(normed, dpre).astype(bf16).reshape(shards, slab, -1)
    results = (last_scatter if kernels else plain_last_scatter)(
        inner_grad,
        output_grad,
        down.reshape(shards, slab, hidden),
        inner,
        dpre,
        middle,
        inputs,
        grad_resid,
        resid,
        mask,
        first_gain,
        ffn_dgain,
        head_dgain,
        dtaps,
    )
    gate_total, up_total, down_total, *results = (finish if kernels else plain_finish)(
        both_total, down_total, results
    )
    query_total, key_total, value_total, gate_out_total, beta_total, output_total, input_grad, output = results[:8]
    first_total, ffn_total, head_total, taps_total = results[8:]
    return (
        output,
        input_grad,
        first_total[0],
        query_total,
        key_total,
        value_total,
        gate_out_total,
        beta_total,
        taps_total,
        head_total[0],
        output_total,
        ffn_total[0],
        gate_total,
        up_total,
        down_total,
    )


def solution(mesh):
    rows = P(("dp", "tensor"), None)
    split = P("dp", "tensor")
    turned = P("tensor", "dp")
    taps = P(None, None, "tensor")
    return jax.shard_map(
        body,
        mesh=mesh,
        in_specs=(rows, rows, P("dp"), P(), split, split, split, split, split, taps, P(), turned, P(), split, split, turned),
        out_specs=(rows, rows, P(), split, split, split, split, split, taps, P(), turned, P(), split, split, turned),
        check_vma=False,
    )
```

```python
import functools
import jax
import jax.numpy as jnp
from jax import lax
from jax.experimental import pallas as pl
from jax.experimental.pallas import tpu as pltpu
from jax.sharding import PartitionSpec as P

norm_epsilon = 1e-06
head_epsilon = 1e-05
HEAD = 128
CHUNK = 128
STEP = 256
TAPS = 4
BETA_PAD = 16
VMEM_LIMIT = 56 * 1024 * 1024
f32 = jnp.float32
bf16 = jnp.bfloat16


def mm(a, b):
    return lax.dot_general(a, b, (((1,), (0,)), ((), ())), preferred_element_type=f32)


def mm_nt(a, b):
    return lax.dot_general(a, b, (((1,), (1,)), ((), ())), preferred_element_type=f32)


def mm_tn(a, b):
    return lax.dot_general(a, b, (((0,), (0,)), ((), ())), preferred_element_type=f32)


def chunk_indices():
    row = lax.broadcasted_iota(jnp.int32, (CHUNK, CHUNK), 0)
    col = lax.broadcasted_iota(jnp.int32, (CHUNK, CHUNK), 1)
    return row, col


def unit_lower_inverses(stricts, row, col):
    apart = row ^ col
    inverses = [jnp.where(row == col, 1.0, jnp.where(apart == 1, -strict, 0.0)) for strict in stricts]
    span = 2
    while span < CHUNK:
        here = (apart >= span) & (apart < 2 * span)
        lows = [inverse.astype(bf16) for inverse in inverses]
        firsts = [mm(low, jnp.where(here, strict, 0.0).astype(bf16)).astype(bf16) for low, strict in zip(lows, stricts)]
        inverses = [inverse - mm(first, low) for inverse, first, low in zip(inverses, firsts, lows)]
        span *= 2
    return [inverse.astype(bf16) for inverse in inverses]


def silu_parts(conv):
    sig = jax.nn.sigmoid(conv)
    return conv * sig, sig


def forward_kernel(
    heads, pre_ref, beta_ref, taps_ref, gain_ref, z_ref, conv_ref, mixed_ref, inv_ref, state_ref, hist, state
):
    step = pl.program_id(0)
    width = heads * HEAD
    rows = pre_ref.shape[0]

    @pl.when(step == 0)
    def _():
        hist[0:8, :] = jnp.zeros((8, 3 * width), f32)
        state[...] = jnp.zeros_like(state)

    @pl.when(step > 0)
    def _():
        hist[0:8, :] = hist[rows : rows + 8, :]

    hist[8 : 8 + rows, :] = pre_ref[:, 0 : 3 * width].astype(f32)
    row, col = chunk_indices()
    beta_all = jax.nn.sigmoid(beta_ref[...])
    work = []
    for head in range(heads):
        parts = []
        for kind in range(3):
            lanes = slice(kind * width + head * HEAD, kind * width + (head + 1) * HEAD)
            total = taps_ref[kind * TAPS : kind * TAPS + 1, head * HEAD : (head + 1) * HEAD] * hist[5 : 5 + rows, lanes]
            for tap in range(1, TAPS):
                total = total + taps_ref[
                    kind * TAPS + tap : kind * TAPS + tap + 1, head * HEAD : (head + 1) * HEAD
                ] * hist[5 + tap : 5 + tap + rows, lanes]
            conv_ref[:, lanes] = total
            act, _ = silu_parts(total)
            if kind < 2:
                act = act * lax.rsqrt(jnp.sum(act * act, axis=-1, keepdims=True) + norm_epsilon)
            if kind == 0:
                act = act * HEAD ** (-0.5)
            parts.append(act)
        beta = beta_all[:, head : head + 1]
        for part in range(rows // CHUNK):
            here = slice(part * CHUNK, (part + 1) * CHUNK)
            query, key, value = (p[here] for p in parts)
            query_low, key_low = query.astype(bf16), key.astype(bf16)
            b = beta[here]
            stacked = jnp.concatenate([(b * key).astype(bf16), (b * value).astype(bf16)], axis=1)
            strict = jnp.where(row > col, b * mm_nt(key_low, key_low), 0.0)
            scores = jnp.where(row >= col, mm_nt(query_low, key_low), 0.0).astype(bf16)
            work.append((head, part, query_low, key_low, stacked, scores, strict))
    inverses = unit_lower_inverses([item[-1] for item in work], row, col)
    solved_all = {}
    for (head, part, query_low, key_low, stacked, scores, _), inverse in zip(work, inverses):
        inv_ref[head, part] = inverse
        solved_all[part, head] = (query_low, key_low, scores, mm(inverse, stacked))
    states = [state[head] for head in range(heads)]
    for part in range(rows // CHUNK):
        here = slice(part * CHUNK, (part + 1) * CHUNK)
        enters = [enter.astype(bf16) for enter in states]
        items = [solved_all[part, head] for head in range(heads)]
        freshes = [
            (solved[:, HEAD:] - mm(solved[:, :HEAD].astype(bf16), enter)).astype(bf16)
            for (_, _, _, solved), enter in zip(items, enters)
        ]
        states = [old + mm_tn(key_low, fresh) for old, (_, key_low, _, _), fresh in zip(states, items, freshes)]
        for head in range(heads):
            lanes = slice(head * HEAD, (head + 1) * HEAD)
            query_low, _, scores, _ = items[head]
            state_ref[head, part] = enters[head]
            mixed = mm(query_low, enters[head]) + mm(scores, freshes[head])
            mixed_ref[here, lanes] = mixed
            gate = pre_ref[here, 3 * width + head * HEAD : 3 * width + (head + 1) * HEAD].astype(f32)
            gate_act, _ = silu_parts(gate)
            normed = mixed * lax.rsqrt(jnp.mean(mixed * mixed, axis=-1, keepdims=True) + head_epsilon)
            z_ref[here, lanes] = (normed * gain_ref[...] * gate_act).astype(bf16)
    for head in range(heads):
        state[head] = states[head]


def mixer_forward(pre, beta, taps, gain, heads):
    length, total = pre.shape
    width = heads * HEAD
    steps, parts = length // STEP, STEP // CHUNK
    return pl.pallas_call(
        functools.partial(forward_kernel, heads),
        grid=(steps,),
        in_specs=[
            pl.BlockSpec((STEP, total), lambda i: (i, 0)),
            pl.BlockSpec((STEP, BETA_PAD), lambda i: (i, 0)),
            pl.BlockSpec((3 * TAPS, width), lambda i: (0, 0)),
            pl.BlockSpec((1, HEAD), lambda i: (0, 0)),
        ],
        out_specs=[
            pl.BlockSpec((STEP, width), lambda i: (i, 0)),
            pl.BlockSpec((STEP, 3 * width), lambda i: (i, 0)),
            pl.BlockSpec((STEP, width), lambda i: (i, 0)),
            pl.BlockSpec((heads, parts, CHUNK, CHUNK), lambda i: (0, i, 0, 0)),
            pl.BlockSpec((heads, parts, HEAD, HEAD), lambda i: (0, i, 0, 0)),
        ],
        out_shape=[
            jax.ShapeDtypeStruct((length, width), bf16),
            jax.ShapeDtypeStruct((length, 3 * width), f32),
            jax.ShapeDtypeStruct((length, width), f32),
            jax.ShapeDtypeStruct((heads, steps * parts, CHUNK, CHUNK), bf16),
            jax.ShapeDtypeStruct((heads, steps * parts, HEAD, HEAD), bf16),
        ],
        scratch_shapes=[
            pltpu.VMEM((STEP + 8, 3 * width), f32),
            pltpu.VMEM((heads, HEAD, HEAD), f32),
        ],
        compiler_params=pltpu.CompilerParams(
            dimension_semantics=("arbitrary",), vmem_limit_bytes=VMEM_LIMIT
        ),
        cost_estimate=pl.CostEstimate(
            flops=2 * length * width * HEAD * 60, bytes_accessed=length * (total * 4 + width * 24), transcendentals=length * width * 8
        ),
    )(pre, beta, taps, gain)


def backward_kernel(
    heads,
    pre_ref,
    beta_ref,
    source_ref,
    conv_ref,
    mixed_ref,
    dz_ref,
    inv_ref,
    state_ref,
    taps_ref,
    gain_ref,
    dpre_ref,
    dbeta_ref,
    dsource_ref,
    dtaps_ref,
    dgain_ref,
    later,
    dstate,
):
    step = pl.program_id(0)
    width = heads * HEAD
    rows = pre_ref.shape[0]
    count = rows // CHUNK

    @pl.when(step == 0)
    def _():
        later[rows : rows + 8, :] = jnp.zeros((8, 3 * width), f32)
        dstate[...] = jnp.zeros_like(dstate)
        dtaps_ref[...] = jnp.zeros_like(dtaps_ref)
        dgain_ref[...] = jnp.zeros_like(dgain_ref)
        dsource_ref[...] = jnp.zeros_like(dsource_ref)

    @pl.when(step > 0)
    def _():
        later[rows : rows + 8, :] = later[0:8, :]

    row, col = chunk_indices()
    beta_all = jax.nn.sigmoid(beta_ref[...])
    beta_lane = lax.broadcasted_iota(jnp.int32, (CHUNK, BETA_PAD), 1)
    dbeta_all = [jnp.zeros((CHUNK, BETA_PAD), f32) for _ in range(count)]
    dgain = jnp.zeros((1, HEAD), f32)
    gain = gain_ref[...]
    every = [(part, head) for part in reversed(range(count)) for head in range(heads)]

    def of(ref, kind, at):
        part, head = at
        lanes = slice(kind * width + head * HEAD, kind * width + (head + 1) * HEAD)
        return ref[part * CHUNK : (part + 1) * CHUNK, lanes].astype(f32)

    betas = {(part, head): beta_all[part * CHUNK : (part + 1) * CHUNK, head : head + 1] for part, head in every}
    unit_queries, keys, query_lows, key_lows, scales, stacks = {}, {}, {}, {}, {}, {}
    for at in every:
        acts = [silu_parts(of(conv_ref, kind, at))[0] for kind in range(3)]
        scales[at] = [lax.rsqrt(jnp.sum(act * act, axis=-1, keepdims=True) + norm_epsilon) for act in acts[:2]]
        unit_queries[at], keys[at] = acts[0] * scales[at][0], acts[1] * scales[at][1]
        query_lows[at] = (unit_queries[at] * HEAD ** (-0.5)).astype(bf16)
        key_lows[at] = keys[at].astype(bf16)
        stacks[at] = jnp.concatenate([(betas[at] * keys[at]).astype(bf16), (betas[at] * acts[2]).astype(bf16)], axis=1)
    solved = {at: mm(inv_ref[at[1], at[0]], stacks[at]) for at in every}
    scores = {at: jnp.where(row >= col, mm_nt(query_lows[at], key_lows[at]), 0.0).astype(bf16) for at in every}
    weights = {at: solved[at][:, :HEAD].astype(bf16) for at in every}
    outs = {}
    for at in every:
        part, head = at
        here = slice(part * CHUNK, (part + 1) * CHUNK)
        gate = of(pre_ref, 3, at)
        gate_act, gate_sig = silu_parts(gate)
        mixed, dz = of(mixed_ref, 0, at), of(dz_ref, 0, at)
        root = lax.rsqrt(jnp.mean(mixed * mixed, axis=-1, keepdims=True) + head_epsilon)
        normed = mixed * root
        dgate = dz * normed * gain * (gate_sig * (1.0 + gate * (1.0 - gate_sig)))
        dpre_ref[here, 3 * width + head * HEAD : 3 * width + (head + 1) * HEAD] = dgate.astype(bf16)
        dgained = dz * gate_act
        dgain = dgain + jnp.sum(dgained * normed, axis=0, keepdims=True)
        dnormed = dgained * gain
        dmixed = root * (dnormed - normed * jnp.mean(dnormed * normed, axis=-1, keepdims=True))
        outs[at] = dmixed.astype(bf16)
    enters = {(part, head): state_ref[head, part] for part, head in every}
    fresh = {at: (solved[at][:, HEAD:] - mm(weights[at], enters[at])).astype(bf16) for at in every}
    within = {at: mm_tn(scores[at], outs[at]) for at in every}
    across = {at: mm_tn(query_lows[at], outs[at]) for at in every}
    leavings, dfresh = {}, {}
    states = [dstate[head] for head in range(heads)]
    for part in reversed(range(count)):
        for head in range(heads):
            leavings[part, head] = states[head].astype(bf16)
        for head in range(heads):
            at = (part, head)
            dfresh[at] = (within[at] + mm(key_lows[at], leavings[at])).astype(bf16)
        for head in range(heads):
            at = (part, head)
            states[head] = states[head] + across[at] - mm_tn(weights[at], dfresh[at])
    for head in range(heads):
        dstate[head] = states[head]
    dscores = {at: jnp.where(row >= col, mm_nt(outs[at], fresh[at]), 0.0).astype(bf16) for at in every}
    dweights = {at: (-mm_nt(dfresh[at], enters[at])).astype(bf16) for at in every}
    dxys = {
        at: mm_tn(inv_ref[at[1], at[0]], jnp.concatenate([dweights[at], dfresh[at]], axis=1)) for at in every
    }
    dqueries = {at: mm_nt(outs[at], enters[at]) + mm(dscores[at], key_lows[at]) for at in every}
    dkeys = {at: mm_tn(dscores[at], query_lows[at]) + mm_nt(fresh[at], leavings[at]) for at in every}
    dsystems = {
        at: jnp.where(row > col, -mm_nt(dxys[at].astype(bf16), solved[at].astype(bf16)), 0.0) for at in every
    }
    dsystem_lows = {at: dsystems[at].astype(bf16) for at in every}
    firsts = {at: mm(dsystem_lows[at], key_lows[at]) for at in every}
    seconds = {at: mm_tn(dsystem_lows[at], stacks[at][:, :HEAD]) for at in every}
    grams = {at: mm_nt(key_lows[at], key_lows[at]) for at in every}
    for at in every:
        part, head = at
        beta, dx, dy, key = betas[at], dxys[at][:, :HEAD], dxys[at][:, HEAD:], keys[at]
        dkey = dkeys[at] + beta * (firsts[at] + dx) + seconds[at]
        convs = [of(conv_ref, kind, at) for kind in range(3)]
        sigs = [jax.nn.sigmoid(conv) for conv in convs]
        dbeta = jnp.sum(dsystems[at] * grams[at] + dx * key + dy * (convs[2] * sigs[2]), axis=-1, keepdims=True)
        dbeta = dbeta * beta * (1.0 - beta)
        dbeta_all[part] = jnp.where(beta_lane == head, dbeta, dbeta_all[part])
        unit_query, dquery = unit_queries[at], dqueries[at] * HEAD ** (-0.5)
        dquery = scales[at][0] * (dquery - unit_query * jnp.sum(unit_query * dquery, axis=-1, keepdims=True))
        dkey = scales[at][1] * (dkey - key * jnp.sum(key * dkey, axis=-1, keepdims=True))
        for kind, grad in enumerate((dquery, dkey, beta * dy)):
            dconv = grad * (sigs[kind] * (1.0 + convs[kind] * (1.0 - sigs[kind])))
            lanes = slice(kind * width + head * HEAD, kind * width + (head + 1) * HEAD)
            later[part * CHUNK : (part + 1) * CHUNK, lanes] = dconv
    for part in range(count):
        here = slice(part * CHUNK, (part + 1) * CHUNK)
        dbeta_low = dbeta_all[part].astype(bf16)
        dbeta_ref[here, :] = dbeta_low
        dsource_ref[...] += mm_tn(dbeta_low, source_ref[here, :])
    dgain_ref[...] += dgain
    for kind in range(3):
        for head in range(heads):
            lanes = slice(kind * width + head * HEAD, kind * width + (head + 1) * HEAD)
            source = pre_ref[:, lanes].astype(f32)
            total = jnp.zeros((rows, HEAD), f32)
            for tap in range(TAPS):
                at = kind * TAPS + tap
                shifted = later[TAPS - 1 - tap : TAPS - 1 - tap + rows, lanes]
                total = total + taps_ref[at : at + 1, head * HEAD : (head + 1) * HEAD] * shifted
                dtaps_ref[at : at + 1, head * HEAD : (head + 1) * HEAD] += jnp.sum(
                    source * shifted, axis=0, keepdims=True
                )
            dpre_ref[:, lanes] = total.astype(bf16)


def mixer_backward(pre, beta, source, conv, mixed, dz, inverse, states, taps, gain, heads):
    length, total = pre.shape
    model = source.shape[1]
    width = heads * HEAD
    steps, parts = length // STEP, STEP // CHUNK
    return pl.pallas_call(
        functools.partial(backward_kernel, heads),
        grid=(steps,),
        in_specs=[
            pl.BlockSpec((STEP, total), lambda i: (steps - 1 - i, 0)),
            pl.BlockSpec((STEP, BETA_PAD), lambda i: (steps - 1 - i, 0)),
            pl.BlockSpec((STEP, model), lambda i: (steps - 1 - i, 0)),
            pl.BlockSpec((STEP, 3 * width), lambda i: (steps - 1 - i, 0)),
            pl.BlockSpec((STEP, width), lambda i: (steps - 1 - i, 0)),
            pl.BlockSpec((STEP, width), lambda i: (steps - 1 - i, 0)),
            pl.BlockSpec((heads, parts, CHUNK, CHUNK), lambda i: (0, steps - 1 - i, 0, 0)),
            pl.BlockSpec((heads, parts, HEAD, HEAD), lambda i: (0, steps - 1 - i, 0, 0)),
            pl.BlockSpec((3 * TAPS, width), lambda i: (0, 0)),
            pl.BlockSpec((1, HEAD), lambda i: (0, 0)),
        ],
        out_specs=[
            pl.BlockSpec((STEP, total), lambda i: (steps - 1 - i, 0)),
            pl.BlockSpec((STEP, BETA_PAD), lambda i: (steps - 1 - i, 0)),
            pl.BlockSpec((BETA_PAD, model), lambda i: (0, 0)),
            pl.BlockSpec((3 * TAPS, width), lambda i: (0, 0)),
            pl.BlockSpec((1, HEAD), lambda i: (0, 0)),
        ],
        out_shape=[
            jax.ShapeDtypeStruct((length, total), bf16),
            jax.ShapeDtypeStruct((length, BETA_PAD), bf16),
            jax.ShapeDtypeStruct((BETA_PAD, model), f32),
            jax.ShapeDtypeStruct((3 * TAPS, width), f32),
            jax.ShapeDtypeStruct((1, HEAD), f32),
        ],
        scratch_shapes=[
            pltpu.VMEM((STEP + 8, 3 * width), f32),
            pltpu.VMEM((heads, HEAD, HEAD), f32),
        ],
        compiler_params=pltpu.CompilerParams(
            dimension_semantics=("arbitrary",), vmem_limit_bytes=VMEM_LIMIT
        ),
        cost_estimate=pl.CostEstimate(
            flops=1_000_000, bytes_accessed=1_000_000, transcendentals=0
        ),
    )(pre, beta, source, conv, mixed, dz, inverse, states, taps, gain)


MESH = pl.DeviceIdType.MESH
TILE = 16
LANES = 128
LARGE_LIMIT = 60 * 1024 * 1024


def remote(source, target, send, receive, **where):
    return pltpu.make_async_remote_copy(
        src_ref=source,
        dst_ref=target,
        send_sem=send,
        recv_sem=receive,
        device_id=where,
        device_id_type=MESH,
    )


def when(condition, action):
    pl.when(condition)(action)


def greet(**where):
    pl.semaphore_signal(
        pltpu.get_barrier_semaphore(), inc=1, device_id=where, device_id_type=MESH
    )


def wait_greetings(count):
    pl.semaphore_wait(pltpu.get_barrier_semaphore(), count)


def plane():
    me = lax.axis_index("tensor")
    across = me + 1 - 2 * lax.rem(me, 2)
    along = lax.rem(me + 2, 4)
    return me, across, along


def chip_and_core():
    index = lax.axis_index("dp")
    return index // 2, lax.rem(index, 2)


def greet_line(chips):
    chip, core = chip_and_core()
    greet(dp=chip * 2 + 1 - core)
    when(chip > 0, lambda: greet(dp=(chip - 1) * 2 + core))
    when(chip < chips - 1, lambda: greet(dp=(chip + 1) * 2 + core))
    return 1 + jnp.where(chip > 0, 1, 0) + jnp.where(chip < chips - 1, 1, 0)


class PlaneGather:
    def __init__(self, own, full, send, receive):
        self.own, self.full, self.send, self.receive = own, full, send, receive
        self.me, self.across, self.along = plane()
        self.far = lax.rem(self.across + 2, 4)
        self.rows = own.shape[0]
        self.half = self.rows // 2

    def slot(self, block, half):
        start = pl.multiple_of(block * self.rows + half * self.half, self.half)
        return self.full.at[pl.ds(start, self.half)]

    def mine(self, half):
        return self.own.at[pl.ds(half * self.half, self.half)]

    def out(self, half, kind):
        where = self.across if kind == 0 else self.along
        at = 2 * kind + half
        return remote(
            self.mine(half), self.slot(self.me, half), self.send.at[at], self.receive.at[at], tensor=where
        )

    def arriving(self, half, kind):
        block = self.across if kind == 0 else self.along
        at = 2 * kind + half
        view = self.slot(block, half)
        return remote(view, view, self.send.at[at], self.receive.at[at], tensor=block)

    def passing(self, kind):
        view = self.slot(self.across if kind == 0 else self.along, kind)
        where = self.along if kind == 0 else self.across
        return remote(view, view, self.send.at[4 + kind], self.receive.at[4 + kind], tensor=where)

    def passed(self, kind):
        view = self.slot(self.far, kind)
        where = self.along if kind == 0 else self.across
        return remote(view, view, self.send.at[4 + kind], self.receive.at[4 + kind], tensor=where)

    def start(self, half):
        for kind in (half, 1 - half):
            self.out(half, kind).start()

    def relay(self, kind):
        self.arriving(kind, kind).wait_recv()
        self.passing(kind).start()

    def near(self, kind):
        self.arriving(1 - kind, kind).wait_recv()

    def diagonal(self):
        self.passed(0).wait_recv()
        self.passed(1).wait_recv()

    def finish(self):
        self.near(0)
        self.near(1)
        self.diagonal()
        self.sent()

    def sent(self):
        for kind in (0, 1):
            self.passing(kind).wait_send()
            for half in (0, 1):
                self.out(half, kind).wait_send()


class PlaneScatter:
    def __init__(self, part, first, second, stage, send, receive):
        self.part, self.first, self.second, self.stage = part, first, second, stage
        self.send, self.receive = send, receive
        self.me, self.across, self.along = plane()
        self.far = lax.rem(self.across + 2, 4)
        self.rows = part.shape[0] // 4
        self.half = self.rows // 2

    def start_of(self, block, half):
        return pl.multiple_of(block * self.rows + half * self.half, self.half)

    def view(self, block, half):
        return self.part.at[pl.ds(self.start_of(block, half), self.half)]

    def out(self, kind, order):
        where = self.across if kind == 0 else self.along
        at = 2 * kind + order
        return remote(
            self.view(self.far if order == 0 else where, kind),
            self.first.at[at],
            self.send.at[at],
            self.receive.at[at],
            tensor=where,
        )

    def over(self, kind):
        where = self.along if kind == 0 else self.across
        return remote(
            self.stage.at[kind], self.second.at[kind], self.send.at[4 + kind], self.receive.at[4 + kind], tensor=where
        )

    def start_far(self):
        for kind in (0, 1):
            self.out(kind, 0).start()

    def start_near(self, kind):
        self.out(kind, 1).start()

    def relay(self, kind):
        self.out(kind, 0).wait_recv()
        block = self.along if kind == 0 else self.across
        start = self.start_of(block, kind)

        def add(index, carry):
            at = pl.multiple_of(index * TILE, TILE)
            mine = self.part[pl.ds(pl.multiple_of(start + at, TILE), TILE), :].astype(f32)
            other = self.first[2 * kind, pl.ds(at, TILE), :].astype(f32)
            self.stage[kind, pl.ds(at, TILE), :] = (mine + other).astype(bf16)
            return carry

        lax.fori_loop(0, self.half // TILE, add, 0)
        self.over(kind).start()

    def ready(self, kind):
        self.out(kind, 1).wait_recv()
        self.over(kind).wait_recv()

    def tile(self, kind, at):
        start = self.start_of(self.me, kind)
        mine = self.part[pl.ds(pl.multiple_of(start + at, TILE), TILE), :].astype(f32)
        near = self.first[2 * kind + 1, pl.ds(at, TILE), :].astype(f32)
        return mine + near + self.second[kind, pl.ds(at, TILE), :].astype(f32)

    def finish(self):
        for kind in (0, 1):
            for order in (0, 1):
                self.out(kind, order).wait_send()
            self.over(kind).wait_send()


def plane_scatter_scratch(rows, columns):
    half = rows // 2
    return [
        pltpu.VMEM((4, half, columns), bf16),
        pltpu.VMEM((2, half, columns), bf16),
        pltpu.VMEM((2, half, columns), bf16),
        pltpu.SemaphoreType.DMA((6,)),
        pltpu.SemaphoreType.DMA((6,)),
    ]


def pieces_of(arrays, size):
    found = []
    for index, array in enumerate(arrays):
        rows, columns = array.shape[-2:]
        count = max(1, min(rows // 64, round(rows * columns / size)))
        while rows % count or (rows // count) % 16:
            count -= 1
        for piece in range(count):
            found.append((index, piece * (rows // count), rows // count))
    return found


PIECE = 64 * 2176


class LineGather:
    def __init__(self, chips, owns, fulls, sems):
        self.chips, self.owns, self.fulls = chips, owns, fulls
        self.pieces = pieces_of(owns, PIECE)
        self.right_send, self.right_receive, self.left_send, self.left_receive = sems[:4]
        self.core_send, self.core_receive, self.local = sems[4:]
        self.chip, self.core = chip_and_core()

    @staticmethod
    def scratch(chips, pieces, arrays):
        return [pltpu.SemaphoreType.DMA((chips, pieces)) for _ in range(6)] + [pltpu.SemaphoreType.DMA((arrays,))]

    def slot(self, piece, chip, core):
        index, start, rows = self.pieces[piece]
        return self.fulls[index].at[chip * 2 + core, pl.ds(start, rows)]

    def source(self, piece, away):
        index, start, rows = self.pieces[piece]
        return self.owns[index].at[pl.ds(start, rows)]

    def right(self, piece, away, chip):
        slot = self.slot(piece, chip, self.core)
        source = self.source(piece, 0) if away == 0 else slot
        to = (self.chip + 1) * 2 + self.core
        return remote(source, slot, self.right_send.at[away, piece], self.right_receive.at[away, piece], dp=to)

    def left(self, piece, away, chip):
        slot = self.slot(piece, chip, self.core)
        source = self.source(piece, 0) if away == 0 else slot
        to = (self.chip - 1) * 2 + self.core
        return remote(source, slot, self.left_send.at[away, piece], self.left_receive.at[away, piece], dp=to)

    def trade(self, piece, chip, own):
        slot = self.slot(piece, chip, self.core)
        source = self.source(piece, 0) if own else slot
        to = self.chip * 2 + 1 - self.core
        return remote(source, slot, self.core_send.at[chip, piece], self.core_receive.at[chip, piece], dp=to)

    def keep(self, index):
        return pltpu.make_async_copy(
            self.owns[index], self.fulls[index].at[self.chip * 2 + self.core], self.local.at[index]
        )

    def start(self):
        for piece in range(len(self.pieces)):
            when(self.chip < self.chips - 1, lambda: self.right(piece, 0, self.chip).start())
            when(self.chip > 0, lambda: self.left(piece, 0, self.chip).start())
        for piece in range(len(self.pieces)):
            self.trade(piece, self.chip, True).start()
        for index in range(len(self.owns)):
            self.keep(index).start()

    def step(self, away):
        for piece in range(len(self.pieces)):

            def from_left():
                chip = self.chip - away
                self.right(piece, away - 1, chip).wait_recv()
                if away < self.chips - 1:
                    when(self.chip < self.chips - 1, lambda: self.right(piece, away, chip).start())
                self.trade(piece, chip, False).start()

            def from_right():
                chip = self.chip + away
                self.left(piece, away - 1, chip).wait_recv()
                if away < self.chips - 1:
                    when(self.chip > 0, lambda: self.left(piece, away, chip).start())
                self.trade(piece, chip, False).start()

            when(self.chip >= away, from_left)
            when(self.chip + away < self.chips, from_right)

    def finish(self):
        for index in range(len(self.owns)):
            self.keep(index).wait()
        for piece in range(len(self.pieces)):
            for away in range(self.chips - 1):
                when(
                    (self.chip < self.chips - 1) & (self.chip >= away),
                    lambda: self.right(piece, away, self.chip - away).wait_send(),
                )
                when(
                    (self.chip > 0) & (self.chip + away < self.chips),
                    lambda: self.left(piece, away, self.chip + away).wait_send(),
                )
            for chip in range(self.chips):
                trade = remote(
                    self.slot(piece, chip, self.core),
                    self.slot(piece, chip, 1 - self.core),
                    self.core_send.at[chip, piece],
                    self.core_receive.at[chip, piece],
                    dp=self.chip * 2 + 1 - self.core,
                )
                trade.wait_send()
                trade.wait_recv()


def first_gather_kernel(chips, *refs):
    w_query, w_key, w_value, w_gate_out, w_beta, w_output, inputs, cotangent, mask, gain = refs[:10]
    w_gate, w_up, w_down = refs[10:13]
    inner_full, output_full, beta_full, normed_full, grad_full, gate_up, down, grad = refs[13:21]
    inner, output, normed, gate_wide, up_wide, down_wide = refs[21:27]
    sems = refs[27:]
    width, hidden = w_query.shape[1], w_gate.shape[1]
    line = LineGather(chips, [inner, output, w_beta], [inner_full, output_full, beta_full], sems[:7])
    rows = [PlaneGather(normed, normed_full, *sems[7:9]), PlaneGather(grad, grad_full, *sems[9:11])]
    local = sems[11]
    keeps = [
        pltpu.make_async_copy(
            own, full.at[pl.ds(pl.multiple_of(each.me * each.rows, each.rows), each.rows)], local.at[at]
        )
        for at, (own, full, each) in enumerate(((normed, normed_full, rows[0]), (grad, grad_full, rows[1])))
    ]
    loads = [
        pltpu.make_async_copy(source, target, local.at[2 + at])
        for at, (source, target) in enumerate(((w_gate, gate_wide), (w_up, up_wide), (w_down, down_wide)))
    ]
    greetings = greet_line(chips)
    greet(tensor=rows[0].across)
    greet(tensor=rows[0].along)
    for kind, weight in enumerate((w_query, w_key, w_value, w_gate_out)):
        inner[:, kind * width : (kind + 1) * width] = weight[...].astype(bf16)
    output[...] = jnp.transpose(w_output[...]).astype(bf16)
    wait_greetings(2 + greetings)
    line.start()
    for load in loads:
        load.start()

    def norm(index, carry):
        here = pl.ds(pl.multiple_of(index * TILE, TILE), TILE)
        value = inputs[here, :].astype(f32)
        scale = lax.rsqrt(jnp.mean(value * value, axis=-1, keepdims=True) + norm_epsilon)
        normed[here, :] = (value * scale * gain[...]).astype(bf16)
        grad[here, :] = (cotangent[here, :].astype(f32) * mask[here, :]).astype(bf16)
        return carry

    lax.fori_loop(0, inputs.shape[0] // TILE, norm, 0)
    for each in rows:
        each.start(0)
        each.start(1)
    for keep in keeps:
        keep.start()
    for load in loads:
        load.wait()
    for kind, wide in enumerate((gate_wide, up_wide)):
        for tile in range(hidden // LANES):
            to = (2 * tile + kind) * LANES
            gate_up[:, to : to + LANES] = wide[:, tile * LANES : (tile + 1) * LANES].astype(bf16)
    down[...] = jnp.transpose(down_wide[...]).astype(bf16)
    rows[0].relay(0)
    rows[0].relay(1)
    line.step(1)
    rows[1].relay(0)
    rows[1].relay(1)
    for away in range(2, chips):
        line.step(away)
    for each in rows:
        each.finish()
    for keep in keeps:
        keep.wait()
    line.finish()


def ffn_kernel(normed, weight, middle, slopes):
    def block(index, carry):
        here = pl.ds(pl.multiple_of(index * 512, 512), 512)
        both = mm(normed[here, :], weight[...])
        gate, up_part = both[:, :LANES], both[:, LANES:]
        act, sig = silu_parts(gate)
        middle[here, :] = (act * up_part).astype(bf16)
        slopes[here, :LANES] = (up_part * sig * (1.0 + gate * (1.0 - sig))).astype(bf16)
        slopes[here, LANES:] = act.astype(bf16)
        return carry

    lax.fori_loop(0, normed.shape[0] // 512, block, 0, unroll=True)


def ffn(normed, gate_up):
    length, model = normed.shape
    hidden = gate_up.shape[1] // 2
    return pl.pallas_call(
        ffn_kernel,
        grid=(hidden // LANES,),
        in_specs=[
            pl.BlockSpec((length, model), lambda i: (0, 0)),
            pl.BlockSpec((model, 2 * LANES), lambda i: (0, i)),
        ],
        out_specs=[
            pl.BlockSpec((length, LANES), lambda i: (0, i)),
            pl.BlockSpec((length, 2 * LANES), lambda i: (0, i)),
        ],
        out_shape=[
            jax.ShapeDtypeStruct((length, hidden), bf16),
            jax.ShapeDtypeStruct((length, 2 * hidden), bf16),
        ],
        compiler_params=pltpu.CompilerParams(
            dimension_semantics=("arbitrary",), vmem_limit_bytes=VMEM_LIMIT
        ),
        cost_estimate=pl.CostEstimate(
            flops=4 * length * model * hidden, bytes_accessed=2 * (length * model + 2 * model * hidden), transcendentals=length * hidden
        ),
    )(normed, gate_up)


def ffn_backward_kernel(grad, weight, slopes, grad_both):
    grad_middle = mm(grad[...], weight[...])
    for tile in range(weight.shape[1] // LANES):
        part = grad_middle[:, tile * LANES : (tile + 1) * LANES]
        for kind in range(2):
            lanes = slice((2 * tile + kind) * LANES, (2 * tile + kind + 1) * LANES)
            grad_both[:, lanes] = (part * slopes[:, lanes].astype(f32)).astype(bf16)


def ffn_backward(grad, down, slopes):
    length, model = grad.shape
    hidden = down.shape[1]
    block = 512
    return pl.pallas_call(
        ffn_backward_kernel,
        grid=(length // block,),
        in_specs=[
            pl.BlockSpec((block, model), lambda i: (i, 0)),
            pl.BlockSpec((model, hidden), lambda i: (0, 0)),
            pl.BlockSpec((block, 2 * hidden), lambda i: (i, 0)),
        ],
        out_specs=pl.BlockSpec((block, 2 * hidden), lambda i: (i, 0)),
        out_shape=jax.ShapeDtypeStruct((length, 2 * hidden), bf16),
        compiler_params=pltpu.CompilerParams(
            dimension_semantics=("arbitrary",), vmem_limit_bytes=VMEM_LIMIT
        ),
        cost_estimate=pl.CostEstimate(
            flops=2 * length * model * hidden, bytes_accessed=2 * (length * model + model * hidden + 4 * length * hidden), transcendentals=0
        ),
    )(grad, down, slopes)


def finish_kernel(count, *refs):
    both, down = refs[:2]
    sources, gate_out, up_out, down_out = refs[2 : 2 + count], *refs[2 + count : 5 + count]
    targets, held, sems = refs[5 + count : 5 + 2 * count], refs[5 + 2 * count : 5 + 3 * count], refs[-1]
    loads = [
        pltpu.make_async_copy(source, here, sems.at[0, at]) for at, (source, here) in enumerate(zip(sources, held))
    ]
    stores = [
        pltpu.make_async_copy(here, target, sems.at[1, at]) for at, (here, target) in enumerate(zip(held, targets))
    ]
    for load in loads:
        load.start()
    for tile in range(gate_out.shape[1] // LANES):
        lanes = slice(tile * LANES, (tile + 1) * LANES)
        gate_out[:, lanes] = both[:, 2 * tile * LANES : (2 * tile + 1) * LANES].astype(f32)
        up_out[:, lanes] = both[:, (2 * tile + 1) * LANES : (2 * tile + 2) * LANES].astype(f32)
    for load, store in zip(loads, stores):
        load.wait()
        store.start()
    for tile in range(gate_out.shape[1] // LANES):
        lanes = slice(tile * LANES, (tile + 1) * LANES)
        down_out[lanes, :] = jnp.transpose(down[:, lanes].astype(f32))
    for store in stores:
        store.wait()


def finish(both, down, arrays):
    slab, hidden = down.shape
    return pl.pallas_call(
        functools.partial(finish_kernel, len(arrays)),
        in_specs=in_vmem(2) + anywhere(len(arrays)),
        out_specs=in_vmem(3) + anywhere(len(arrays)),
        out_shape=[
            jax.ShapeDtypeStruct((slab, hidden), f32),
            jax.ShapeDtypeStruct((slab, hidden), f32),
            jax.ShapeDtypeStruct((hidden, slab), f32),
        ]
        + [jax.ShapeDtypeStruct(array.shape, array.dtype) for array in arrays],
        scratch_shapes=[pltpu.VMEM(array.shape, array.dtype) for array in arrays]
        + [pltpu.SemaphoreType.DMA((2, len(arrays)))],
        compiler_params=pltpu.CompilerParams(vmem_limit_bytes=VMEM_LIMIT),
        cost_estimate=pl.CostEstimate(flops=0, bytes_accessed=40 * slab * hidden, transcendentals=0),
    )(both, down, *arrays)


def plain_ffn(normed, gate_up):
    gate, up_part = jnp.split(jnp.dot(normed, gate_up, preferred_element_type=f32), 2, axis=1)
    act, sig = silu_parts(gate)
    slopes = jnp.concatenate([up_part * sig * (1.0 + gate * (1.0 - sig)), act], axis=1)
    return (act * up_part).astype(bf16), slopes.astype(bf16)


def plain_ffn_backward(grad, down, slopes):
    grad_middle = jnp.dot(grad, down, preferred_element_type=f32)
    return (jnp.concatenate([grad_middle, grad_middle], axis=1) * slopes.astype(f32)).astype(bf16)


def plain_finish(both, down, arrays):
    gate, up_part = jnp.split(both.astype(f32), 2, axis=1)
    return gate, up_part, down.astype(f32).T, *arrays


def anywhere(count):
    return [pl.BlockSpec(memory_space=pl.ANY)] * count


def in_vmem(count):
    return [pl.BlockSpec(memory_space=pltpu.VMEM)] * count


def first_gather(w_query, w_key, w_value, w_gate_out, w_beta, w_output, inputs, cotangent, mask, gain, w_gate, w_up, w_down):
    shards = lax.axis_size("dp")
    rows, model = inputs.shape
    slab, width = w_query.shape
    hidden = w_gate.shape[1]
    inner = jax.ShapeDtypeStruct((slab, 4 * width), bf16)
    output = jax.ShapeDtypeStruct((slab, width), bf16)
    pieces = len(pieces_of([inner, output, w_beta], PIECE))
    return pl.pallas_call(
        functools.partial(first_gather_kernel, shards // 2),
        in_specs=in_vmem(10) + anywhere(3),
        out_specs=anywhere(5) + in_vmem(3),
        out_shape=[
            jax.ShapeDtypeStruct((shards, *inner.shape), bf16),
            jax.ShapeDtypeStruct((shards, *output.shape), bf16),
            jax.ShapeDtypeStruct((shards, *w_beta.shape), bf16),
            jax.ShapeDtypeStruct((4 * rows, model), bf16),
            jax.ShapeDtypeStruct((4 * rows, model), bf16),
            jax.ShapeDtypeStruct((slab, 2 * hidden), bf16),
            jax.ShapeDtypeStruct((slab, hidden), bf16),
            jax.ShapeDtypeStruct((rows, model), bf16),
        ],
        scratch_shapes=[
            pltpu.VMEM(inner.shape, bf16),
            pltpu.VMEM(output.shape, bf16),
            pltpu.VMEM((rows, model), bf16),
            pltpu.VMEM((slab, hidden), f32),
            pltpu.VMEM((slab, hidden), f32),
            pltpu.VMEM((hidden, slab), f32),
        ]
        + LineGather.scratch(shards // 2, pieces, 3)
        + [pltpu.SemaphoreType.DMA((6,)) for _ in range(4)]
        + [pltpu.SemaphoreType.DMA((5,))],
        compiler_params=pltpu.CompilerParams(
            collective_id=1, has_side_effects=True, vmem_limit_bytes=VMEM_LIMIT
        ),
        cost_estimate=pl.CostEstimate(flops=80_000_000_000, bytes_accessed=20_000_000, transcendentals=0),
    )(w_query, w_key, w_value, w_gate_out, w_beta, w_output, inputs, cotangent, mask, gain, w_gate, w_up, w_down)


def branch_kernel(z, weight, inputs, gain, resid, full, part, first, second, stage, low, s_send, s_recv, g_send, g_recv, local):
    scatter = PlaneScatter(part, first, second, stage, s_send, s_recv)
    gather = PlaneGather(low, full, g_send, g_recv)
    rows = scatter.rows
    slab = weight.shape[1]
    greet(tensor=scatter.across)
    greet(tensor=scatter.along)

    def compute(block):
        here = pl.ds(scatter.start_of(block, 0), rows)

        def column(index, carry):
            part[here, pl.ds(pl.multiple_of(index * slab, slab), slab)] = mm_nt(z[here, :], weight[index]).astype(bf16)
            return carry

        lax.fori_loop(0, weight.shape[0], column, 0)

    compute(scatter.far)
    wait_greetings(2)
    scatter.start_far()
    compute(scatter.across)
    scatter.start_near(0)
    compute(scatter.along)
    scatter.start_near(1)
    compute(scatter.me)
    scatter.relay(0)
    scatter.relay(1)
    for half in (0, 1):
        scatter.ready(half)

        def norm(index, carry):
            at = pl.multiple_of(index * TILE, TILE)
            here = pl.ds(pl.multiple_of(half * scatter.half + at, TILE), TILE)
            value = inputs[here, :].astype(f32) + scatter.tile(half, at)
            resid[here, :] = value
            scale = lax.rsqrt(jnp.mean(value * value, axis=-1, keepdims=True) + norm_epsilon)
            low[here, :] = (value * scale * gain[...]).astype(bf16)
            return carry

        lax.fori_loop(0, scatter.half // TILE, norm, 0)
        gather.start(half)
    keep = pltpu.make_async_copy(low, full.at[pl.ds(pl.multiple_of(gather.me * rows, rows), rows)], local.at[0])
    keep.start()
    gather.relay(0)
    gather.relay(1)
    scatter.finish()
    gather.finish()
    keep.wait()


def branch_and_norm(z, weight, inputs, gain):
    rows, model = inputs.shape
    return pl.pallas_call(
        branch_kernel,
        in_specs=in_vmem(4),
        out_specs=in_vmem(1) + anywhere(1),
        out_shape=[
            jax.ShapeDtypeStruct((rows, model), f32),
            jax.ShapeDtypeStruct((4 * rows, model), bf16),
        ],
        scratch_shapes=[pltpu.VMEM((4 * rows, model), bf16)]
        + plane_scatter_scratch(rows, model)[:3]
        + [pltpu.VMEM((rows, model), bf16)]
        + [pltpu.SemaphoreType.DMA((6,)) for _ in range(4)]
        + [pltpu.SemaphoreType.DMA((1,))],
        compiler_params=pltpu.CompilerParams(
            collective_id=2, has_side_effects=True, vmem_limit_bytes=VMEM_LIMIT
        ),
        cost_estimate=pl.CostEstimate(flops=50_000_000_000, bytes_accessed=20_000_000, transcendentals=0),
    )(z, weight, inputs, gain)


def norm_backward(value, grad, gain):
    scale = lax.rsqrt(jnp.mean(value * value, axis=-1, keepdims=True) + norm_epsilon)
    normed = value * scale
    inner = grad * gain
    return scale * (inner - normed * jnp.mean(inner * normed, axis=-1, keepdims=True)), grad * normed


class LineScatter:
    def __init__(self, chips, parts, stages, trades, arrived, sems):
        self.chips, self.parts, self.stages, self.trades, self.arrived = chips, parts, stages, trades, arrived
        self.pieces = pieces_of(parts, PIECE)
        self.right_send, self.right_receive, self.left_send, self.left_receive = sems[:4]
        self.core_send, self.core_receive, self.local = sems[4:]
        self.chip, self.core = chip_and_core()

    @staticmethod
    def scratch(chips, arrays):
        shapes = [array.shape[-2:] for array in arrays]
        pieces = len(pieces_of(arrays, PIECE))
        return (
            [pltpu.VMEM((chips, *shape), bf16) for shape in shapes]
            + [pltpu.VMEM((chips, *shape), bf16) for shape in shapes]
            + [pltpu.VMEM((chips + 1, *shape), bf16) for shape in shapes]
            + [pltpu.SemaphoreType.DMA((chips, pieces)) for _ in range(6)]
            + [pltpu.SemaphoreType.DMA((len(arrays), chips))]
        )

    def order(self):
        order = []
        for step in range(self.chips // 2):
            order += [self.chips - 1 - step, step]
        return order

    def trade(self, piece, dest):
        index, start, rows = self.pieces[piece]
        return remote(
            self.parts[index].at[dest * 2 + 1 - self.core, pl.ds(start, rows)],
            self.trades[index].at[dest, pl.ds(start, rows)],
            self.core_send.at[dest, piece],
            self.core_receive.at[dest, piece],
            dp=self.chip * 2 + 1 - self.core,
        )

    def load(self, index, dest):
        return pltpu.make_async_copy(
            self.parts[index].at[dest * 2 + self.core], self.stages[index].at[dest], self.local.at[index, dest]
        )

    def right(self, piece, dest):
        index, start, rows = self.pieces[piece]
        here = pl.ds(start, rows)
        return remote(
            self.stages[index].at[dest, here],
            self.arrived[index].at[dest, here],
            self.right_send.at[dest, piece],
            self.right_receive.at[dest, piece],
            dp=(self.chip + 1) * 2 + self.core,
        )

    def left_slot(self, dest, chip):
        return jnp.where(dest == chip, self.chips, dest)

    def left(self, piece, dest):
        index, start, rows = self.pieces[piece]
        here = pl.ds(start, rows)
        return remote(
            self.stages[index].at[dest, here],
            self.arrived[index].at[self.left_slot(dest, self.chip - 1), here],
            self.left_send.at[dest, piece],
            self.left_receive.at[dest, piece],
            dp=(self.chip - 1) * 2 + self.core,
        )

    def start(self):
        for dest in self.order():
            for index in range(len(self.parts)):
                self.load(index, dest).start()
            for piece in range(len(self.pieces)):
                self.trade(piece, dest).start()

    def add(self, piece, dest, slots, put=None):
        index, start, rows = self.pieces[piece]

        def tile(at, carry):
            here = pl.ds(pl.multiple_of(start + at * TILE, TILE), TILE)
            total = self.stages[index][dest, here, :].astype(f32) + self.trades[index][dest, here, :].astype(f32)
            for slot in slots:
                total = total + self.arrived[index][slot, here, :].astype(f32)
            if put is None:
                self.stages[index][dest, here, :] = total.astype(bf16)
            else:
                put[index](here, total)
            return carry

        lax.fori_loop(0, rows // TILE, tile, 0)

    def first_of(self, piece):
        return piece == 0 or self.pieces[piece - 1][0] != self.pieces[piece][0]

    def receive(self, piece, dest):
        if self.first_of(piece):
            self.load(self.pieces[piece][0], dest).wait()
        self.trade(piece, dest).wait_recv()

    def step(self, step, ends):
        to_right, to_left = self.chips - 1 - step, step

        def send_right(piece):
            self.receive(piece, to_right)
            if not ends:
                self.right(piece, to_right).wait_recv()
            self.add(piece, to_right, [] if ends else [to_right])
            self.right(piece, to_right).start()

        def send_left(piece):
            self.receive(piece, to_left)
            if not ends:
                self.left(piece, to_left).wait_recv()
            self.add(piece, to_left, [] if ends else [to_left])
            self.left(piece, to_left).start()

        count = len(self.pieces)
        if ends:
            when(self.chip == 0, lambda: [send_right(piece) for piece in range(count)] and None)
            when(self.chip == self.chips - 1, lambda: [send_left(piece) for piece in range(count)] and None)
            return
        inner_right = (self.chip > 0) & (to_right > self.chip)
        inner_left = (self.chip < self.chips - 1) & (to_left < self.chip)
        low = self.chip < self.chips // 2
        lead = 2
        for at in range(count + lead):
            early, late = at, at - lead
            if early < count:
                when(low & inner_right, functools.partial(send_right, early))
                when(jnp.logical_not(low) & inner_left, functools.partial(send_left, early))
            if late >= 0:
                when(low & inner_left, functools.partial(send_left, late))
                when(jnp.logical_not(low) & inner_right, functools.partial(send_right, late))

    def keep(self, outs, pieces):
        me = self.chip
        for piece in pieces:
            self.receive(piece, me)
            when(me > 0, lambda: self.right(piece, me).wait_recv())
            when(me < self.chips - 1, lambda: self.left(piece, me).wait_recv())
            when((me > 0) & (me < self.chips - 1), lambda: self.add(piece, me, [me, self.chips], outs))
            when(me == 0, lambda: self.add(piece, me, [self.chips], outs))
            when(me == self.chips - 1, lambda: self.add(piece, me, [me], outs))

    def finish(self):
        for piece in range(len(self.pieces)):
            for dest in range(self.chips):
                self.trade(piece, dest).wait_send()
                when(dest > self.chip, lambda: self.right(piece, dest).wait_send())
                when(dest < self.chip, lambda: self.left(piece, dest).wait_send())


def resid_kernel(
    slab, grad_far, weight_far, z_far, out_weight_far, resid, grad_out, gain, grad_resid, dgain, dz, output_grad,
    part, first, second, stage, low, full, total, s_send, s_recv, g_send, g_recv,
    grad_both, weight, z, out_weight, load_sems
):
    scatter = PlaneScatter(part, first, second, stage, s_send, s_recv)
    gather = PlaneGather(low, full, g_send, g_recv)
    rows = scatter.rows
    slabs = weight.shape[0] // slab
    order = (scatter.far, scatter.across, scatter.along, scatter.me)
    greet(tensor=scatter.across)
    greet(tensor=scatter.along)

    def rows_load(at):
        here = pl.ds(scatter.start_of(order[at], 0), rows)
        return pltpu.make_async_copy(grad_far.at[here], grad_both.at[here], load_sems.at[slabs + at])

    def slab_load(index):
        here = pl.ds(pl.multiple_of(index * slab, slab), slab)
        return pltpu.make_async_copy(weight_far.at[here], weight.at[here], load_sems.at[index])

    late_loads = [
        pltpu.make_async_copy(z_far, z, load_sems.at[slabs + 4]),
        pltpu.make_async_copy(out_weight_far, out_weight, load_sems.at[slabs + 5]),
    ]
    for at in range(4):
        rows_load(at).start()
        if at == 0:
            for index in range(slabs):
                slab_load(index).start()
    for load in late_loads:
        load.start()

    def compute(at):
        here = pl.ds(scatter.start_of(order[at], 0), rows)
        rows_load(at).wait()

        def column(index, carry):
            lanes = pl.ds(pl.multiple_of(index * slab, slab), slab)
            if at == 0:
                slab_load(index).wait()
            part[here, lanes] = mm_nt(grad_both[here, :], weight[lanes, :]).astype(bf16)
            return carry

        lax.fori_loop(0, slabs, column, 0)

    compute(0)
    wait_greetings(2)
    scatter.start_far()
    compute(1)
    scatter.start_near(0)
    compute(2)
    scatter.start_near(1)
    compute(3)
    dgain[...] = jnp.zeros_like(dgain)
    scatter.relay(0)
    scatter.relay(1)
    for half in (0, 1):
        scatter.ready(half)

        def norm(index, carry):
            at = pl.multiple_of(index * TILE, TILE)
            here = pl.ds(pl.multiple_of(half * scatter.half + at, TILE), TILE)
            back, gain_part = norm_backward(resid[here, :], scatter.tile(half, at), gain[...])
            value = grad_out[here, :].astype(f32) + back
            grad_resid[here, :] = value
            low[here, :] = value.astype(bf16)
            dgain[...] += jnp.sum(gain_part, axis=0, keepdims=True)
            return carry

        lax.fori_loop(0, scatter.half // TILE, norm, 0)
        gather.start(half)
    for load in late_loads:
        load.wait()

    def use(block, left, fresh=False):
        here = pl.ds(pl.multiple_of(block * rows, rows), rows)
        dz[here, :] = mm(left[...], out_weight[...]).astype(bf16)

        def column(index, carry):
            lanes = pl.ds(pl.multiple_of(index * slab, slab), slab)
            product = mm_tn(left[:, lanes], z[here, :])
            total[lanes, :] = product if fresh else total[lanes, :] + product
            return carry

        lax.fori_loop(0, slabs, column, 0)

    def block_of(block):
        return full.at[pl.ds(pl.multiple_of(block * rows, rows), rows)]

    gather.relay(0)
    gather.relay(1)
    use(scatter.me, low, True)
    gather.near(0)
    use(scatter.across, block_of(scatter.across))
    gather.near(1)
    use(scatter.along, block_of(scatter.along))

    gather.diagonal()
    use(scatter.far, block_of(scatter.far))
    output_grad[...] = total[...].astype(bf16)
    gather.sent()
    scatter.finish()


def resid_backward(grad_both, weight, z, out_weight, resid, grad_out, gain):
    rows, model = resid.shape
    width = z.shape[1]
    return pl.pallas_call(
        functools.partial(resid_kernel, 256),
        in_specs=anywhere(4) + in_vmem(3),
        out_specs=in_vmem(4),
        out_shape=[
            jax.ShapeDtypeStruct((rows, model), f32),
            jax.ShapeDtypeStruct((1, model), f32),
            jax.ShapeDtypeStruct((4 * rows, width), bf16),
            jax.ShapeDtypeStruct((model, width), bf16),
        ],
        scratch_shapes=[pltpu.VMEM((4 * rows, model), bf16)]
        + plane_scatter_scratch(rows, model)[:3]
        + [
            pltpu.VMEM((rows, model), bf16),
            pltpu.VMEM((4 * rows, model), bf16),
            pltpu.VMEM((model, width), f32),
        ]
        + [pltpu.SemaphoreType.DMA((6,)) for _ in range(4)]
        + [
            pltpu.VMEM((4 * rows, weight.shape[1]), bf16),
            pltpu.VMEM(weight.shape, bf16),
            pltpu.VMEM(z.shape, bf16),
            pltpu.VMEM(out_weight.shape, bf16),
            pltpu.SemaphoreType.DMA((model // 256 + 6,)),
        ],
        compiler_params=pltpu.CompilerParams(
            collective_id=3, has_side_effects=True, vmem_limit_bytes=LARGE_LIMIT
        ),
        cost_estimate=pl.CostEstimate(flops=1_000_000, bytes_accessed=1_000_000, transcendentals=0),
    )(grad_both, weight, z, out_weight, resid, grad_out, gain)


SMALL = 512


def last_kernel(chips, *refs):
    inner_part, output_part, weight, inner, dpre_far, middle_far, inputs_far, grad_resid_far, resid_far = refs[:9]
    mask, first_gain, ffn_dgain, head_dgain, dtaps, dbeta, beta, beta_part = refs[9:17]
    refs = refs[3:]
    query_out, key_out, value_out, gate_out, beta_out, output_out, input_grad, out = refs[14:22]
    first_out, ffn_out, head_out, taps_out = refs[22:26]
    refs = refs[26:]
    line = LineScatter(chips, [inner_part, output_part], refs[:2], refs[2:4], refs[4:6], refs[6:13])
    grad = PlaneScatter(*refs[13:19])
    ffn = PlaneScatter(*refs[19:25])
    turned, small, near, lined, dgain, small_send, small_receive, inner_slabs, down_slabs, slab_sems = refs[25:35]
    dpre, middle, inputs, grad_resid, resid, load_sems = refs[35:41]
    chip, core = line.chip, line.core
    slab = inner_part.shape[1]
    shards = 2 * chips
    sibling = chip * 2 + 1 - core
    greet(tensor=grad.across)
    greet(tensor=grad.along)
    greet(dp=sibling)
    for other in range(1, chips):
        greet(dp=lax.rem(chip + other, chips) * 2 + core)

    def stream(at, source, buffers, kind):
        return pltpu.make_async_copy(source.at[at], buffers.at[lax.rem(at, 2)], slab_sems.at[kind, lax.rem(at, 2)])

    def product(left, source, buffers, target, kind, extra=None):
        def column(index, carry):
            when(index < shards - 1, lambda: stream(index + 1, source, buffers, kind).start())
            stream(index, source, buffers, kind).wait()
            lanes = pl.ds(pl.multiple_of(index * slab, slab), slab)
            total = mm_nt(left[...], buffers[lax.rem(index, 2)])
            if extra is not None:
                total = total + mm(extra[0][...], extra[1][index])
            target[:, lanes] = total.astype(bf16)
            return carry

        lax.fori_loop(0, shards, column, 0)

    loads = [
        pltpu.make_async_copy(source, target, load_sems.at[at])
        for at, (source, target) in enumerate(
            (
                (dpre_far, dpre),
                (middle_far, middle),
                (inputs_far, inputs),
                (grad_resid_far, grad_resid),
                (resid_far, resid),
            )
        )
    ]
    wait_greetings(2 + chips)
    line.start()
    for load in loads[:2]:
        load.start()
    stream(0, inner, inner_slabs, 0).start()
    stream(0, weight, down_slabs, 1).start()
    for load in loads[2:]:
        load.start()
    dgain[...] = jnp.zeros_like(dgain)
    small[...] = jnp.zeros_like(small)
    line.step(0, True)
    loads[0].wait()
    product(dpre, inner, inner_slabs, grad.part, 0, (dbeta, beta))
    grad.start_far()
    grad.start_near(0)
    grad.start_near(1)
    line.step(1, True)
    loads[1].wait()
    product(middle, weight, down_slabs, ffn.part, 1)
    for step in range(2, chips - 1):
        line.step(step, True)
    line.step(0, False)
    grad.relay(0)
    grad.relay(1)
    ffn.start_far()
    ffn.start_near(0)
    ffn.start_near(1)
    for step in range(1, chips - 1):
        line.step(step, False)
    for load in loads[2:]:
        load.wait()
    for half in (0, 1):
        grad.ready(half)

        def norm(index, carry):
            at = pl.multiple_of(index * TILE, TILE)
            here = pl.ds(pl.multiple_of(half * grad.half + at, TILE), TILE)
            back, gain_part = norm_backward(inputs[here, :].astype(f32), grad.tile(half, at), first_gain[...])
            input_grad[here, :] = grad_resid[here, :] + back
            dgain[...] += jnp.sum(gain_part, axis=0, keepdims=True)
            return carry

        lax.fori_loop(0, grad.half // TILE, norm, 0)
    model = dgain.shape[1]
    count = model // SMALL
    for row in range(count):
        lanes = slice(row * SMALL, (row + 1) * SMALL)
        small[0, row : row + 1, :] = dgain[:, lanes]
        small[0, count + row : count + row + 1, :] = ffn_dgain[:, lanes]
    small[0, 2 * count : 2 * count + 1, 0:HEAD] = head_dgain[...]
    small[0, 16 : 16 + 3 * TAPS, :] = dtaps[...]
    heads = beta_out.shape[0]
    for head in range(heads):
        for row in range(count):
            at = 32 + head * count + row
            small[0, at : at + 1, :] = beta_part[head : head + 1, row * SMALL : (row + 1) * SMALL]

    def hop(at):
        where = (dict(tensor=grad.across), dict(tensor=grad.along), dict(dp=sibling))[at]
        return remote(small.at[at], near.at[at], small_send.at[at], small_receive.at[at], **where)

    def hopped(at):
        hop(at).wait()
        if at < 2:
            small[at + 1, 0:16, :] = small[at, 0:16, :] + near[at, 0:16, :]
            small[at + 1, 16:, :] = small[at, 16:, :]
        else:
            small[3] = small[2] + near[2]

    def tell(other):
        to = lax.rem(chip + other, chips)
        return remote(
            small.at[3], lined.at[chip], small_send.at[2 + other], small_receive.at[2 + other], dp=to * 2 + core
        )

    def put_inner(here, total):
        width = query_out.shape[1]
        for kind, target in enumerate((query_out, key_out, value_out, gate_out)):
            target[here, :] = total[:, kind * width : (kind + 1) * width]

    def put_output(here, total):
        turned[here, :] = total

    puts = [put_inner, put_output]
    hop(0).start()
    ffn.relay(0)
    ffn.relay(1)
    hopped(0)
    hop(1).start()
    pieces = len(line.pieces)
    line.keep(puts, range(0, pieces - 3))
    hopped(1)
    hop(2).start()
    for half in (0, 1):
        ffn.ready(half)

        def finish_rows(index, carry):
            at = pl.multiple_of(index * TILE, TILE)
            here = pl.ds(pl.multiple_of(half * ffn.half + at, TILE), TILE)
            out[here, :] = ((resid[here, :] + ffn.tile(half, at)) * mask[here, :]).astype(bf16)
            return carry

        lax.fori_loop(0, ffn.half // TILE, finish_rows, 0)
    hopped(2)
    lined[chip] = small[3]
    for other in range(1, chips):
        tell(other).start()
    line.keep(puts, range(pieces - 3, pieces))
    output_out[...] = jnp.transpose(turned[...])
    for other in range(1, chips):
        tell(other).wait()
    total = lined[0]
    for other in range(1, chips):
        total = total + lined[other]
    for row in range(count):
        lanes = slice(row * SMALL, (row + 1) * SMALL)
        first_out[:, lanes] = total[row : row + 1, :]
        ffn_out[:, lanes] = total[count + row : count + row + 1, :]
    head_out[...] = total[2 * count : 2 * count + 1, 0:HEAD]
    summed = small.at[0]
    summed[...] = total
    mine = (chip * 2 + core) * slab
    lanes = pl.ds(pl.multiple_of(lax.rem(mine, SMALL), slab), slab)
    for head in range(heads):
        beta_out[head : head + 1, :] = summed[pl.ds(32 + head * count + mine // SMALL, 1), lanes]
    for kind in range(3):
        taps_out[kind] = total[16 + kind * TAPS : 16 + (kind + 1) * TAPS, :]
    grad.finish()
    ffn.finish()
    line.finish()


def last_scatter(
    inner_part, output_part, weight, inner, dpre, middle, inputs, grad_resid, resid, mask, gain, ffn_dgain, head_dgain, dtaps,
    dbeta, beta, beta_part
):
    chips = lax.axis_size("dp") // 2
    rows, model = inputs.shape
    slab, width = output_part.shape[1:]
    arrays = [inner_part, output_part]
    shape = jax.ShapeDtypeStruct
    return pl.pallas_call(
        functools.partial(last_kernel, chips),
        in_specs=anywhere(9) + in_vmem(8),
        out_specs=in_vmem(12),
        out_shape=[shape((slab, width), f32)] * 4
        + [
            shape((width // HEAD, slab), f32),
            shape((width, slab), f32),
            shape((rows, model), f32),
            shape((rows, model), bf16),
            shape((1, model), f32),
            shape((1, model), f32),
            shape((1, HEAD), f32),
            shape((3, TAPS, dtaps.shape[1]), f32),
        ],
        scratch_shapes=LineScatter.scratch(chips, arrays)
        + [pltpu.VMEM((4 * rows, model), bf16)]
        + plane_scatter_scratch(rows, model)
        + [pltpu.VMEM((4 * rows, model), bf16)]
        + plane_scatter_scratch(rows, model)
        + [
            pltpu.VMEM((slab, width), f32),
            pltpu.VMEM((4, 48, SMALL), f32),
            pltpu.VMEM((3, 48, SMALL), f32),
            pltpu.VMEM((chips, 48, SMALL), f32),
            pltpu.VMEM((1, model), f32),
            pltpu.SemaphoreType.DMA((2 + chips,)),
            pltpu.SemaphoreType.DMA((2 + chips,)),
            pltpu.VMEM((2, *inner.shape[1:]), bf16),
            pltpu.VMEM((2, *weight.shape[1:]), bf16),
            pltpu.SemaphoreType.DMA((2, 2)),
            pltpu.VMEM(dpre.shape, bf16),
            pltpu.VMEM(middle.shape, bf16),
            pltpu.VMEM((rows, model), bf16),
            pltpu.VMEM((rows, model), f32),
            pltpu.VMEM((rows, model), f32),
            pltpu.SemaphoreType.DMA((5,)),
        ],
        compiler_params=pltpu.CompilerParams(
            collective_id=4, has_side_effects=True, vmem_limit_bytes=LARGE_LIMIT
        ),
        cost_estimate=pl.CostEstimate(flops=1_000_000, bytes_accessed=1_000_000, transcendentals=0),
    )(inner_part, output_part, weight, inner, dpre, middle, inputs, grad_resid, resid, mask, gain, ffn_dgain, head_dgain, dtaps, dbeta, beta, beta_part)


def rms_norm(values, gain):
    return (
        values * lax.rsqrt(jnp.mean(values * values, axis=-1, keepdims=True) + norm_epsilon) * gain
    )


def gather(values, axis):
    return lax.all_gather(values, axis, axis=0, tiled=True)


def scatter(values, axis):
    return lax.psum_scatter(values, axis, scatter_dimension=0, tiled=True)


def plain_first_gather(
    w_query, w_key, w_value, w_gate_out, w_beta, w_output, inputs, cotangent, mask, gain, w_gate, w_up, w_down
):
    shards = lax.axis_size("dp")
    inner = jnp.concatenate([w_query, w_key, w_value, w_gate_out], axis=1).astype(bf16)
    output = w_output.T.astype(bf16)
    grad = (cotangent.astype(f32) * mask).astype(bf16)
    return (
        gather(inner, "dp").reshape(shards, *inner.shape),
        gather(output, "dp").reshape(shards, *output.shape),
        gather(w_beta, "dp").reshape(shards, *w_beta.shape),
        gather(rms_norm(inputs.astype(f32), gain[0]).astype(bf16), "tensor"),
        gather(grad, "tensor"),
        jnp.concatenate([w_gate, w_up], axis=1).astype(bf16),
        w_down.T.astype(bf16),
        grad,
    )


def plain_branch_and_norm(z, weight, inputs, gain):
    branch = mm_nt(z, weight.reshape(-1, z.shape[1])).astype(bf16)
    resid = inputs.astype(f32) + scatter(branch, "tensor").astype(f32)
    return resid, gather(rms_norm(resid, gain[0]).astype(bf16), "tensor")


def plain_resid_backward(grad_both, weight, z, out_weight, resid, grad_out, gain):
    part = mm_nt(grad_both, weight).astype(bf16)
    back, gain_part = norm_backward(resid, scatter(part, "tensor").astype(f32), gain)
    value = grad_out.astype(f32) + back
    full = gather(value.astype(bf16), "tensor")
    dgain = jnp.sum(gain_part, axis=0, keepdims=True)
    return value, dgain, mm(full, out_weight).astype(bf16), mm_tn(full, z).astype(bf16)


def plain_last_scatter(
    inner_part, output_part, weight, inner, dpre, middle, inputs, grad_resid, resid, mask, gain, ffn_dgain, head_dgain, dtaps,
    dbeta, beta, beta_part
):
    beta = beta.transpose(1, 0, 2).reshape(BETA_PAD, -1)
    grad_part = (mm_nt(dpre, inner.reshape(-1, inner.shape[2])) + mm(dbeta, beta)).astype(bf16)
    slab = inner_part.shape[1]
    beta_total = lax.psum(beta_part[: output_part.shape[2] // HEAD], "dp")
    beta_total = lax.dynamic_slice_in_dim(beta_total, lax.axis_index("dp") * slab, slab, axis=1)
    inner, output = (
        scatter(part.reshape(-1, part.shape[-1]), "dp").astype(f32) for part in (inner_part, output_part)
    )
    width = output.shape[1]
    back, gain_part = norm_backward(inputs.astype(f32), scatter(grad_part, "tensor").astype(f32), gain)
    ffn_part = mm_nt(middle, weight.reshape(-1, weight.shape[2])).astype(bf16)
    out = ((resid + scatter(ffn_part, "tensor").astype(f32)) * mask).astype(bf16)
    gains = (jnp.sum(gain_part, axis=0, keepdims=True), ffn_dgain, head_dgain)
    return (
        *(inner[:, kind * width : (kind + 1) * width] for kind in range(4)),
        beta_total,
        output.T,
        grad_resid + back,
        out,
        *lax.psum(gains, ("dp", "tensor")),
        lax.psum(dtaps, "dp").reshape(3, TAPS, -1),
    )


def body(
    inputs,
    cotangent,
    lengths,
    norm_gain,
    w_query,
    w_key,
    w_value,
    w_gate_out,
    w_beta,
    conv_weight,
    out_norm_gain,
    w_output,
    ffn_norm_gain,
    w_gate,
    w_up,
    w_down,
):
    tensor_count = lax.axis_size("tensor")
    shards = lax.axis_size("dp")
    kernels = tensor_count == 4 and shards == 8
    rows, model = inputs.shape
    length = rows * tensor_count
    width = w_query.shape[1]
    heads = width // HEAD
    hidden = w_gate.shape[1]
    slab = w_query.shape[0]
    taps = conv_weight.reshape(3 * TAPS, width)
    first_gain, head_gain = norm_gain.reshape(1, model), out_norm_gain.reshape(1, HEAD)
    ffn_gain = ffn_norm_gain.reshape(1, model)

    positions = lax.axis_index("tensor") * rows + jnp.arange(rows, dtype=jnp.int32)
    mask = (positions < lengths[0]).astype(f32)[:, None]
    beta_rows = jnp.pad(w_beta.T, ((0, BETA_PAD - w_beta.shape[1]), (0, 0))).astype(bf16)
    inner, full_output, full_beta, normed, grad_full, gate_up, down, grad_out = (
        first_gather if kernels else plain_first_gather
    )(w_query, w_key, w_value, w_gate_out, beta_rows, w_output, inputs, cotangent, mask, first_gain, w_gate, w_up, w_down)
    gate_up = gather(gate_up, "dp")
    down = gather(down, "dp")

    pre = jnp.dot(normed, inner.reshape(model, -1), preferred_element_type=f32).astype(bf16)
    beta_pre = mm_nt(normed, full_beta.transpose(1, 0, 2).reshape(BETA_PAD, model))
    z, conv, mixed, inverse, states = mixer_forward(pre, beta_pre, taps, head_gain, heads)
    resid, normed2 = (branch_and_norm if kernels else plain_branch_and_norm)(z, full_output, inputs, ffn_gain)
    middle, slopes = (ffn if kernels else plain_ffn)(normed2, gate_up)
    down_part = mm_tn(grad_full, middle).astype(bf16)
    down, down_part = lax.optimization_barrier((down, down_part))
    down_total = scatter(down_part, "dp")
    grad_both = (ffn_backward if kernels else plain_ffn_backward)(grad_full, down, slopes)
    grad_both, both_part = lax.optimization_barrier((grad_both, mm_tn(normed2, grad_both).astype(bf16)))
    both_total = scatter(both_part, "dp")
    grad_resid, ffn_dgain, dz, output_grad = (resid_backward if kernels else plain_resid_backward)(
        grad_both, gate_up, z, full_output.reshape(model, width), resid, grad_out, ffn_gain
    )
    dpre, dbeta, beta_part, dtaps, head_dgain = mixer_backward(
        pre, beta_pre, normed, conv, mixed, dz, inverse, states, taps, head_gain, heads
    )
    output_grad = output_grad.reshape(shards, slab, width)
    inner_grad = mm_tn(normed, dpre).astype(bf16).reshape(shards, slab, -1)
    results = (last_scatter if kernels else plain_last_scatter)(
        inner_grad,
        output_grad,
        down.reshape(shards, slab, hidden),
        inner,
        dpre,
        middle,
        inputs,
        grad_resid,
        resid,
        mask,
        first_gain,
        ffn_dgain,
        head_dgain,
        dtaps,
        dbeta,
        full_beta,
        beta_part,
    )
    gate_total, up_total, down_total, *results = (finish if kernels else plain_finish)(
        both_total, down_total, results
    )
    query_total, key_total, value_total, gate_out_total, beta_total, output_total, input_grad, output = results[:8]
    first_total, ffn_total, head_total, taps_total = results[8:]
    return (
        output,
        input_grad,
        first_total[0],
        query_total,
        key_total,
        value_total,
        gate_out_total,
        beta_total.T,
        taps_total,
        head_total[0],
        output_total,
        ffn_total[0],
        gate_total,
        up_total,
        down_total,
    )


def solution(mesh):
    rows = P(("dp", "tensor"), None)
    split = P("dp", "tensor")
    turned = P("tensor", "dp")
    taps = P(None, None, "tensor")
    return jax.shard_map(
        body,
        mesh=mesh,
        in_specs=(rows, rows, P("dp"), P(), split, split, split, split, split, taps, P(), turned, P(), split, split, turned),
        out_specs=(rows, rows, P(), split, split, split, split, split, taps, P(), turned, P(), split, split, turned),
        check_vma=False,
    )
```

```python
import functools
import jax
import jax.numpy as jnp
from jax import lax
from jax.experimental import pallas as pl
from jax.experimental.pallas import tpu as pltpu
from jax.sharding import PartitionSpec as P

norm_epsilon = 1e-06
head_epsilon = 1e-05
HEAD = 128
CHUNK = 128
STEP = 256
TAPS = 4
BETA_PAD = 16
VMEM_LIMIT = 56 * 1024 * 1024
f32 = jnp.float32
bf16 = jnp.bfloat16


def mm(a, b):
    return lax.dot_general(a, b, (((1,), (0,)), ((), ())), preferred_element_type=f32)


def mm_nt(a, b):
    return lax.dot_general(a, b, (((1,), (1,)), ((), ())), preferred_element_type=f32)


def mm_tn(a, b):
    return lax.dot_general(a, b, (((0,), (0,)), ((), ())), preferred_element_type=f32)


def chunk_indices():
    row = lax.broadcasted_iota(jnp.int32, (CHUNK, CHUNK), 0)
    col = lax.broadcasted_iota(jnp.int32, (CHUNK, CHUNK), 1)
    return row, col


def unit_lower_inverses(stricts, row, col):
    apart = row ^ col
    inverses = [jnp.where(row == col, 1.0, jnp.where(apart == 1, -strict, 0.0)) for strict in stricts]
    span = 2
    while span < CHUNK:
        here = (apart >= span) & (apart < 2 * span)
        lows = [inverse.astype(bf16) for inverse in inverses]
        firsts = [mm(low, jnp.where(here, strict, 0.0).astype(bf16)).astype(bf16) for low, strict in zip(lows, stricts)]
        inverses = [inverse - mm(first, low) for inverse, first, low in zip(inverses, firsts, lows)]
        span *= 2
    return [inverse.astype(bf16) for inverse in inverses]


def silu_parts(conv):
    sig = jax.nn.sigmoid(conv)
    return conv * sig, sig


def forward_kernel(
    heads, pre_ref, beta_ref, taps_ref, gain_ref, z_ref, conv_ref, mixed_ref, inv_ref, state_ref, hist, state
):
    step = pl.program_id(0)
    width = heads * HEAD
    rows = pre_ref.shape[0]

    @pl.when(step == 0)
    def _():
        hist[0:8, :] = jnp.zeros((8, 3 * width), f32)
        state[...] = jnp.zeros_like(state)

    @pl.when(step > 0)
    def _():
        hist[0:8, :] = hist[rows : rows + 8, :]

    hist[8 : 8 + rows, :] = pre_ref[:, 0 : 3 * width].astype(f32)
    row, col = chunk_indices()
    beta_all = jax.nn.sigmoid(beta_ref[...])
    work = []
    for head in range(heads):
        parts = []
        for kind in range(3):
            lanes = slice(kind * width + head * HEAD, kind * width + (head + 1) * HEAD)
            total = taps_ref[kind * TAPS : kind * TAPS + 1, head * HEAD : (head + 1) * HEAD] * hist[5 : 5 + rows, lanes]
            for tap in range(1, TAPS):
                total = total + taps_ref[
                    kind * TAPS + tap : kind * TAPS + tap + 1, head * HEAD : (head + 1) * HEAD
                ] * hist[5 + tap : 5 + tap + rows, lanes]
            conv_ref[:, lanes] = total
            act, _ = silu_parts(total)
            if kind < 2:
                act = act * lax.rsqrt(jnp.sum(act * act, axis=-1, keepdims=True) + norm_epsilon)
            if kind == 0:
                act = act * HEAD ** (-0.5)
            parts.append(act)
        beta = beta_all[:, head : head + 1]
        for part in range(rows // CHUNK):
            here = slice(part * CHUNK, (part + 1) * CHUNK)
            query, key, value = (p[here] for p in parts)
            query_low, key_low = query.astype(bf16), key.astype(bf16)
            b = beta[here]
            stacked = jnp.concatenate([(b * key).astype(bf16), (b * value).astype(bf16)], axis=1)
            strict = jnp.where(row > col, b * mm_nt(key_low, key_low), 0.0)
            scores = jnp.where(row >= col, mm_nt(query_low, key_low), 0.0).astype(bf16)
            work.append((head, part, query_low, key_low, stacked, scores, strict))
    inverses = unit_lower_inverses([item[-1] for item in work], row, col)
    solved_all = {}
    for (head, part, query_low, key_low, stacked, scores, _), inverse in zip(work, inverses):
        inv_ref[head, part] = inverse
        solved_all[part, head] = (query_low, key_low, scores, mm(inverse, stacked))
    states = [state[head] for head in range(heads)]
    for part in range(rows // CHUNK):
        here = slice(part * CHUNK, (part + 1) * CHUNK)
        enters = [enter.astype(bf16) for enter in states]
        items = [solved_all[part, head] for head in range(heads)]
        freshes = [
            (solved[:, HEAD:] - mm(solved[:, :HEAD].astype(bf16), enter)).astype(bf16)
            for (_, _, _, solved), enter in zip(items, enters)
        ]
        states = [old + mm_tn(key_low, fresh) for old, (_, key_low, _, _), fresh in zip(states, items, freshes)]
        for head in range(heads):
            lanes = slice(head * HEAD, (head + 1) * HEAD)
            query_low, _, scores, _ = items[head]
            state_ref[head, part] = enters[head]
            mixed = mm(query_low, enters[head]) + mm(scores, freshes[head])
            mixed_ref[here, lanes] = mixed
            gate = pre_ref[here, 3 * width + head * HEAD : 3 * width + (head + 1) * HEAD].astype(f32)
            gate_act, _ = silu_parts(gate)
            normed = mixed * lax.rsqrt(jnp.mean(mixed * mixed, axis=-1, keepdims=True) + head_epsilon)
            z_ref[here, lanes] = (normed * gain_ref[...] * gate_act).astype(bf16)
    for head in range(heads):
        state[head] = states[head]


def mixer_forward(pre, beta, taps, gain, heads):
    length, total = pre.shape
    width = heads * HEAD
    steps, parts = length // STEP, STEP // CHUNK
    return pl.pallas_call(
        functools.partial(forward_kernel, heads),
        grid=(steps,),
        in_specs=[
            pl.BlockSpec((STEP, total), lambda i: (i, 0)),
            pl.BlockSpec((STEP, BETA_PAD), lambda i: (i, 0)),
            pl.BlockSpec((3 * TAPS, width), lambda i: (0, 0)),
            pl.BlockSpec((1, HEAD), lambda i: (0, 0)),
        ],
        out_specs=[
            pl.BlockSpec((STEP, width), lambda i: (i, 0)),
            pl.BlockSpec((STEP, 3 * width), lambda i: (i, 0)),
            pl.BlockSpec((STEP, width), lambda i: (i, 0)),
            pl.BlockSpec((heads, parts, CHUNK, CHUNK), lambda i: (0, i, 0, 0)),
            pl.BlockSpec((heads, parts, HEAD, HEAD), lambda i: (0, i, 0, 0)),
        ],
        out_shape=[
            jax.ShapeDtypeStruct((length, width), bf16),
            jax.ShapeDtypeStruct((length, 3 * width), f32),
            jax.ShapeDtypeStruct((length, width), f32),
            jax.ShapeDtypeStruct((heads, steps * parts, CHUNK, CHUNK), bf16),
            jax.ShapeDtypeStruct((heads, steps * parts, HEAD, HEAD), bf16),
        ],
        scratch_shapes=[
            pltpu.VMEM((STEP + 8, 3 * width), f32),
            pltpu.VMEM((heads, HEAD, HEAD), f32),
        ],
        compiler_params=pltpu.CompilerParams(
            dimension_semantics=("arbitrary",), vmem_limit_bytes=VMEM_LIMIT
        ),
        cost_estimate=pl.CostEstimate(
            flops=2 * length * width * HEAD * 60, bytes_accessed=length * (total * 4 + width * 24), transcendentals=length * width * 8
        ),
    )(pre, beta, taps, gain)


def backward_kernel(
    heads,
    pre_ref,
    beta_ref,
    source_ref,
    conv_ref,
    mixed_ref,
    dz_ref,
    inv_ref,
    state_ref,
    taps_ref,
    gain_ref,
    dpre_ref,
    dbeta_ref,
    dsource_ref,
    dtaps_ref,
    dgain_ref,
    later,
    dstate,
):
    step = pl.program_id(0)
    width = heads * HEAD
    rows = pre_ref.shape[0]
    count = rows // CHUNK

    @pl.when(step == 0)
    def _():
        later[rows : rows + 8, :] = jnp.zeros((8, 3 * width), f32)
        dstate[...] = jnp.zeros_like(dstate)
        dtaps_ref[...] = jnp.zeros_like(dtaps_ref)
        dgain_ref[...] = jnp.zeros_like(dgain_ref)
        dsource_ref[...] = jnp.zeros_like(dsource_ref)

    @pl.when(step > 0)
    def _():
        later[rows : rows + 8, :] = later[0:8, :]

    row, col = chunk_indices()
    beta_all = jax.nn.sigmoid(beta_ref[...])
    beta_lane = lax.broadcasted_iota(jnp.int32, (CHUNK, BETA_PAD), 1)
    dbeta_all = [jnp.zeros((CHUNK, BETA_PAD), f32) for _ in range(count)]
    dgain = jnp.zeros((1, HEAD), f32)
    gain = gain_ref[...]
    every = [(part, head) for part in reversed(range(count)) for head in range(heads)]

    def of(ref, kind, at):
        part, head = at
        lanes = slice(kind * width + head * HEAD, kind * width + (head + 1) * HEAD)
        return ref[part * CHUNK : (part + 1) * CHUNK, lanes].astype(f32)

    betas = {(part, head): beta_all[part * CHUNK : (part + 1) * CHUNK, head : head + 1] for part, head in every}
    unit_queries, keys, query_lows, key_lows, scales, stacks = {}, {}, {}, {}, {}, {}
    for at in every:
        acts = [silu_parts(of(conv_ref, kind, at))[0] for kind in range(3)]
        scales[at] = [lax.rsqrt(jnp.sum(act * act, axis=-1, keepdims=True) + norm_epsilon) for act in acts[:2]]
        unit_queries[at], keys[at] = acts[0] * scales[at][0], acts[1] * scales[at][1]
        query_lows[at] = (unit_queries[at] * HEAD ** (-0.5)).astype(bf16)
        key_lows[at] = keys[at].astype(bf16)
        stacks[at] = jnp.concatenate([(betas[at] * keys[at]).astype(bf16), (betas[at] * acts[2]).astype(bf16)], axis=1)
    solved = {at: mm(inv_ref[at[1], at[0]], stacks[at]) for at in every}
    scores = {at: jnp.where(row >= col, mm_nt(query_lows[at], key_lows[at]), 0.0).astype(bf16) for at in every}
    weights = {at: solved[at][:, :HEAD].astype(bf16) for at in every}
    outs = {}
    for at in every:
        part, head = at
        here = slice(part * CHUNK, (part + 1) * CHUNK)
        gate = of(pre_ref, 3, at)
        gate_act, gate_sig = silu_parts(gate)
        mixed, dz = of(mixed_ref, 0, at), of(dz_ref, 0, at)
        root = lax.rsqrt(jnp.mean(mixed * mixed, axis=-1, keepdims=True) + head_epsilon)
        normed = mixed * root
        dgate = dz * normed * gain * (gate_sig * (1.0 + gate * (1.0 - gate_sig)))
        dpre_ref[here, 3 * width + head * HEAD : 3 * width + (head + 1) * HEAD] = dgate.astype(bf16)
        dgained = dz * gate_act
        dgain = dgain + jnp.sum(dgained * normed, axis=0, keepdims=True)
        dnormed = dgained * gain
        dmixed = root * (dnormed - normed * jnp.mean(dnormed * normed, axis=-1, keepdims=True))
        outs[at] = dmixed.astype(bf16)
    enters = {(part, head): state_ref[head, part] for part, head in every}
    fresh = {at: (solved[at][:, HEAD:] - mm(weights[at], enters[at])).astype(bf16) for at in every}
    within = {at: mm_tn(scores[at], outs[at]) for at in every}
    across = {at: mm_tn(query_lows[at], outs[at]) for at in every}
    leavings, dfresh = {}, {}
    states = [dstate[head] for head in range(heads)]
    for part in reversed(range(count)):
        for head in range(heads):
            leavings[part, head] = states[head].astype(bf16)
        for head in range(heads):
            at = (part, head)
            dfresh[at] = (within[at] + mm(key_lows[at], leavings[at])).astype(bf16)
        for head in range(heads):
            at = (part, head)
            states[head] = states[head] + across[at] - mm_tn(weights[at], dfresh[at])
    for head in range(heads):
        dstate[head] = states[head]
    dscores = {at: jnp.where(row >= col, mm_nt(outs[at], fresh[at]), 0.0).astype(bf16) for at in every}
    dweights = {at: (-mm_nt(dfresh[at], enters[at])).astype(bf16) for at in every}
    dxys = {
        at: mm_tn(inv_ref[at[1], at[0]], jnp.concatenate([dweights[at], dfresh[at]], axis=1)) for at in every
    }
    dqueries = {at: mm_nt(outs[at], enters[at]) + mm(dscores[at], key_lows[at]) for at in every}
    dkeys = {at: mm_tn(dscores[at], query_lows[at]) + mm_nt(fresh[at], leavings[at]) for at in every}
    dsystems = {
        at: jnp.where(row > col, -mm_nt(dxys[at].astype(bf16), solved[at].astype(bf16)), 0.0) for at in every
    }
    dsystem_lows = {at: dsystems[at].astype(bf16) for at in every}
    firsts = {at: mm(dsystem_lows[at], key_lows[at]) for at in every}
    seconds = {at: mm_tn(dsystem_lows[at], stacks[at][:, :HEAD]) for at in every}
    grams = {at: mm_nt(key_lows[at], key_lows[at]) for at in every}
    for at in every:
        part, head = at
        beta, dx, dy, key = betas[at], dxys[at][:, :HEAD], dxys[at][:, HEAD:], keys[at]
        dkey = dkeys[at] + beta * (firsts[at] + dx) + seconds[at]
        convs = [of(conv_ref, kind, at) for kind in range(3)]
        sigs = [jax.nn.sigmoid(conv) for conv in convs]
        dbeta = jnp.sum(dsystems[at] * grams[at] + dx * key + dy * (convs[2] * sigs[2]), axis=-1, keepdims=True)
        dbeta = dbeta * beta * (1.0 - beta)
        dbeta_all[part] = jnp.where(beta_lane == head, dbeta, dbeta_all[part])
        unit_query, dquery = unit_queries[at], dqueries[at] * HEAD ** (-0.5)
        dquery = scales[at][0] * (dquery - unit_query * jnp.sum(unit_query * dquery, axis=-1, keepdims=True))
        dkey = scales[at][1] * (dkey - key * jnp.sum(key * dkey, axis=-1, keepdims=True))
        for kind, grad in enumerate((dquery, dkey, beta * dy)):
            dconv = grad * (sigs[kind] * (1.0 + convs[kind] * (1.0 - sigs[kind])))
            lanes = slice(kind * width + head * HEAD, kind * width + (head + 1) * HEAD)
            later[part * CHUNK : (part + 1) * CHUNK, lanes] = dconv
    for part in range(count):
        here = slice(part * CHUNK, (part + 1) * CHUNK)
        dbeta_low = dbeta_all[part].astype(bf16)
        dbeta_ref[here, :] = dbeta_low
        dsource_ref[...] += mm_tn(dbeta_low, source_ref[here, :])
    dgain_ref[...] += dgain
    for kind in range(3):
        for head in range(heads):
            lanes = slice(kind * width + head * HEAD, kind * width + (head + 1) * HEAD)
            source = pre_ref[:, lanes].astype(f32)
            total = jnp.zeros((rows, HEAD), f32)
            for tap in range(TAPS):
                at = kind * TAPS + tap
                shifted = later[TAPS - 1 - tap : TAPS - 1 - tap + rows, lanes]
                total = total + taps_ref[at : at + 1, head * HEAD : (head + 1) * HEAD] * shifted
                dtaps_ref[at : at + 1, head * HEAD : (head + 1) * HEAD] += jnp.sum(
                    source * shifted, axis=0, keepdims=True
                )
            dpre_ref[:, lanes] = total.astype(bf16)


def mixer_backward(pre, beta, source, conv, mixed, dz, inverse, states, taps, gain, heads):
    length, total = pre.shape
    model = source.shape[1]
    width = heads * HEAD
    steps, parts = length // STEP, STEP // CHUNK
    return pl.pallas_call(
        functools.partial(backward_kernel, heads),
        grid=(steps,),
        in_specs=[
            pl.BlockSpec((STEP, total), lambda i: (steps - 1 - i, 0)),
            pl.BlockSpec((STEP, BETA_PAD), lambda i: (steps - 1 - i, 0)),
            pl.BlockSpec((STEP, model), lambda i: (steps - 1 - i, 0)),
            pl.BlockSpec((STEP, 3 * width), lambda i: (steps - 1 - i, 0)),
            pl.BlockSpec((STEP, width), lambda i: (steps - 1 - i, 0)),
            pl.BlockSpec((STEP, width), lambda i: (steps - 1 - i, 0)),
            pl.BlockSpec((heads, parts, CHUNK, CHUNK), lambda i: (0, steps - 1 - i, 0, 0)),
            pl.BlockSpec((heads, parts, HEAD, HEAD), lambda i: (0, steps - 1 - i, 0, 0)),
            pl.BlockSpec((3 * TAPS, width), lambda i: (0, 0)),
            pl.BlockSpec((1, HEAD), lambda i: (0, 0)),
        ],
        out_specs=[
            pl.BlockSpec((STEP, total), lambda i: (steps - 1 - i, 0)),
            pl.BlockSpec((STEP, BETA_PAD), lambda i: (steps - 1 - i, 0)),
            pl.BlockSpec((BETA_PAD, model), lambda i: (0, 0)),
            pl.BlockSpec((3 * TAPS, width), lambda i: (0, 0)),
            pl.BlockSpec((1, HEAD), lambda i: (0, 0)),
        ],
        out_shape=[
            jax.ShapeDtypeStruct((length, total), bf16),
            jax.ShapeDtypeStruct((length, BETA_PAD), bf16),
            jax.ShapeDtypeStruct((BETA_PAD, model), f32),
            jax.ShapeDtypeStruct((3 * TAPS, width), f32),
            jax.ShapeDtypeStruct((1, HEAD), f32),
        ],
        scratch_shapes=[
            pltpu.VMEM((STEP + 8, 3 * width), f32),
            pltpu.VMEM((heads, HEAD, HEAD), f32),
        ],
        compiler_params=pltpu.CompilerParams(
            dimension_semantics=("arbitrary",), vmem_limit_bytes=VMEM_LIMIT
        ),
        cost_estimate=pl.CostEstimate(
            flops=1_000_000, bytes_accessed=1_000_000, transcendentals=0
        ),
    )(pre, beta, source, conv, mixed, dz, inverse, states, taps, gain)


MESH = pl.DeviceIdType.MESH
TILE = 16
BOTH_LAST = 512
LANES = 128
LARGE_LIMIT = 60 * 1024 * 1024


def remote(source, target, send, receive, **where):
    return pltpu.make_async_remote_copy(
        src_ref=source,
        dst_ref=target,
        send_sem=send,
        recv_sem=receive,
        device_id=where,
        device_id_type=MESH,
    )


def when(condition, action):
    pl.when(condition)(action)


def greet(**where):
    pl.semaphore_signal(
        pltpu.get_barrier_semaphore(), inc=1, device_id=where, device_id_type=MESH
    )


def wait_greetings(count):
    pl.semaphore_wait(pltpu.get_barrier_semaphore(), count)


def plane():
    me = lax.axis_index("tensor")
    across = me + 1 - 2 * lax.rem(me, 2)
    along = lax.rem(me + 2, 4)
    return me, across, along


def chip_and_core():
    index = lax.axis_index("dp")
    return index // 2, lax.rem(index, 2)


def greet_line(chips):
    chip, core = chip_and_core()
    greet(dp=chip * 2 + 1 - core)
    when(chip > 0, lambda: greet(dp=(chip - 1) * 2 + core))
    when(chip < chips - 1, lambda: greet(dp=(chip + 1) * 2 + core))
    return 1 + jnp.where(chip > 0, 1, 0) + jnp.where(chip < chips - 1, 1, 0)


class PlaneGather:
    def __init__(self, own, full, send, receive):
        self.own, self.full, self.send, self.receive = own, full, send, receive
        self.me, self.across, self.along = plane()
        self.far = lax.rem(self.across + 2, 4)
        self.rows = own.shape[0]
        self.half = self.rows // 2

    def slot(self, block, half):
        start = pl.multiple_of(block * self.rows + half * self.half, self.half)
        return self.full.at[pl.ds(start, self.half)]

    def mine(self, half):
        return self.own.at[pl.ds(half * self.half, self.half)]

    def out(self, half, kind):
        where = self.across if kind == 0 else self.along
        at = 2 * kind + half
        return remote(
            self.mine(half), self.slot(self.me, half), self.send.at[at], self.receive.at[at], tensor=where
        )

    def arriving(self, half, kind):
        block = self.across if kind == 0 else self.along
        at = 2 * kind + half
        view = self.slot(block, half)
        return remote(view, view, self.send.at[at], self.receive.at[at], tensor=block)

    def passing(self, kind):
        view = self.slot(self.across if kind == 0 else self.along, kind)
        where = self.along if kind == 0 else self.across
        return remote(view, view, self.send.at[4 + kind], self.receive.at[4 + kind], tensor=where)

    def passed(self, kind):
        view = self.slot(self.far, kind)
        where = self.along if kind == 0 else self.across
        return remote(view, view, self.send.at[4 + kind], self.receive.at[4 + kind], tensor=where)

    def start(self, half):
        for kind in (half, 1 - half):
            self.out(half, kind).start()

    def relay(self, kind):
        self.arriving(kind, kind).wait_recv()
        self.passing(kind).start()

    def near(self, kind):
        self.arriving(1 - kind, kind).wait_recv()

    def diagonal(self):
        self.passed(0).wait_recv()
        self.passed(1).wait_recv()

    def finish(self):
        self.near(0)
        self.near(1)
        self.diagonal()
        self.sent()

    def sent(self):
        for kind in (0, 1):
            self.passing(kind).wait_send()
            for half in (0, 1):
                self.out(half, kind).wait_send()


class PlaneScatter:
    def __init__(self, part, first, second, stage, send, receive):
        self.part, self.first, self.second, self.stage = part, first, second, stage
        self.send, self.receive = send, receive
        self.me, self.across, self.along = plane()
        self.far = lax.rem(self.across + 2, 4)
        self.rows = part.shape[0] // 4
        self.half = self.rows // 2

    def start_of(self, block, half):
        return pl.multiple_of(block * self.rows + half * self.half, self.half)

    def view(self, block, half):
        return self.part.at[pl.ds(self.start_of(block, half), self.half)]

    def out(self, kind, order):
        where = self.across if kind == 0 else self.along
        at = 2 * kind + order
        return remote(
            self.view(self.far if order == 0 else where, kind),
            self.first.at[at],
            self.send.at[at],
            self.receive.at[at],
            tensor=where,
        )

    def over(self, kind):
        where = self.along if kind == 0 else self.across
        return remote(
            self.stage.at[kind], self.second.at[kind], self.send.at[4 + kind], self.receive.at[4 + kind], tensor=where
        )

    def start_far(self):
        for kind in (0, 1):
            self.out(kind, 0).start()

    def start_near(self, kind):
        self.out(kind, 1).start()

    def relay(self, kind):
        self.out(kind, 0).wait_recv()
        block = self.along if kind == 0 else self.across
        start = self.start_of(block, kind)

        def add(index, carry):
            at = pl.multiple_of(index * TILE, TILE)
            mine = self.part[pl.ds(pl.multiple_of(start + at, TILE), TILE), :].astype(f32)
            other = self.first[2 * kind, pl.ds(at, TILE), :].astype(f32)
            self.stage[kind, pl.ds(at, TILE), :] = (mine + other).astype(bf16)
            return carry

        lax.fori_loop(0, self.half // TILE, add, 0)
        self.over(kind).start()

    def ready(self, kind):
        self.out(kind, 1).wait_recv()
        self.over(kind).wait_recv()

    def tile(self, kind, at):
        start = self.start_of(self.me, kind)
        mine = self.part[pl.ds(pl.multiple_of(start + at, TILE), TILE), :].astype(f32)
        near = self.first[2 * kind + 1, pl.ds(at, TILE), :].astype(f32)
        return mine + near + self.second[kind, pl.ds(at, TILE), :].astype(f32)

    def finish(self):
        for kind in (0, 1):
            for order in (0, 1):
                self.out(kind, order).wait_send()
            self.over(kind).wait_send()


def plane_scatter_scratch(rows, columns):
    half = rows // 2
    return [
        pltpu.VMEM((4, half, columns), bf16),
        pltpu.VMEM((2, half, columns), bf16),
        pltpu.VMEM((2, half, columns), bf16),
        pltpu.SemaphoreType.DMA((6,)),
        pltpu.SemaphoreType.DMA((6,)),
    ]


def pieces_of(arrays, size):
    found = []
    for index, array in enumerate(arrays):
        rows, columns = array.shape[-2:]
        count = max(1, min(rows // 64, round(rows * columns / size)))
        while rows % count or (rows // count) % 16:
            count -= 1
        for piece in range(count):
            found.append((index, piece * (rows // count), rows // count))
    return found


PIECE = 64 * 2176


class LineGather:
    def __init__(self, chips, owns, fulls, sems):
        self.chips, self.owns, self.fulls = chips, owns, fulls
        self.pieces = pieces_of(owns, PIECE)
        self.right_send, self.right_receive, self.left_send, self.left_receive = sems[:4]
        self.core_send, self.core_receive, self.local = sems[4:]
        self.chip, self.core = chip_and_core()

    @staticmethod
    def scratch(chips, pieces, arrays):
        return [pltpu.SemaphoreType.DMA((chips, pieces)) for _ in range(6)] + [pltpu.SemaphoreType.DMA((arrays,))]

    def slot(self, piece, chip, core):
        index, start, rows = self.pieces[piece]
        return self.fulls[index].at[chip * 2 + core, pl.ds(start, rows)]

    def source(self, piece, away):
        index, start, rows = self.pieces[piece]
        return self.owns[index].at[pl.ds(start, rows)]

    def right(self, piece, away, chip):
        slot = self.slot(piece, chip, self.core)
        source = self.source(piece, 0) if away == 0 else slot
        to = (self.chip + 1) * 2 + self.core
        return remote(source, slot, self.right_send.at[away, piece], self.right_receive.at[away, piece], dp=to)

    def left(self, piece, away, chip):
        slot = self.slot(piece, chip, self.core)
        source = self.source(piece, 0) if away == 0 else slot
        to = (self.chip - 1) * 2 + self.core
        return remote(source, slot, self.left_send.at[away, piece], self.left_receive.at[away, piece], dp=to)

    def trade(self, piece, chip, own):
        slot = self.slot(piece, chip, self.core)
        source = self.source(piece, 0) if own else slot
        to = self.chip * 2 + 1 - self.core
        return remote(source, slot, self.core_send.at[chip, piece], self.core_receive.at[chip, piece], dp=to)

    def keep(self, index):
        return pltpu.make_async_copy(
            self.owns[index], self.fulls[index].at[self.chip * 2 + self.core], self.local.at[index]
        )

    def start(self):
        for piece in range(len(self.pieces)):
            when(self.chip < self.chips - 1, lambda: self.right(piece, 0, self.chip).start())
            when(self.chip > 0, lambda: self.left(piece, 0, self.chip).start())
        for piece in range(len(self.pieces)):
            self.trade(piece, self.chip, True).start()
        for index in range(len(self.owns)):
            self.keep(index).start()

    def step(self, away):
        for piece in range(len(self.pieces)):

            def from_left():
                chip = self.chip - away
                self.right(piece, away - 1, chip).wait_recv()
                if away < self.chips - 1:
                    when(self.chip < self.chips - 1, lambda: self.right(piece, away, chip).start())
                self.trade(piece, chip, False).start()

            def from_right():
                chip = self.chip + away
                self.left(piece, away - 1, chip).wait_recv()
                if away < self.chips - 1:
                    when(self.chip > 0, lambda: self.left(piece, away, chip).start())
                self.trade(piece, chip, False).start()

            when(self.chip >= away, from_left)
            when(self.chip + away < self.chips, from_right)

    def finish(self):
        for index in range(len(self.owns)):
            self.keep(index).wait()
        for piece in range(len(self.pieces)):
            for away in range(self.chips - 1):
                when(
                    (self.chip < self.chips - 1) & (self.chip >= away),
                    lambda: self.right(piece, away, self.chip - away).wait_send(),
                )
                when(
                    (self.chip > 0) & (self.chip + away < self.chips),
                    lambda: self.left(piece, away, self.chip + away).wait_send(),
                )
            for chip in range(self.chips):
                trade = remote(
                    self.slot(piece, chip, self.core),
                    self.slot(piece, chip, 1 - self.core),
                    self.core_send.at[chip, piece],
                    self.core_receive.at[chip, piece],
                    dp=self.chip * 2 + 1 - self.core,
                )
                trade.wait_send()
                trade.wait_recv()


def first_gather_kernel(chips, *refs):
    w_query, w_key, w_value, w_gate_out, w_beta, w_output, inputs, cotangent, mask, gain = refs[:10]
    w_gate, w_up, w_down = refs[10:13]
    inner_full, output_full, beta_full, normed_full, grad_full, gate_up, down, grad = refs[13:21]
    inner, output, normed, gate_wide, up_wide, down_wide = refs[21:27]
    sems = refs[27:]
    width, hidden = w_query.shape[1], w_gate.shape[1]
    line = LineGather(chips, [inner, output, w_beta], [inner_full, output_full, beta_full], sems[:7])
    rows = [PlaneGather(normed, normed_full, *sems[7:9]), PlaneGather(grad, grad_full, *sems[9:11])]
    local = sems[11]
    keeps = [
        pltpu.make_async_copy(
            own, full.at[pl.ds(pl.multiple_of(each.me * each.rows, each.rows), each.rows)], local.at[at]
        )
        for at, (own, full, each) in enumerate(((normed, normed_full, rows[0]), (grad, grad_full, rows[1])))
    ]
    loads = [
        pltpu.make_async_copy(source, target, local.at[2 + at])
        for at, (source, target) in enumerate(((w_gate, gate_wide), (w_up, up_wide), (w_down, down_wide)))
    ]
    greetings = greet_line(chips)
    greet(tensor=rows[0].across)
    greet(tensor=rows[0].along)
    for kind, weight in enumerate((w_query, w_key, w_value, w_gate_out)):
        inner[:, kind * width : (kind + 1) * width] = weight[...].astype(bf16)
    output[...] = jnp.transpose(w_output[...]).astype(bf16)
    wait_greetings(2 + greetings)
    line.start()
    for load in loads:
        load.start()

    def norm(index, carry):
        here = pl.ds(pl.multiple_of(index * TILE, TILE), TILE)
        value = inputs[here, :].astype(f32)
        scale = lax.rsqrt(jnp.mean(value * value, axis=-1, keepdims=True) + norm_epsilon)
        normed[here, :] = (value * scale * gain[...]).astype(bf16)
        grad[here, :] = (cotangent[here, :].astype(f32) * mask[here, :]).astype(bf16)
        return carry

    lax.fori_loop(0, inputs.shape[0] // TILE, norm, 0)
    for each in rows:
        each.start(0)
        each.start(1)
    for keep in keeps:
        keep.start()
    for load in loads:
        load.wait()
    for kind, wide in enumerate((gate_wide, up_wide)):
        for tile in range(hidden // LANES):
            to = (2 * tile + kind) * LANES
            gate_up[:, to : to + LANES] = wide[:, tile * LANES : (tile + 1) * LANES].astype(bf16)
    down[...] = jnp.transpose(down_wide[...]).astype(bf16)
    rows[0].relay(0)
    rows[0].relay(1)
    line.step(1)
    rows[1].relay(0)
    rows[1].relay(1)
    for away in range(2, chips):
        line.step(away)
    for each in rows:
        each.finish()
    for keep in keeps:
        keep.wait()
    line.finish()


def ffn_kernel(normed, weight, middle, slopes):
    def block(index, carry):
        here = pl.ds(pl.multiple_of(index * 512, 512), 512)
        both = mm(normed[here, :], weight[...])
        gate, up_part = both[:, :LANES], both[:, LANES:]
        act, sig = silu_parts(gate)
        middle[here, :] = (act * up_part).astype(bf16)
        slopes[here, :LANES] = (up_part * sig * (1.0 + gate * (1.0 - sig))).astype(bf16)
        slopes[here, LANES:] = act.astype(bf16)
        return carry

    lax.fori_loop(0, normed.shape[0] // 512, block, 0, unroll=True)


def ffn(normed, gate_up):
    length, model = normed.shape
    hidden = gate_up.shape[1] // 2
    return pl.pallas_call(
        ffn_kernel,
        grid=(hidden // LANES,),
        in_specs=[
            pl.BlockSpec((length, model), lambda i: (0, 0)),
            pl.BlockSpec((model, 2 * LANES), lambda i: (0, i)),
        ],
        out_specs=[
            pl.BlockSpec((length, LANES), lambda i: (0, i)),
            pl.BlockSpec((length, 2 * LANES), lambda i: (0, i)),
        ],
        out_shape=[
            jax.ShapeDtypeStruct((length, hidden), bf16),
            jax.ShapeDtypeStruct((length, 2 * hidden), bf16),
        ],
        compiler_params=pltpu.CompilerParams(
            dimension_semantics=("arbitrary",), vmem_limit_bytes=VMEM_LIMIT
        ),
        cost_estimate=pl.CostEstimate(
            flops=4 * length * model * hidden, bytes_accessed=2 * (length * model + 2 * model * hidden), transcendentals=length * hidden
        ),
    )(normed, gate_up)


def ffn_backward_kernel(grad, weight, slopes, low, high):
    split = low.shape[1] // LANES
    grad_middle = mm(grad[...], weight[...])
    for tile in range(weight.shape[1] // LANES):
        part = grad_middle[:, tile * LANES : (tile + 1) * LANES]
        for kind in range(2):
            at = 2 * tile + kind
            target, to = (low, at) if at < split else (high, at - split)
            slope = slopes[:, at * LANES : (at + 1) * LANES].astype(f32)
            target[:, to * LANES : (to + 1) * LANES] = (part * slope).astype(bf16)


def ffn_backward(grad, down, slopes):
    length, model = grad.shape
    hidden = down.shape[1]
    block = 512
    widths = (2 * hidden - BOTH_LAST, BOTH_LAST)
    return pl.pallas_call(
        ffn_backward_kernel,
        grid=(length // block,),
        in_specs=[
            pl.BlockSpec((block, model), lambda i: (i, 0)),
            pl.BlockSpec((model, hidden), lambda i: (0, 0)),
            pl.BlockSpec((block, 2 * hidden), lambda i: (i, 0)),
        ],
        out_specs=[pl.BlockSpec((block, width), lambda i: (i, 0)) for width in widths],
        out_shape=[jax.ShapeDtypeStruct((length, width), bf16) for width in widths],
        compiler_params=pltpu.CompilerParams(
            dimension_semantics=("arbitrary",), vmem_limit_bytes=VMEM_LIMIT
        ),
        cost_estimate=pl.CostEstimate(
            flops=2 * length * model * hidden, bytes_accessed=2 * (length * model + model * hidden + 4 * length * hidden), transcendentals=0
        ),
    )(grad, down, slopes)


def finish_kernel(count, *refs):
    sources, targets, held, sems = refs[:count], refs[count : 2 * count], refs[2 * count : 3 * count], refs[-1]
    kept, outs = held[:3], refs[3 * count : 3 * count + 3]
    loads = [
        pltpu.make_async_copy(source, here, sems.at[0, at]) for at, (source, here) in enumerate(zip(sources, held))
    ]
    stores = [
        pltpu.make_async_copy(here, target, sems.at[1, at])
        for at, (here, target) in enumerate(zip((*outs, *held[3:]), targets))
    ]
    for load in loads:
        load.start()
    low, high, down = kept
    gate_out, up_out, down_out = outs
    split = low.shape[1] // LANES
    for load in loads[:3]:
        load.wait()
    for tile in range(gate_out.shape[1] // LANES):
        for kind, target in enumerate((gate_out, up_out)):
            at = 2 * tile + kind
            source, start = (low, at) if at < split else (high, at - split)
            target[:, tile * LANES : (tile + 1) * LANES] = source[:, start * LANES : (start + 1) * LANES].astype(f32)
    stores[0].start()
    stores[1].start()
    for load, store in zip(loads[3:], stores[3:]):
        load.wait()
        store.start()
    for tile in range(gate_out.shape[1] // LANES):
        lanes = slice(tile * LANES, (tile + 1) * LANES)
        down_out[lanes, :] = jnp.transpose(down[:, lanes].astype(f32))
    stores[2].start()
    for store in stores:
        store.wait()


def finish(low, high, down, arrays):
    slab, hidden = down.shape
    sources = [low, high, down, *arrays]
    count = len(sources)
    outs = [
        jax.ShapeDtypeStruct((slab, hidden), f32),
        jax.ShapeDtypeStruct((slab, hidden), f32),
        jax.ShapeDtypeStruct((hidden, slab), f32),
    ]
    return pl.pallas_call(
        functools.partial(finish_kernel, count),
        in_specs=anywhere(count),
        out_specs=anywhere(count),
        out_shape=outs + [jax.ShapeDtypeStruct(array.shape, array.dtype) for array in arrays],
        scratch_shapes=[pltpu.VMEM(array.shape, array.dtype) for array in sources]
        + [pltpu.VMEM(out.shape, f32) for out in outs]
        + [pltpu.SemaphoreType.DMA((2, count))],
        compiler_params=pltpu.CompilerParams(vmem_limit_bytes=VMEM_LIMIT),
        cost_estimate=pl.CostEstimate(flops=0, bytes_accessed=40 * slab * hidden, transcendentals=0),
    )(*sources)


def plain_ffn(normed, gate_up):
    gate, up_part = jnp.split(jnp.dot(normed, gate_up, preferred_element_type=f32), 2, axis=1)
    act, sig = silu_parts(gate)
    slopes = jnp.concatenate([up_part * sig * (1.0 + gate * (1.0 - sig)), act], axis=1)
    return (act * up_part).astype(bf16), slopes.astype(bf16)


def plain_ffn_backward(grad, down, slopes):
    grad_middle = jnp.dot(grad, down, preferred_element_type=f32)
    both = (jnp.concatenate([grad_middle, grad_middle], axis=1) * slopes.astype(f32)).astype(bf16)
    return both[:, :-BOTH_LAST], both[:, -BOTH_LAST:]


def plain_finish(low, high, down, arrays):
    gate, up_part = jnp.split(jnp.concatenate([low.astype(f32), high], axis=1), 2, axis=1)
    return gate, up_part, down.astype(f32).T, *arrays


def anywhere(count):
    return [pl.BlockSpec(memory_space=pl.ANY)] * count


def in_vmem(count):
    return [pl.BlockSpec(memory_space=pltpu.VMEM)] * count


def first_gather(w_query, w_key, w_value, w_gate_out, w_beta, w_output, inputs, cotangent, mask, gain, w_gate, w_up, w_down):
    shards = lax.axis_size("dp")
    rows, model = inputs.shape
    slab, width = w_query.shape
    hidden = w_gate.shape[1]
    inner = jax.ShapeDtypeStruct((slab, 4 * width), bf16)
    output = jax.ShapeDtypeStruct((slab, width), bf16)
    pieces = len(pieces_of([inner, output, w_beta], PIECE))
    return pl.pallas_call(
        functools.partial(first_gather_kernel, shards // 2),
        in_specs=in_vmem(10) + anywhere(3),
        out_specs=anywhere(5) + in_vmem(3),
        out_shape=[
            jax.ShapeDtypeStruct((shards, *inner.shape), bf16),
            jax.ShapeDtypeStruct((shards, *output.shape), bf16),
            jax.ShapeDtypeStruct((shards, *w_beta.shape), bf16),
            jax.ShapeDtypeStruct((4 * rows, model), bf16),
            jax.ShapeDtypeStruct((4 * rows, model), bf16),
            jax.ShapeDtypeStruct((slab, 2 * hidden), bf16),
            jax.ShapeDtypeStruct((slab, hidden), bf16),
            jax.ShapeDtypeStruct((rows, model), bf16),
        ],
        scratch_shapes=[
            pltpu.VMEM(inner.shape, bf16),
            pltpu.VMEM(output.shape, bf16),
            pltpu.VMEM((rows, model), bf16),
            pltpu.VMEM((slab, hidden), f32),
            pltpu.VMEM((slab, hidden), f32),
            pltpu.VMEM((hidden, slab), f32),
        ]
        + LineGather.scratch(shards // 2, pieces, 3)
        + [pltpu.SemaphoreType.DMA((6,)) for _ in range(4)]
        + [pltpu.SemaphoreType.DMA((5,))],
        compiler_params=pltpu.CompilerParams(
            collective_id=1, has_side_effects=True, vmem_limit_bytes=VMEM_LIMIT
        ),
        cost_estimate=pl.CostEstimate(flops=80_000_000_000, bytes_accessed=20_000_000, transcendentals=0),
    )(w_query, w_key, w_value, w_gate_out, w_beta, w_output, inputs, cotangent, mask, gain, w_gate, w_up, w_down)


def branch_kernel(z, weight, inputs, gain, resid, full, part, first, second, stage, low, s_send, s_recv, g_send, g_recv, local):
    scatter = PlaneScatter(part, first, second, stage, s_send, s_recv)
    gather = PlaneGather(low, full, g_send, g_recv)
    rows = scatter.rows
    slab = weight.shape[1]
    greet(tensor=scatter.across)
    greet(tensor=scatter.along)

    def compute(block):
        here = pl.ds(scatter.start_of(block, 0), rows)

        def column(index, carry):
            part[here, pl.ds(pl.multiple_of(index * slab, slab), slab)] = mm_nt(z[here, :], weight[index]).astype(bf16)
            return carry

        lax.fori_loop(0, weight.shape[0], column, 0)

    compute(scatter.far)
    wait_greetings(2)
    scatter.start_far()
    compute(scatter.across)
    scatter.start_near(0)
    compute(scatter.along)
    scatter.start_near(1)
    compute(scatter.me)
    scatter.relay(0)
    scatter.relay(1)
    for half in (0, 1):
        scatter.ready(half)

        def norm(index, carry):
            at = pl.multiple_of(index * TILE, TILE)
            here = pl.ds(pl.multiple_of(half * scatter.half + at, TILE), TILE)
            value = inputs[here, :].astype(f32) + scatter.tile(half, at)
            resid[here, :] = value
            scale = lax.rsqrt(jnp.mean(value * value, axis=-1, keepdims=True) + norm_epsilon)
            low[here, :] = (value * scale * gain[...]).astype(bf16)
            return carry

        lax.fori_loop(0, scatter.half // TILE, norm, 0)
        gather.start(half)
    keep = pltpu.make_async_copy(low, full.at[pl.ds(pl.multiple_of(gather.me * rows, rows), rows)], local.at[0])
    keep.start()
    gather.relay(0)
    gather.relay(1)
    scatter.finish()
    gather.finish()
    keep.wait()


def branch_and_norm(z, weight, inputs, gain):
    rows, model = inputs.shape
    return pl.pallas_call(
        branch_kernel,
        in_specs=in_vmem(4),
        out_specs=in_vmem(1) + anywhere(1),
        out_shape=[
            jax.ShapeDtypeStruct((rows, model), f32),
            jax.ShapeDtypeStruct((4 * rows, model), bf16),
        ],
        scratch_shapes=[pltpu.VMEM((4 * rows, model), bf16)]
        + plane_scatter_scratch(rows, model)[:3]
        + [pltpu.VMEM((rows, model), bf16)]
        + [pltpu.SemaphoreType.DMA((6,)) for _ in range(4)]
        + [pltpu.SemaphoreType.DMA((1,))],
        compiler_params=pltpu.CompilerParams(
            collective_id=2, has_side_effects=True, vmem_limit_bytes=VMEM_LIMIT
        ),
        cost_estimate=pl.CostEstimate(flops=50_000_000_000, bytes_accessed=20_000_000, transcendentals=0),
    )(z, weight, inputs, gain)


def norm_backward(value, grad, gain):
    scale = lax.rsqrt(jnp.mean(value * value, axis=-1, keepdims=True) + norm_epsilon)
    normed = value * scale
    inner = grad * gain
    return scale * (inner - normed * jnp.mean(inner * normed, axis=-1, keepdims=True)), grad * normed


class LineScatter:
    def __init__(self, chips, parts, stages, trades, arrived, sems):
        self.chips, self.parts, self.stages, self.trades, self.arrived = chips, parts, stages, trades, arrived
        self.pieces = pieces_of(parts, PIECE)
        self.right_send, self.right_receive, self.left_send, self.left_receive = sems[:4]
        self.core_send, self.core_receive, self.local = sems[4:]
        self.chip, self.core = chip_and_core()

    @staticmethod
    def scratch(chips, arrays):
        shapes = [array.shape[-2:] for array in arrays]
        pieces = len(pieces_of(arrays, PIECE))
        return (
            [pltpu.VMEM((chips, *shape), bf16) for shape in shapes]
            + [pltpu.VMEM((chips, *shape), bf16) for shape in shapes]
            + [pltpu.VMEM((chips + 1, *shape), bf16) for shape in shapes]
            + [pltpu.SemaphoreType.DMA((chips, pieces)) for _ in range(6)]
            + [pltpu.SemaphoreType.DMA((len(arrays), chips))]
        )

    def order(self):
        order = []
        for step in range(self.chips // 2):
            order += [self.chips - 1 - step, step]
        return order

    def trade(self, piece, dest):
        index, start, rows = self.pieces[piece]
        return remote(
            self.parts[index].at[dest * 2 + 1 - self.core, pl.ds(start, rows)],
            self.trades[index].at[dest, pl.ds(start, rows)],
            self.core_send.at[dest, piece],
            self.core_receive.at[dest, piece],
            dp=self.chip * 2 + 1 - self.core,
        )

    def load(self, index, dest):
        return pltpu.make_async_copy(
            self.parts[index].at[dest * 2 + self.core], self.stages[index].at[dest], self.local.at[index, dest]
        )

    def right(self, piece, dest):
        index, start, rows = self.pieces[piece]
        here = pl.ds(start, rows)
        return remote(
            self.stages[index].at[dest, here],
            self.arrived[index].at[dest, here],
            self.right_send.at[dest, piece],
            self.right_receive.at[dest, piece],
            dp=(self.chip + 1) * 2 + self.core,
        )

    def left_slot(self, dest, chip):
        return jnp.where(dest == chip, self.chips, dest)

    def left(self, piece, dest):
        index, start, rows = self.pieces[piece]
        here = pl.ds(start, rows)
        return remote(
            self.stages[index].at[dest, here],
            self.arrived[index].at[self.left_slot(dest, self.chip - 1), here],
            self.left_send.at[dest, piece],
            self.left_receive.at[dest, piece],
            dp=(self.chip - 1) * 2 + self.core,
        )

    def start(self):
        for dest in self.order():
            for index in range(len(self.parts)):
                self.load(index, dest).start()
            for piece in range(len(self.pieces)):
                self.trade(piece, dest).start()

    def add(self, piece, dest, slots, put=None):
        index, start, rows = self.pieces[piece]

        def tile(at, carry):
            here = pl.ds(pl.multiple_of(start + at * TILE, TILE), TILE)
            total = self.stages[index][dest, here, :].astype(f32) + self.trades[index][dest, here, :].astype(f32)
            for slot in slots:
                total = total + self.arrived[index][slot, here, :].astype(f32)
            if put is None:
                self.stages[index][dest, here, :] = total.astype(bf16)
            else:
                put[index](here, total)
            return carry

        lax.fori_loop(0, rows // TILE, tile, 0)

    def first_of(self, piece):
        return piece == 0 or self.pieces[piece - 1][0] != self.pieces[piece][0]

    def receive(self, piece, dest):
        if self.first_of(piece):
            self.load(self.pieces[piece][0], dest).wait()
        self.trade(piece, dest).wait_recv()

    def step(self, step, ends, turns=(0, 1)):
        to_right, to_left = self.chips - 1 - step, step

        def send_right(piece):
            self.receive(piece, to_right)
            if not ends:
                self.right(piece, to_right).wait_recv()
            self.add(piece, to_right, [] if ends else [to_right])
            self.right(piece, to_right).start()

        def send_left(piece):
            self.receive(piece, to_left)
            if not ends:
                self.left(piece, to_left).wait_recv()
            self.add(piece, to_left, [] if ends else [to_left])
            self.left(piece, to_left).start()

        count = len(self.pieces)
        if ends:
            when(self.chip == 0, lambda: [send_right(piece) for piece in range(count)] and None)
            when(self.chip == self.chips - 1, lambda: [send_left(piece) for piece in range(count)] and None)
            return
        inner_right = (self.chip > 0) & (to_right > self.chip)
        inner_left = (self.chip < self.chips - 1) & (to_left < self.chip)
        low = self.chip < self.chips // 2
        lead = 2
        for at in range(count + lead):
            early, late = at, at - lead
            if 0 in turns and early < count:
                when(low & inner_right, functools.partial(send_right, early))
                when(jnp.logical_not(low) & inner_left, functools.partial(send_left, early))
            if 1 in turns and late >= 0:
                when(low & inner_left, functools.partial(send_left, late))
                when(jnp.logical_not(low) & inner_right, functools.partial(send_right, late))

    def keep(self, outs, pieces):
        me = self.chip
        for piece in pieces:
            self.receive(piece, me)
            when(me > 0, lambda: self.right(piece, me).wait_recv())
            when(me < self.chips - 1, lambda: self.left(piece, me).wait_recv())
            when((me > 0) & (me < self.chips - 1), lambda: self.add(piece, me, [me, self.chips], outs))
            when(me == 0, lambda: self.add(piece, me, [self.chips], outs))
            when(me == self.chips - 1, lambda: self.add(piece, me, [me], outs))

    def finish(self):
        for piece in range(len(self.pieces)):
            for dest in range(self.chips):
                self.trade(piece, dest).wait_send()
                when(dest > self.chip, lambda: self.right(piece, dest).wait_send())
                when(dest < self.chip, lambda: self.left(piece, dest).wait_send())


def resid_kernel(
    chips, slab, low_far, high_far, weight_far, z_far, out_weight_far, resid, grad_out, gain, high_part,
    grad_resid, dgain, dz, output_grad, high_out,
    part, first, second, stage, low, full, total, s_send, s_recv, g_send, g_recv,
    grad_both, weight, z, out_weight, load_sems, *rest
):
    scatter = PlaneScatter(part, first, second, stage, s_send, s_recv)
    gather = PlaneGather(low, full, g_send, g_recv)
    line = LineScatter(chips, [high_part], rest[:1], rest[1:2], rest[2:3], rest[3:])
    rows = scatter.rows
    split = low_far.shape[1]
    slabs = weight.shape[0] // slab
    order = (scatter.far, scatter.across, scatter.along, scatter.me)
    greetings = greet_line(chips)
    greet(tensor=scatter.across)
    greet(tensor=scatter.along)

    def rows_loads(at):
        here = pl.ds(scatter.start_of(order[at], 0), rows)
        return [
            pltpu.make_async_copy(far.at[here], grad_both.at[here, lanes], load_sems.at[slabs + 2 * at + which])
            for which, (far, lanes) in enumerate(
                ((low_far, pl.ds(0, split)), (high_far, pl.ds(split, grad_both.shape[1] - split)))
            )
        ]

    def slab_load(index):
        here = pl.ds(pl.multiple_of(index * slab, slab), slab)
        return pltpu.make_async_copy(weight_far.at[here], weight.at[here], load_sems.at[index])

    late_loads = [
        pltpu.make_async_copy(z_far, z, load_sems.at[slabs + 8]),
        pltpu.make_async_copy(out_weight_far, out_weight, load_sems.at[slabs + 9]),
    ]
    for at in range(4):
        for load in rows_loads(at):
            load.start()
        if at == 0:
            for index in range(slabs):
                slab_load(index).start()
    for load in late_loads:
        load.start()

    def compute(at):
        here = pl.ds(scatter.start_of(order[at], 0), rows)
        for load in rows_loads(at):
            load.wait()

        def column(index, carry):
            lanes = pl.ds(pl.multiple_of(index * slab, slab), slab)
            if at == 0:
                slab_load(index).wait()
            part[here, lanes] = mm_nt(grad_both[here, :], weight[lanes, :]).astype(bf16)
            return carry

        lax.fori_loop(0, slabs, column, 0)

    compute(0)
    wait_greetings(2 + greetings)
    scatter.start_far()
    line.start()
    compute(1)
    scatter.start_near(0)
    compute(2)
    scatter.start_near(1)
    line.step(0, True)
    compute(3)
    dgain[...] = jnp.zeros_like(dgain)
    scatter.relay(0)
    scatter.relay(1)
    for step in range(1, chips - 1):
        line.step(step, True)
    for half in (0, 1):
        scatter.ready(half)

        def norm(index, carry):
            at = pl.multiple_of(index * TILE, TILE)
            here = pl.ds(pl.multiple_of(half * scatter.half + at, TILE), TILE)
            back, gain_part = norm_backward(resid[here, :], scatter.tile(half, at), gain[...])
            value = grad_out[here, :].astype(f32) + back
            grad_resid[here, :] = value
            low[here, :] = value.astype(bf16)
            dgain[...] += jnp.sum(gain_part, axis=0, keepdims=True)
            return carry

        lax.fori_loop(0, scatter.half // TILE, norm, 0)
        gather.start(half)
        if half == 0:
            line.step(0, False, (0,))
    for load in late_loads:
        load.wait()

    def use(block, left, fresh=False):
        here = pl.ds(pl.multiple_of(block * rows, rows), rows)
        dz[here, :] = mm(left[...], out_weight[...]).astype(bf16)

        def column(index, carry):
            lanes = pl.ds(pl.multiple_of(index * slab, slab), slab)
            product = mm_tn(left[:, lanes], z[here, :])
            total[lanes, :] = product if fresh else total[lanes, :] + product
            return carry

        lax.fori_loop(0, slabs, column, 0)

    def block_of(block):
        return full.at[pl.ds(pl.multiple_of(block * rows, rows), rows)]

    gather.relay(0)
    gather.relay(1)
    line.step(0, False, (1,))
    for step in range(1, chips - 1):
        line.step(step, False)
    use(scatter.me, low, True)
    gather.near(0)
    use(scatter.across, block_of(scatter.across))
    gather.near(1)
    use(scatter.along, block_of(scatter.along))

    def put(here, total):
        high_out[here, :] = total

    line.keep([put], range(len(line.pieces)))
    gather.diagonal()
    use(scatter.far, block_of(scatter.far))
    output_grad[...] = total[...].astype(bf16)
    gather.sent()
    scatter.finish()
    line.finish()


def resid_backward(grad_low, grad_high, weight, z, out_weight, resid, grad_out, gain, high_part):
    chips = lax.axis_size("dp") // 2
    rows, model = resid.shape
    width = z.shape[1]
    slab, columns = high_part.shape[1:]
    return pl.pallas_call(
        functools.partial(resid_kernel, chips, 256),
        in_specs=anywhere(5) + in_vmem(3) + anywhere(1),
        out_specs=in_vmem(5),
        out_shape=[
            jax.ShapeDtypeStruct((rows, model), f32),
            jax.ShapeDtypeStruct((1, model), f32),
            jax.ShapeDtypeStruct((4 * rows, width), bf16),
            jax.ShapeDtypeStruct((model, width), bf16),
            jax.ShapeDtypeStruct((slab, columns), f32),
        ],
        scratch_shapes=[pltpu.VMEM((4 * rows, model), bf16)]
        + plane_scatter_scratch(rows, model)[:3]
        + [
            pltpu.VMEM((rows, model), bf16),
            pltpu.VMEM((4 * rows, model), bf16),
            pltpu.VMEM((model, width), f32),
        ]
        + [pltpu.SemaphoreType.DMA((6,)) for _ in range(4)]
        + [
            pltpu.VMEM((4 * rows, weight.shape[1]), bf16),
            pltpu.VMEM(weight.shape, bf16),
            pltpu.VMEM(z.shape, bf16),
            pltpu.VMEM(out_weight.shape, bf16),
            pltpu.SemaphoreType.DMA((model // 256 + 10,)),
        ]
        + LineScatter.scratch(chips, [high_part]),
        compiler_params=pltpu.CompilerParams(
            collective_id=3, has_side_effects=True, vmem_limit_bytes=LARGE_LIMIT
        ),
        cost_estimate=pl.CostEstimate(flops=1_000_000, bytes_accessed=1_000_000, transcendentals=0),
    )(grad_low, grad_high, weight, z, out_weight, resid, grad_out, gain, high_part)


SMALL = 512


def last_kernel(chips, *refs):
    inner_part, output_part, weight, inner, dpre_far, middle_far, inputs_far, grad_resid_far, resid_far = refs[:9]
    mask, first_gain, ffn_dgain, head_dgain, dtaps, dbeta, beta, beta_part = refs[9:17]
    refs = refs[3:]
    query_out, key_out, value_out, gate_out, beta_out, output_out, input_grad, out = refs[14:22]
    first_out, ffn_out, head_out, taps_out = refs[22:26]
    refs = refs[26:]
    line = LineScatter(chips, [inner_part, output_part], refs[:2], refs[2:4], refs[4:6], refs[6:13])
    grad = PlaneScatter(*refs[13:19])
    ffn = PlaneScatter(*refs[19:25])
    turned, small, near, lined, dgain, small_send, small_receive, inner_slabs, down_slabs, slab_sems = refs[25:35]
    dpre, middle, inputs, grad_resid, resid, load_sems = refs[35:41]
    chip, core = line.chip, line.core
    slab = inner_part.shape[1]
    shards = 2 * chips
    sibling = chip * 2 + 1 - core
    greet(tensor=grad.across)
    greet(tensor=grad.along)
    greet(dp=sibling)
    for other in range(1, chips):
        greet(dp=lax.rem(chip + other, chips) * 2 + core)

    def stream(at, source, buffers, kind):
        return pltpu.make_async_copy(source.at[at], buffers.at[lax.rem(at, 2)], slab_sems.at[kind, lax.rem(at, 2)])

    def product(left, source, buffers, target, kind, extra=None):
        def column(index, carry):
            when(index < shards - 1, lambda: stream(index + 1, source, buffers, kind).start())
            stream(index, source, buffers, kind).wait()
            lanes = pl.ds(pl.multiple_of(index * slab, slab), slab)
            total = mm_nt(left[...], buffers[lax.rem(index, 2)])
            if extra is not None:
                total = total + mm(extra[0][...], extra[1][index])
            target[:, lanes] = total.astype(bf16)
            return carry

        lax.fori_loop(0, shards, column, 0)

    loads = [
        pltpu.make_async_copy(source, target, load_sems.at[at])
        for at, (source, target) in enumerate(
            (
                (dpre_far, dpre),
                (middle_far, middle),
                (inputs_far, inputs),
                (grad_resid_far, grad_resid),
                (resid_far, resid),
            )
        )
    ]
    wait_greetings(2 + chips)
    line.start()
    for load in loads[:2]:
        load.start()
    stream(0, inner, inner_slabs, 0).start()
    stream(0, weight, down_slabs, 1).start()
    for load in loads[2:]:
        load.start()
    dgain[...] = jnp.zeros_like(dgain)
    small[...] = jnp.zeros_like(small)
    line.step(0, True)
    loads[0].wait()
    product(dpre, inner, inner_slabs, grad.part, 0, (dbeta, beta))
    grad.start_far()
    grad.start_near(0)
    grad.start_near(1)
    line.step(1, True)
    loads[1].wait()
    product(middle, weight, down_slabs, ffn.part, 1)
    for step in range(2, chips - 1):
        line.step(step, True)
    line.step(0, False)
    grad.relay(0)
    grad.relay(1)
    ffn.start_far()
    ffn.start_near(0)
    ffn.start_near(1)
    for step in range(1, chips - 1):
        line.step(step, False)
    for load in loads[2:]:
        load.wait()
    for half in (0, 1):
        grad.ready(half)

        def norm(index, carry):
            at = pl.multiple_of(index * TILE, TILE)
            here = pl.ds(pl.multiple_of(half * grad.half + at, TILE), TILE)
            back, gain_part = norm_backward(inputs[here, :].astype(f32), grad.tile(half, at), first_gain[...])
            input_grad[here, :] = grad_resid[here, :] + back
            dgain[...] += jnp.sum(gain_part, axis=0, keepdims=True)
            return carry

        lax.fori_loop(0, grad.half // TILE, norm, 0)
    model = dgain.shape[1]
    count = model // SMALL
    for row in range(count):
        lanes = slice(row * SMALL, (row + 1) * SMALL)
        small[0, row : row + 1, :] = dgain[:, lanes]
        small[0, count + row : count + row + 1, :] = ffn_dgain[:, lanes]
    small[0, 2 * count : 2 * count + 1, 0:HEAD] = head_dgain[...]
    small[0, 16 : 16 + 3 * TAPS, :] = dtaps[...]
    heads = beta_out.shape[0]
    for head in range(heads):
        for row in range(count):
            at = 32 + head * count + row
            small[0, at : at + 1, :] = beta_part[head : head + 1, row * SMALL : (row + 1) * SMALL]

    def hop(at):
        where = (dict(tensor=grad.across), dict(tensor=grad.along), dict(dp=sibling))[at]
        return remote(small.at[at], near.at[at], small_send.at[at], small_receive.at[at], **where)

    def hopped(at):
        hop(at).wait()
        if at < 2:
            small[at + 1, 0:16, :] = small[at, 0:16, :] + near[at, 0:16, :]
            small[at + 1, 16:, :] = small[at, 16:, :]
        else:
            small[3] = small[2] + near[2]

    def tell(other):
        to = lax.rem(chip + other, chips)
        return remote(
            small.at[3], lined.at[chip], small_send.at[2 + other], small_receive.at[2 + other], dp=to * 2 + core
        )

    def put_inner(here, total):
        width = query_out.shape[1]
        for kind, target in enumerate((query_out, key_out, value_out, gate_out)):
            target[here, :] = total[:, kind * width : (kind + 1) * width]

    def put_output(here, total):
        turned[here, :] = total

    puts = [put_inner, put_output]
    hop(0).start()
    ffn.relay(0)
    ffn.relay(1)
    hopped(0)
    hop(1).start()
    pieces = len(line.pieces)
    line.keep(puts, range(0, pieces - 3))
    hopped(1)
    hop(2).start()
    for half in (0, 1):
        ffn.ready(half)

        def finish_rows(index, carry):
            at = pl.multiple_of(index * TILE, TILE)
            here = pl.ds(pl.multiple_of(half * ffn.half + at, TILE), TILE)
            out[here, :] = ((resid[here, :] + ffn.tile(half, at)) * mask[here, :]).astype(bf16)
            return carry

        lax.fori_loop(0, ffn.half // TILE, finish_rows, 0)
    hopped(2)
    lined[chip] = small[3]
    for other in range(1, chips):
        tell(other).start()
    line.keep(puts, range(pieces - 3, pieces))
    output_out[...] = jnp.transpose(turned[...])
    for other in range(1, chips):
        tell(other).wait()
    total = lined[0]
    for other in range(1, chips):
        total = total + lined[other]
    for row in range(count):
        lanes = slice(row * SMALL, (row + 1) * SMALL)
        first_out[:, lanes] = total[row : row + 1, :]
        ffn_out[:, lanes] = total[count + row : count + row + 1, :]
    head_out[...] = total[2 * count : 2 * count + 1, 0:HEAD]
    summed = small.at[0]
    summed[...] = total
    mine = (chip * 2 + core) * slab
    lanes = pl.ds(pl.multiple_of(lax.rem(mine, SMALL), slab), slab)
    for head in range(heads):
        beta_out[head : head + 1, :] = summed[pl.ds(32 + head * count + mine // SMALL, 1), lanes]
    for kind in range(3):
        taps_out[kind] = total[16 + kind * TAPS : 16 + (kind + 1) * TAPS, :]
    grad.finish()
    ffn.finish()
    line.finish()


def last_scatter(
    inner_part, output_part, weight, inner, dpre, middle, inputs, grad_resid, resid, mask, gain, ffn_dgain, head_dgain, dtaps,
    dbeta, beta, beta_part
):
    chips = lax.axis_size("dp") // 2
    rows, model = inputs.shape
    slab, width = output_part.shape[1:]
    arrays = [inner_part, output_part]
    shape = jax.ShapeDtypeStruct
    return pl.pallas_call(
        functools.partial(last_kernel, chips),
        in_specs=anywhere(9) + in_vmem(8),
        out_specs=in_vmem(12),
        out_shape=[shape((slab, width), f32)] * 4
        + [
            shape((width // HEAD, slab), f32),
            shape((width, slab), f32),
            shape((rows, model), f32),
            shape((rows, model), bf16),
            shape((1, model), f32),
            shape((1, model), f32),
            shape((1, HEAD), f32),
            shape((3, TAPS, dtaps.shape[1]), f32),
        ],
        scratch_shapes=LineScatter.scratch(chips, arrays)
        + [pltpu.VMEM((4 * rows, model), bf16)]
        + plane_scatter_scratch(rows, model)
        + [pltpu.VMEM((4 * rows, model), bf16)]
        + plane_scatter_scratch(rows, model)
        + [
            pltpu.VMEM((slab, width), f32),
            pltpu.VMEM((4, 48, SMALL), f32),
            pltpu.VMEM((3, 48, SMALL), f32),
            pltpu.VMEM((chips, 48, SMALL), f32),
            pltpu.VMEM((1, model), f32),
            pltpu.SemaphoreType.DMA((2 + chips,)),
            pltpu.SemaphoreType.DMA((2 + chips,)),
            pltpu.VMEM((2, *inner.shape[1:]), bf16),
            pltpu.VMEM((2, *weight.shape[1:]), bf16),
            pltpu.SemaphoreType.DMA((2, 2)),
            pltpu.VMEM(dpre.shape, bf16),
            pltpu.VMEM(middle.shape, bf16),
            pltpu.VMEM((rows, model), bf16),
            pltpu.VMEM((rows, model), f32),
            pltpu.VMEM((rows, model), f32),
            pltpu.SemaphoreType.DMA((5,)),
        ],
        compiler_params=pltpu.CompilerParams(
            collective_id=4, has_side_effects=True, vmem_limit_bytes=LARGE_LIMIT
        ),
        cost_estimate=pl.CostEstimate(flops=1_000_000, bytes_accessed=1_000_000, transcendentals=0),
    )(inner_part, output_part, weight, inner, dpre, middle, inputs, grad_resid, resid, mask, gain, ffn_dgain, head_dgain, dtaps, dbeta, beta, beta_part)


def rms_norm(values, gain):
    return (
        values * lax.rsqrt(jnp.mean(values * values, axis=-1, keepdims=True) + norm_epsilon) * gain
    )


def gather(values, axis):
    return lax.all_gather(values, axis, axis=0, tiled=True)


def scatter(values, axis):
    return lax.psum_scatter(values, axis, scatter_dimension=0, tiled=True)


def plain_first_gather(
    w_query, w_key, w_value, w_gate_out, w_beta, w_output, inputs, cotangent, mask, gain, w_gate, w_up, w_down
):
    shards = lax.axis_size("dp")
    inner = jnp.concatenate([w_query, w_key, w_value, w_gate_out], axis=1).astype(bf16)
    output = w_output.T.astype(bf16)
    grad = (cotangent.astype(f32) * mask).astype(bf16)
    return (
        gather(inner, "dp").reshape(shards, *inner.shape),
        gather(output, "dp").reshape(shards, *output.shape),
        gather(w_beta, "dp").reshape(shards, *w_beta.shape),
        gather(rms_norm(inputs.astype(f32), gain[0]).astype(bf16), "tensor"),
        gather(grad, "tensor"),
        jnp.concatenate([w_gate, w_up], axis=1).astype(bf16),
        w_down.T.astype(bf16),
        grad,
    )


def plain_branch_and_norm(z, weight, inputs, gain):
    branch = mm_nt(z, weight.reshape(-1, z.shape[1])).astype(bf16)
    resid = inputs.astype(f32) + scatter(branch, "tensor").astype(f32)
    return resid, gather(rms_norm(resid, gain[0]).astype(bf16), "tensor")


def plain_resid_backward(grad_low, grad_high, weight, z, out_weight, resid, grad_out, gain, high_part):
    part = mm_nt(jnp.concatenate([grad_low, grad_high], axis=1), weight).astype(bf16)
    back, gain_part = norm_backward(resid, scatter(part, "tensor").astype(f32), gain)
    value = grad_out.astype(f32) + back
    full = gather(value.astype(bf16), "tensor")
    high = scatter(high_part.reshape(-1, high_part.shape[2]), "dp").astype(f32)
    dgain = jnp.sum(gain_part, axis=0, keepdims=True)
    return value, dgain, mm(full, out_weight).astype(bf16), mm_tn(full, z).astype(bf16), high


def plain_last_scatter(
    inner_part, output_part, weight, inner, dpre, middle, inputs, grad_resid, resid, mask, gain, ffn_dgain, head_dgain, dtaps,
    dbeta, beta, beta_part
):
    beta = beta.transpose(1, 0, 2).reshape(BETA_PAD, -1)
    grad_part = (mm_nt(dpre, inner.reshape(-1, inner.shape[2])) + mm(dbeta, beta)).astype(bf16)
    slab = inner_part.shape[1]
    beta_total = lax.psum(beta_part[: output_part.shape[2] // HEAD], "dp")
    beta_total = lax.dynamic_slice_in_dim(beta_total, lax.axis_index("dp") * slab, slab, axis=1)
    inner, output = (
        scatter(part.reshape(-1, part.shape[-1]), "dp").astype(f32) for part in (inner_part, output_part)
    )
    width = output.shape[1]
    back, gain_part = norm_backward(inputs.astype(f32), scatter(grad_part, "tensor").astype(f32), gain)
    ffn_part = mm_nt(middle, weight.reshape(-1, weight.shape[2])).astype(bf16)
    out = ((resid + scatter(ffn_part, "tensor").astype(f32)) * mask).astype(bf16)
    gains = (jnp.sum(gain_part, axis=0, keepdims=True), ffn_dgain, head_dgain)
    return (
        *(inner[:, kind * width : (kind + 1) * width] for kind in range(4)),
        beta_total,
        output.T,
        grad_resid + back,
        out,
        *lax.psum(gains, ("dp", "tensor")),
        lax.psum(dtaps, "dp").reshape(3, TAPS, -1),
    )


def body(
    inputs,
    cotangent,
    lengths,
    norm_gain,
    w_query,
    w_key,
    w_value,
    w_gate_out,
    w_beta,
    conv_weight,
    out_norm_gain,
    w_output,
    ffn_norm_gain,
    w_gate,
    w_up,
    w_down,
):
    tensor_count = lax.axis_size("tensor")
    shards = lax.axis_size("dp")
    kernels = tensor_count == 4 and shards == 8
    rows, model = inputs.shape
    length = rows * tensor_count
    width = w_query.shape[1]
    heads = width // HEAD
    hidden = w_gate.shape[1]
    slab = w_query.shape[0]
    taps = conv_weight.reshape(3 * TAPS, width)
    first_gain, head_gain = norm_gain.reshape(1, model), out_norm_gain.reshape(1, HEAD)
    ffn_gain = ffn_norm_gain.reshape(1, model)

    positions = lax.axis_index("tensor") * rows + jnp.arange(rows, dtype=jnp.int32)
    mask = (positions < lengths[0]).astype(f32)[:, None]
    beta_rows = jnp.pad(w_beta.T, ((0, BETA_PAD - w_beta.shape[1]), (0, 0))).astype(bf16)
    inner, full_output, full_beta, normed, grad_full, gate_up, down, grad_out = (
        first_gather if kernels else plain_first_gather
    )(w_query, w_key, w_value, w_gate_out, beta_rows, w_output, inputs, cotangent, mask, first_gain, w_gate, w_up, w_down)
    gate_up = gather(gate_up, "dp")
    down = gather(down, "dp")

    pre = jnp.dot(normed, inner.reshape(model, -1), preferred_element_type=f32).astype(bf16)
    beta_pre = mm_nt(normed, full_beta.transpose(1, 0, 2).reshape(BETA_PAD, model))
    z, conv, mixed, inverse, states = mixer_forward(pre, beta_pre, taps, head_gain, heads)
    resid, normed2 = (branch_and_norm if kernels else plain_branch_and_norm)(z, full_output, inputs, ffn_gain)
    middle, slopes = (ffn if kernels else plain_ffn)(normed2, gate_up)
    down_part = mm_tn(grad_full, middle).astype(bf16)
    down, down_part = lax.optimization_barrier((down, down_part))
    down_total = scatter(down_part, "dp")
    grad_low, grad_high = (ffn_backward if kernels else plain_ffn_backward)(grad_full, down, slopes)
    low_part, high_part = mm_tn(normed2, grad_low).astype(bf16), mm_tn(normed2, grad_high).astype(bf16)
    grad_low, grad_high, low_part = lax.optimization_barrier((grad_low, grad_high, low_part))
    low_total = scatter(low_part, "dp")
    grad_resid, ffn_dgain, dz, output_grad, high_total = (resid_backward if kernels else plain_resid_backward)(
        grad_low,
        grad_high,
        gate_up,
        z,
        full_output.reshape(model, width),
        resid,
        grad_out,
        ffn_gain,
        high_part.reshape(shards, slab, -1),
    )
    dpre, dbeta, beta_part, dtaps, head_dgain = mixer_backward(
        pre, beta_pre, normed, conv, mixed, dz, inverse, states, taps, head_gain, heads
    )
    output_grad = output_grad.reshape(shards, slab, width)
    inner_grad = mm_tn(normed, dpre).astype(bf16).reshape(shards, slab, -1)
    results = (last_scatter if kernels else plain_last_scatter)(
        inner_grad,
        output_grad,
        down.reshape(shards, slab, hidden),
        inner,
        dpre,
        middle,
        inputs,
        grad_resid,
        resid,
        mask,
        first_gain,
        ffn_dgain,
        head_dgain,
        dtaps,
        dbeta,
        full_beta,
        beta_part,
    )
    gate_total, up_total, down_total, *results = (finish if kernels else plain_finish)(
        low_total, high_total, down_total, results
    )
    query_total, key_total, value_total, gate_out_total, beta_total, output_total, input_grad, output = results[:8]
    first_total, ffn_total, head_total, taps_total = results[8:]
    return (
        output,
        input_grad,
        first_total[0],
        query_total,
        key_total,
        value_total,
        gate_out_total,
        beta_total.T,
        taps_total,
        head_total[0],
        output_total,
        ffn_total[0],
        gate_total,
        up_total,
        down_total,
    )


def solution(mesh):
    rows = P(("dp", "tensor"), None)
    split = P("dp", "tensor")
    turned = P("tensor", "dp")
    taps = P(None, None, "tensor")
    return jax.shard_map(
        body,
        mesh=mesh,
        in_specs=(rows, rows, P("dp"), P(), split, split, split, split, split, taps, P(), turned, P(), split, split, turned),
        out_specs=(rows, rows, P(), split, split, split, split, split, taps, P(), turned, P(), split, split, turned),
        check_vma=False,
    )
```

```python
import functools
import jax
import jax.numpy as jnp
from jax import lax
from jax.experimental import pallas as pl
from jax.experimental.pallas import tpu as pltpu
from jax.sharding import PartitionSpec as P

norm_epsilon = 1e-06
head_epsilon = 1e-05
HEAD = 128
CHUNK = 128
STEP = 256
TAPS = 4
BETA_PAD = 16
VMEM_LIMIT = 56 * 1024 * 1024
f32 = jnp.float32
bf16 = jnp.bfloat16


def mm(a, b):
    return lax.dot_general(a, b, (((1,), (0,)), ((), ())), preferred_element_type=f32)


def mm_nt(a, b):
    return lax.dot_general(a, b, (((1,), (1,)), ((), ())), preferred_element_type=f32)


def mm_tn(a, b):
    return lax.dot_general(a, b, (((0,), (0,)), ((), ())), preferred_element_type=f32)


def chunk_indices():
    row = lax.broadcasted_iota(jnp.int32, (CHUNK, CHUNK), 0)
    col = lax.broadcasted_iota(jnp.int32, (CHUNK, CHUNK), 1)
    return row, col


def unit_lower_inverses(stricts, row, col):
    apart = row ^ col
    inverses = [jnp.where(row == col, 1.0, jnp.where(apart == 1, -strict, 0.0)) for strict in stricts]
    span = 2
    while span < CHUNK:
        here = (apart >= span) & (apart < 2 * span)
        lows = [inverse.astype(bf16) for inverse in inverses]
        firsts = [mm(low, jnp.where(here, strict, 0.0).astype(bf16)).astype(bf16) for low, strict in zip(lows, stricts)]
        inverses = [inverse - mm(first, low) for inverse, first, low in zip(inverses, firsts, lows)]
        span *= 2
    return [inverse.astype(bf16) for inverse in inverses]


def silu_parts(conv):
    sig = jax.nn.sigmoid(conv)
    return conv * sig, sig


def forward_kernel(
    heads, pre_ref, beta_ref, taps_ref, gain_ref, z_ref, conv_ref, mixed_ref, inv_ref, state_ref, hist, state
):
    step = pl.program_id(0)
    width = heads * HEAD
    rows = pre_ref.shape[0]

    @pl.when(step == 0)
    def _():
        hist[0:8, :] = jnp.zeros((8, 3 * width), f32)
        state[...] = jnp.zeros_like(state)

    @pl.when(step > 0)
    def _():
        hist[0:8, :] = hist[rows : rows + 8, :]

    hist[8 : 8 + rows, :] = pre_ref[:, 0 : 3 * width].astype(f32)
    row, col = chunk_indices()
    beta_all = jax.nn.sigmoid(beta_ref[...])
    work = []
    for head in range(heads):
        parts = []
        for kind in range(3):
            lanes = slice(kind * width + head * HEAD, kind * width + (head + 1) * HEAD)
            total = taps_ref[kind * TAPS : kind * TAPS + 1, head * HEAD : (head + 1) * HEAD] * hist[5 : 5 + rows, lanes]
            for tap in range(1, TAPS):
                total = total + taps_ref[
                    kind * TAPS + tap : kind * TAPS + tap + 1, head * HEAD : (head + 1) * HEAD
                ] * hist[5 + tap : 5 + tap + rows, lanes]
            conv_ref[:, lanes] = total
            act, _ = silu_parts(total)
            if kind < 2:
                act = act * lax.rsqrt(jnp.sum(act * act, axis=-1, keepdims=True) + norm_epsilon)
            if kind == 0:
                act = act * HEAD ** (-0.5)
            parts.append(act)
        beta = beta_all[:, head : head + 1]
        for part in range(rows // CHUNK):
            here = slice(part * CHUNK, (part + 1) * CHUNK)
            query, key, value = (p[here] for p in parts)
            query_low, key_low = query.astype(bf16), key.astype(bf16)
            b = beta[here]
            stacked = jnp.concatenate([(b * key).astype(bf16), (b * value).astype(bf16)], axis=1)
            strict = jnp.where(row > col, b * mm_nt(key_low, key_low), 0.0)
            scores = jnp.where(row >= col, mm_nt(query_low, key_low), 0.0).astype(bf16)
            work.append((head, part, query_low, key_low, stacked, scores, strict))
    inverses = unit_lower_inverses([item[-1] for item in work], row, col)
    solved_all = {}
    for (head, part, query_low, key_low, stacked, scores, _), inverse in zip(work, inverses):
        inv_ref[head, part] = inverse
        solved_all[part, head] = (query_low, key_low, scores, mm(inverse, stacked))
    states = [state[head] for head in range(heads)]
    for part in range(rows // CHUNK):
        here = slice(part * CHUNK, (part + 1) * CHUNK)
        enters = [enter.astype(bf16) for enter in states]
        items = [solved_all[part, head] for head in range(heads)]
        freshes = [
            (solved[:, HEAD:] - mm(solved[:, :HEAD].astype(bf16), enter)).astype(bf16)
            for (_, _, _, solved), enter in zip(items, enters)
        ]
        states = [old + mm_tn(key_low, fresh) for old, (_, key_low, _, _), fresh in zip(states, items, freshes)]
        for head in range(heads):
            lanes = slice(head * HEAD, (head + 1) * HEAD)
            query_low, _, scores, _ = items[head]
            state_ref[head, part] = enters[head]
            mixed = mm(query_low, enters[head]) + mm(scores, freshes[head])
            mixed_ref[here, lanes] = mixed
            gate = pre_ref[here, 3 * width + head * HEAD : 3 * width + (head + 1) * HEAD].astype(f32)
            gate_act, _ = silu_parts(gate)
            normed = mixed * lax.rsqrt(jnp.mean(mixed * mixed, axis=-1, keepdims=True) + head_epsilon)
            z_ref[here, lanes] = (normed * gain_ref[...] * gate_act).astype(bf16)
    for head in range(heads):
        state[head] = states[head]


def mixer_forward(pre, beta, taps, gain, heads):
    length, total = pre.shape
    width = heads * HEAD
    steps, parts = length // STEP, STEP // CHUNK
    return pl.pallas_call(
        functools.partial(forward_kernel, heads),
        grid=(steps,),
        in_specs=[
            pl.BlockSpec((STEP, total), lambda i: (i, 0)),
            pl.BlockSpec((STEP, BETA_PAD), lambda i: (i, 0)),
            pl.BlockSpec((3 * TAPS, width), lambda i: (0, 0)),
            pl.BlockSpec((1, HEAD), lambda i: (0, 0)),
        ],
        out_specs=[
            pl.BlockSpec((STEP, width), lambda i: (i, 0)),
            pl.BlockSpec((STEP, 3 * width), lambda i: (i, 0)),
            pl.BlockSpec((STEP, width), lambda i: (i, 0)),
            pl.BlockSpec((heads, parts, CHUNK, CHUNK), lambda i: (0, i, 0, 0)),
            pl.BlockSpec((heads, parts, HEAD, HEAD), lambda i: (0, i, 0, 0)),
        ],
        out_shape=[
            jax.ShapeDtypeStruct((length, width), bf16),
            jax.ShapeDtypeStruct((length, 3 * width), f32),
            jax.ShapeDtypeStruct((length, width), f32),
            jax.ShapeDtypeStruct((heads, steps * parts, CHUNK, CHUNK), bf16),
            jax.ShapeDtypeStruct((heads, steps * parts, HEAD, HEAD), bf16),
        ],
        scratch_shapes=[
            pltpu.VMEM((STEP + 8, 3 * width), f32),
            pltpu.VMEM((heads, HEAD, HEAD), f32),
        ],
        compiler_params=pltpu.CompilerParams(
            dimension_semantics=("arbitrary",), vmem_limit_bytes=VMEM_LIMIT
        ),
        cost_estimate=pl.CostEstimate(
            flops=2 * length * width * HEAD * 60, bytes_accessed=length * (total * 4 + width * 24), transcendentals=length * width * 8
        ),
    )(pre, beta, taps, gain)


def backward_kernel(
    heads,
    pre_ref,
    beta_ref,
    source_ref,
    conv_ref,
    mixed_ref,
    dz_ref,
    inv_ref,
    state_ref,
    taps_ref,
    gain_ref,
    dpre_ref,
    dbeta_ref,
    dsource_ref,
    dtaps_ref,
    dgain_ref,
    later,
    dstate,
):
    step = pl.program_id(0)
    width = heads * HEAD
    rows = pre_ref.shape[0]
    count = rows // CHUNK

    @pl.when(step == 0)
    def _():
        later[rows : rows + 8, :] = jnp.zeros((8, 3 * width), f32)
        dstate[...] = jnp.zeros_like(dstate)
        dtaps_ref[...] = jnp.zeros_like(dtaps_ref)
        dgain_ref[...] = jnp.zeros_like(dgain_ref)
        dsource_ref[...] = jnp.zeros_like(dsource_ref)

    @pl.when(step > 0)
    def _():
        later[rows : rows + 8, :] = later[0:8, :]

    row, col = chunk_indices()
    beta_all = jax.nn.sigmoid(beta_ref[...])
    beta_lane = lax.broadcasted_iota(jnp.int32, (CHUNK, BETA_PAD), 1)
    dbeta_all = [jnp.zeros((CHUNK, BETA_PAD), f32) for _ in range(count)]
    dgain = jnp.zeros((1, HEAD), f32)
    gain = gain_ref[...]
    every = [(part, head) for part in reversed(range(count)) for head in range(heads)]

    def of(ref, kind, at):
        part, head = at
        lanes = slice(kind * width + head * HEAD, kind * width + (head + 1) * HEAD)
        return ref[part * CHUNK : (part + 1) * CHUNK, lanes].astype(f32)

    betas = {(part, head): beta_all[part * CHUNK : (part + 1) * CHUNK, head : head + 1] for part, head in every}
    unit_queries, keys, query_lows, key_lows, scales, stacks = {}, {}, {}, {}, {}, {}
    for at in every:
        acts = [silu_parts(of(conv_ref, kind, at))[0] for kind in range(3)]
        scales[at] = [lax.rsqrt(jnp.sum(act * act, axis=-1, keepdims=True) + norm_epsilon) for act in acts[:2]]
        unit_queries[at], keys[at] = acts[0] * scales[at][0], acts[1] * scales[at][1]
        query_lows[at] = (unit_queries[at] * HEAD ** (-0.5)).astype(bf16)
        key_lows[at] = keys[at].astype(bf16)
        stacks[at] = jnp.concatenate([(betas[at] * keys[at]).astype(bf16), (betas[at] * acts[2]).astype(bf16)], axis=1)
    solved = {at: mm(inv_ref[at[1], at[0]], stacks[at]) for at in every}
    scores = {at: jnp.where(row >= col, mm_nt(query_lows[at], key_lows[at]), 0.0).astype(bf16) for at in every}
    weights = {at: solved[at][:, :HEAD].astype(bf16) for at in every}
    outs = {}
    for at in every:
        part, head = at
        here = slice(part * CHUNK, (part + 1) * CHUNK)
        gate = of(pre_ref, 3, at)
        gate_act, gate_sig = silu_parts(gate)
        mixed, dz = of(mixed_ref, 0, at), of(dz_ref, 0, at)
        root = lax.rsqrt(jnp.mean(mixed * mixed, axis=-1, keepdims=True) + head_epsilon)
        normed = mixed * root
        dgate = dz * normed * gain * (gate_sig * (1.0 + gate * (1.0 - gate_sig)))
        dpre_ref[here, 3 * width + head * HEAD : 3 * width + (head + 1) * HEAD] = dgate.astype(bf16)
        dgained = dz * gate_act
        dgain = dgain + jnp.sum(dgained * normed, axis=0, keepdims=True)
        dnormed = dgained * gain
        dmixed = root * (dnormed - normed * jnp.mean(dnormed * normed, axis=-1, keepdims=True))
        outs[at] = dmixed.astype(bf16)
    enters = {(part, head): state_ref[head, part] for part, head in every}
    fresh = {at: (solved[at][:, HEAD:] - mm(weights[at], enters[at])).astype(bf16) for at in every}
    within = {at: mm_tn(scores[at], outs[at]) for at in every}
    across = {at: mm_tn(query_lows[at], outs[at]) for at in every}
    leavings, dfresh = {}, {}
    states = [dstate[head] for head in range(heads)]
    for part in reversed(range(count)):
        for head in range(heads):
            leavings[part, head] = states[head].astype(bf16)
        for head in range(heads):
            at = (part, head)
            dfresh[at] = (within[at] + mm(key_lows[at], leavings[at])).astype(bf16)
        for head in range(heads):
            at = (part, head)
            states[head] = states[head] + across[at] - mm_tn(weights[at], dfresh[at])
    for head in range(heads):
        dstate[head] = states[head]
    dscores = {at: jnp.where(row >= col, mm_nt(outs[at], fresh[at]), 0.0).astype(bf16) for at in every}
    dweights = {at: (-mm_nt(dfresh[at], enters[at])).astype(bf16) for at in every}
    dxys = {
        at: mm_tn(inv_ref[at[1], at[0]], jnp.concatenate([dweights[at], dfresh[at]], axis=1)) for at in every
    }
    dqueries = {at: mm_nt(outs[at], enters[at]) + mm(dscores[at], key_lows[at]) for at in every}
    dkeys = {at: mm_tn(dscores[at], query_lows[at]) + mm_nt(fresh[at], leavings[at]) for at in every}
    dsystems = {
        at: jnp.where(row > col, -mm_nt(dxys[at].astype(bf16), solved[at].astype(bf16)), 0.0) for at in every
    }
    dsystem_lows = {at: dsystems[at].astype(bf16) for at in every}
    firsts = {at: mm(dsystem_lows[at], key_lows[at]) for at in every}
    seconds = {at: mm_tn(dsystem_lows[at], stacks[at][:, :HEAD]) for at in every}
    grams = {at: mm_nt(key_lows[at], key_lows[at]) for at in every}
    for at in every:
        part, head = at
        beta, dx, dy, key = betas[at], dxys[at][:, :HEAD], dxys[at][:, HEAD:], keys[at]
        dkey = dkeys[at] + beta * (firsts[at] + dx) + seconds[at]
        convs = [of(conv_ref, kind, at) for kind in range(3)]
        sigs = [jax.nn.sigmoid(conv) for conv in convs]
        dbeta = jnp.sum(dsystems[at] * grams[at] + dx * key + dy * (convs[2] * sigs[2]), axis=-1, keepdims=True)
        dbeta = dbeta * beta * (1.0 - beta)
        dbeta_all[part] = jnp.where(beta_lane == head, dbeta, dbeta_all[part])
        unit_query, dquery = unit_queries[at], dqueries[at] * HEAD ** (-0.5)
        dquery = scales[at][0] * (dquery - unit_query * jnp.sum(unit_query * dquery, axis=-1, keepdims=True))
        dkey = scales[at][1] * (dkey - key * jnp.sum(key * dkey, axis=-1, keepdims=True))
        for kind, grad in enumerate((dquery, dkey, beta * dy)):
            dconv = grad * (sigs[kind] * (1.0 + convs[kind] * (1.0 - sigs[kind])))
            lanes = slice(kind * width + head * HEAD, kind * width + (head + 1) * HEAD)
            later[part * CHUNK : (part + 1) * CHUNK, lanes] = dconv
    for part in range(count):
        here = slice(part * CHUNK, (part + 1) * CHUNK)
        dbeta_low = dbeta_all[part].astype(bf16)
        dbeta_ref[here, :] = dbeta_low
        dsource_ref[...] += mm_tn(dbeta_low, source_ref[here, :])
    dgain_ref[...] += dgain
    for kind in range(3):
        for head in range(heads):
            lanes = slice(kind * width + head * HEAD, kind * width + (head + 1) * HEAD)
            source = pre_ref[:, lanes].astype(f32)
            total = jnp.zeros((rows, HEAD), f32)
            for tap in range(TAPS):
                at = kind * TAPS + tap
                shifted = later[TAPS - 1 - tap : TAPS - 1 - tap + rows, lanes]
                total = total + taps_ref[at : at + 1, head * HEAD : (head + 1) * HEAD] * shifted
                dtaps_ref[at : at + 1, head * HEAD : (head + 1) * HEAD] += jnp.sum(
                    source * shifted, axis=0, keepdims=True
                )
            dpre_ref[:, lanes] = total.astype(bf16)


def mixer_backward(pre, beta, source, conv, mixed, dz, inverse, states, taps, gain, heads):
    length, total = pre.shape
    model = source.shape[1]
    width = heads * HEAD
    steps, parts = length // STEP, STEP // CHUNK
    return pl.pallas_call(
        functools.partial(backward_kernel, heads),
        grid=(steps,),
        in_specs=[
            pl.BlockSpec((STEP, total), lambda i: (steps - 1 - i, 0)),
            pl.BlockSpec((STEP, BETA_PAD), lambda i: (steps - 1 - i, 0)),
            pl.BlockSpec((STEP, model), lambda i: (steps - 1 - i, 0)),
            pl.BlockSpec((STEP, 3 * width), lambda i: (steps - 1 - i, 0)),
            pl.BlockSpec((STEP, width), lambda i: (steps - 1 - i, 0)),
            pl.BlockSpec((STEP, width), lambda i: (steps - 1 - i, 0)),
            pl.BlockSpec((heads, parts, CHUNK, CHUNK), lambda i: (0, steps - 1 - i, 0, 0)),
            pl.BlockSpec((heads, parts, HEAD, HEAD), lambda i: (0, steps - 1 - i, 0, 0)),
            pl.BlockSpec((3 * TAPS, width), lambda i: (0, 0)),
            pl.BlockSpec((1, HEAD), lambda i: (0, 0)),
        ],
        out_specs=[
            pl.BlockSpec((STEP, total), lambda i: (steps - 1 - i, 0)),
            pl.BlockSpec((STEP, BETA_PAD), lambda i: (steps - 1 - i, 0)),
            pl.BlockSpec((BETA_PAD, model), lambda i: (0, 0)),
            pl.BlockSpec((3 * TAPS, width), lambda i: (0, 0)),
            pl.BlockSpec((1, HEAD), lambda i: (0, 0)),
        ],
        out_shape=[
            jax.ShapeDtypeStruct((length, total), bf16),
            jax.ShapeDtypeStruct((length, BETA_PAD), bf16),
            jax.ShapeDtypeStruct((BETA_PAD, model), f32),
            jax.ShapeDtypeStruct((3 * TAPS, width), f32),
            jax.ShapeDtypeStruct((1, HEAD), f32),
        ],
        scratch_shapes=[
            pltpu.VMEM((STEP + 8, 3 * width), f32),
            pltpu.VMEM((heads, HEAD, HEAD), f32),
        ],
        compiler_params=pltpu.CompilerParams(
            dimension_semantics=("arbitrary",), vmem_limit_bytes=VMEM_LIMIT
        ),
        cost_estimate=pl.CostEstimate(
            flops=1_000_000, bytes_accessed=1_000_000, transcendentals=0
        ),
    )(pre, beta, source, conv, mixed, dz, inverse, states, taps, gain)


MESH = pl.DeviceIdType.MESH
TILE = 16
BOTH_LAST = 512
LANES = 128
LARGE_LIMIT = 60 * 1024 * 1024


def remote(source, target, send, receive, **where):
    return pltpu.make_async_remote_copy(
        src_ref=source,
        dst_ref=target,
        send_sem=send,
        recv_sem=receive,
        device_id=where,
        device_id_type=MESH,
    )


def when(condition, action):
    pl.when(condition)(action)


def greet(**where):
    pl.semaphore_signal(
        pltpu.get_barrier_semaphore(), inc=1, device_id=where, device_id_type=MESH
    )


def wait_greetings(count):
    pl.semaphore_wait(pltpu.get_barrier_semaphore(), count)


def plane():
    me = lax.axis_index("tensor")
    across = me + 1 - 2 * lax.rem(me, 2)
    along = lax.rem(me + 2, 4)
    return me, across, along


def chip_and_core():
    index = lax.axis_index("dp")
    return index // 2, lax.rem(index, 2)


def greet_line(chips):
    chip, core = chip_and_core()
    greet(dp=chip * 2 + 1 - core)
    when(chip > 0, lambda: greet(dp=(chip - 1) * 2 + core))
    when(chip < chips - 1, lambda: greet(dp=(chip + 1) * 2 + core))
    return 1 + jnp.where(chip > 0, 1, 0) + jnp.where(chip < chips - 1, 1, 0)


class PlaneGather:
    def __init__(self, own, full, send, receive):
        self.own, self.full, self.send, self.receive = own, full, send, receive
        self.me, self.across, self.along = plane()
        self.far = lax.rem(self.across + 2, 4)
        self.rows = own.shape[0]
        self.half = self.rows // 2

    def slot(self, block, half):
        start = pl.multiple_of(block * self.rows + half * self.half, self.half)
        return self.full.at[pl.ds(start, self.half)]

    def mine(self, half):
        return self.own.at[pl.ds(half * self.half, self.half)]

    def out(self, half, kind):
        where = self.across if kind == 0 else self.along
        at = 2 * kind + half
        return remote(
            self.mine(half), self.slot(self.me, half), self.send.at[at], self.receive.at[at], tensor=where
        )

    def arriving(self, half, kind):
        block = self.across if kind == 0 else self.along
        at = 2 * kind + half
        view = self.slot(block, half)
        return remote(view, view, self.send.at[at], self.receive.at[at], tensor=block)

    def passing(self, kind):
        view = self.slot(self.across if kind == 0 else self.along, kind)
        where = self.along if kind == 0 else self.across
        return remote(view, view, self.send.at[4 + kind], self.receive.at[4 + kind], tensor=where)

    def passed(self, kind):
        view = self.slot(self.far, kind)
        where = self.along if kind == 0 else self.across
        return remote(view, view, self.send.at[4 + kind], self.receive.at[4 + kind], tensor=where)

    def start(self, half):
        for kind in (half, 1 - half):
            self.out(half, kind).start()

    def relay(self, kind):
        self.arriving(kind, kind).wait_recv()
        self.passing(kind).start()

    def near(self, kind):
        self.arriving(1 - kind, kind).wait_recv()

    def diagonal(self):
        self.passed(0).wait_recv()
        self.passed(1).wait_recv()

    def finish(self):
        self.near(0)
        self.near(1)
        self.diagonal()
        self.sent()

    def sent(self):
        for kind in (0, 1):
            self.passing(kind).wait_send()
            for half in (0, 1):
                self.out(half, kind).wait_send()


class PlaneScatter:
    def __init__(self, part, first, second, stage, send, receive):
        self.part, self.first, self.second, self.stage = part, first, second, stage
        self.send, self.receive = send, receive
        self.me, self.across, self.along = plane()
        self.far = lax.rem(self.across + 2, 4)
        self.rows = part.shape[0] // 4
        self.half = self.rows // 2

    def start_of(self, block, half):
        return pl.multiple_of(block * self.rows + half * self.half, self.half)

    def view(self, block, half):
        return self.part.at[pl.ds(self.start_of(block, half), self.half)]

    def out(self, kind, order):
        where = self.across if kind == 0 else self.along
        at = 2 * kind + order
        return remote(
            self.view(self.far if order == 0 else where, kind),
            self.first.at[at],
            self.send.at[at],
            self.receive.at[at],
            tensor=where,
        )

    def over(self, kind):
        where = self.along if kind == 0 else self.across
        return remote(
            self.stage.at[kind], self.second.at[kind], self.send.at[4 + kind], self.receive.at[4 + kind], tensor=where
        )

    def start_far(self):
        for kind in (0, 1):
            self.out(kind, 0).start()

    def start_near(self, kind):
        self.out(kind, 1).start()

    def relay(self, kind):
        self.out(kind, 0).wait_recv()
        block = self.along if kind == 0 else self.across
        start = self.start_of(block, kind)

        def add(index, carry):
            at = pl.multiple_of(index * TILE, TILE)
            mine = self.part[pl.ds(pl.multiple_of(start + at, TILE), TILE), :].astype(f32)
            other = self.first[2 * kind, pl.ds(at, TILE), :].astype(f32)
            self.stage[kind, pl.ds(at, TILE), :] = (mine + other).astype(bf16)
            return carry

        lax.fori_loop(0, self.half // TILE, add, 0)
        self.over(kind).start()

    def ready(self, kind):
        self.out(kind, 1).wait_recv()
        self.over(kind).wait_recv()

    def tile(self, kind, at):
        start = self.start_of(self.me, kind)
        mine = self.part[pl.ds(pl.multiple_of(start + at, TILE), TILE), :].astype(f32)
        near = self.first[2 * kind + 1, pl.ds(at, TILE), :].astype(f32)
        return mine + near + self.second[kind, pl.ds(at, TILE), :].astype(f32)

    def finish(self):
        for kind in (0, 1):
            for order in (0, 1):
                self.out(kind, order).wait_send()
            self.over(kind).wait_send()


def plane_scatter_scratch(rows, columns):
    half = rows // 2
    return [
        pltpu.VMEM((4, half, columns), bf16),
        pltpu.VMEM((2, half, columns), bf16),
        pltpu.VMEM((2, half, columns), bf16),
        pltpu.SemaphoreType.DMA((6,)),
        pltpu.SemaphoreType.DMA((6,)),
    ]


def pieces_of(arrays, size):
    found = []
    for index, array in enumerate(arrays):
        rows, columns = array.shape[-2:]
        count = max(1, min(rows // 64, round(rows * columns / size)))
        while rows % count or (rows // count) % 16:
            count -= 1
        for piece in range(count):
            found.append((index, piece * (rows // count), rows // count))
    return found


PIECE = 64 * 2176


class LineGather:
    def __init__(self, chips, owns, fulls, sems):
        self.chips, self.owns, self.fulls = chips, owns, fulls
        self.pieces = pieces_of(owns, PIECE)
        self.right_send, self.right_receive, self.left_send, self.left_receive = sems[:4]
        self.core_send, self.core_receive, self.local = sems[4:]
        self.chip, self.core = chip_and_core()

    @staticmethod
    def scratch(chips, pieces, arrays):
        return [pltpu.SemaphoreType.DMA((chips, pieces)) for _ in range(6)] + [pltpu.SemaphoreType.DMA((arrays,))]

    def slot(self, piece, chip, core):
        index, start, rows = self.pieces[piece]
        return self.fulls[index].at[chip * 2 + core, pl.ds(start, rows)]

    def source(self, piece, away):
        index, start, rows = self.pieces[piece]
        return self.owns[index].at[pl.ds(start, rows)]

    def right(self, piece, away, chip):
        slot = self.slot(piece, chip, self.core)
        source = self.source(piece, 0) if away == 0 else slot
        to = (self.chip + 1) * 2 + self.core
        return remote(source, slot, self.right_send.at[away, piece], self.right_receive.at[away, piece], dp=to)

    def left(self, piece, away, chip):
        slot = self.slot(piece, chip, self.core)
        source = self.source(piece, 0) if away == 0 else slot
        to = (self.chip - 1) * 2 + self.core
        return remote(source, slot, self.left_send.at[away, piece], self.left_receive.at[away, piece], dp=to)

    def trade(self, piece, chip, own):
        slot = self.slot(piece, chip, self.core)
        source = self.source(piece, 0) if own else slot
        to = self.chip * 2 + 1 - self.core
        return remote(source, slot, self.core_send.at[chip, piece], self.core_receive.at[chip, piece], dp=to)

    def keep(self, index):
        return pltpu.make_async_copy(
            self.owns[index], self.fulls[index].at[self.chip * 2 + self.core], self.local.at[index]
        )

    def start(self):
        for piece in range(len(self.pieces)):
            when(self.chip < self.chips - 1, lambda: self.right(piece, 0, self.chip).start())
            when(self.chip > 0, lambda: self.left(piece, 0, self.chip).start())
        for piece in range(len(self.pieces)):
            self.trade(piece, self.chip, True).start()
        for index in range(len(self.owns)):
            self.keep(index).start()

    def step(self, away):
        for piece in range(len(self.pieces)):

            def from_left():
                chip = self.chip - away
                self.right(piece, away - 1, chip).wait_recv()
                if away < self.chips - 1:
                    when(self.chip < self.chips - 1, lambda: self.right(piece, away, chip).start())
                self.trade(piece, chip, False).start()

            def from_right():
                chip = self.chip + away
                self.left(piece, away - 1, chip).wait_recv()
                if away < self.chips - 1:
                    when(self.chip > 0, lambda: self.left(piece, away, chip).start())
                self.trade(piece, chip, False).start()

            when(self.chip >= away, from_left)
            when(self.chip + away < self.chips, from_right)

    def finish(self):
        for index in range(len(self.owns)):
            self.keep(index).wait()
        for piece in range(len(self.pieces)):
            for away in range(self.chips - 1):
                when(
                    (self.chip < self.chips - 1) & (self.chip >= away),
                    lambda: self.right(piece, away, self.chip - away).wait_send(),
                )
                when(
                    (self.chip > 0) & (self.chip + away < self.chips),
                    lambda: self.left(piece, away, self.chip + away).wait_send(),
                )
            for chip in range(self.chips):
                trade = remote(
                    self.slot(piece, chip, self.core),
                    self.slot(piece, chip, 1 - self.core),
                    self.core_send.at[chip, piece],
                    self.core_receive.at[chip, piece],
                    dp=self.chip * 2 + 1 - self.core,
                )
                trade.wait_send()
                trade.wait_recv()


def first_gather_kernel(chips, *refs):
    w_query, w_key, w_value, w_gate_out, w_beta, w_output, inputs, cotangent, mask, gain = refs[:10]
    w_gate, w_up, w_down = refs[10:13]
    inner_full, output_full, beta_full, normed_full, grad_full, gate_up, down, grad = refs[13:21]
    inner, output, normed, gate_wide, up_wide, down_wide = refs[21:27]
    sems = refs[27:]
    width, hidden = w_query.shape[1], w_gate.shape[1]
    line = LineGather(chips, [inner, output, w_beta], [inner_full, output_full, beta_full], sems[:7])
    rows = [PlaneGather(normed, normed_full, *sems[7:9]), PlaneGather(grad, grad_full, *sems[9:11])]
    local = sems[11]
    keeps = [
        pltpu.make_async_copy(
            own, full.at[pl.ds(pl.multiple_of(each.me * each.rows, each.rows), each.rows)], local.at[at]
        )
        for at, (own, full, each) in enumerate(((normed, normed_full, rows[0]), (grad, grad_full, rows[1])))
    ]
    loads = [
        pltpu.make_async_copy(source, target, local.at[2 + at])
        for at, (source, target) in enumerate(((w_gate, gate_wide), (w_up, up_wide), (w_down, down_wide)))
    ]
    greetings = greet_line(chips)
    greet(tensor=rows[0].across)
    greet(tensor=rows[0].along)
    for kind, weight in enumerate((w_query, w_key, w_value, w_gate_out)):
        inner[:, kind * width : (kind + 1) * width] = weight[...].astype(bf16)
    output[...] = jnp.transpose(w_output[...]).astype(bf16)
    wait_greetings(2 + greetings)
    line.start()
    for load in loads:
        load.start()

    def norm(index, carry):
        here = pl.ds(pl.multiple_of(index * TILE, TILE), TILE)
        value = inputs[here, :].astype(f32)
        scale = lax.rsqrt(jnp.mean(value * value, axis=-1, keepdims=True) + norm_epsilon)
        normed[here, :] = (value * scale * gain[...]).astype(bf16)
        grad[here, :] = (cotangent[here, :].astype(f32) * mask[here, :]).astype(bf16)
        return carry

    lax.fori_loop(0, inputs.shape[0] // TILE, norm, 0)
    for each in rows:
        each.start(0)
        each.start(1)
    for keep in keeps:
        keep.start()
    for load in loads:
        load.wait()
    for kind, wide in enumerate((gate_wide, up_wide)):
        for tile in range(hidden // LANES):
            to = (2 * tile + kind) * LANES
            gate_up[:, to : to + LANES] = wide[:, tile * LANES : (tile + 1) * LANES].astype(bf16)
    down[...] = jnp.transpose(down_wide[...]).astype(bf16)
    rows[0].relay(0)
    rows[0].relay(1)
    line.step(1)
    rows[1].relay(0)
    rows[1].relay(1)
    for away in range(2, chips):
        line.step(away)
    for each in rows:
        each.finish()
    for keep in keeps:
        keep.wait()
    line.finish()


def ffn_kernel(normed, weight, middle, slopes):
    def block(index, carry):
        here = pl.ds(pl.multiple_of(index * 512, 512), 512)
        both = mm(normed[here, :], weight[...])
        gate, up_part = both[:, :LANES], both[:, LANES:]
        act, sig = silu_parts(gate)
        middle[here, :] = (act * up_part).astype(bf16)
        slopes[here, :LANES] = (up_part * sig * (1.0 + gate * (1.0 - sig))).astype(bf16)
        slopes[here, LANES:] = act.astype(bf16)
        return carry

    lax.fori_loop(0, normed.shape[0] // 512, block, 0, unroll=True)


def ffn(normed, gate_up):
    length, model = normed.shape
    hidden = gate_up.shape[1] // 2
    return pl.pallas_call(
        ffn_kernel,
        grid=(hidden // LANES,),
        in_specs=[
            pl.BlockSpec((length, model), lambda i: (0, 0)),
            pl.BlockSpec((model, 2 * LANES), lambda i: (0, i)),
        ],
        out_specs=[
            pl.BlockSpec((length, LANES), lambda i: (0, i)),
            pl.BlockSpec((length, 2 * LANES), lambda i: (0, i)),
        ],
        out_shape=[
            jax.ShapeDtypeStruct((length, hidden), bf16),
            jax.ShapeDtypeStruct((length, 2 * hidden), bf16),
        ],
        compiler_params=pltpu.CompilerParams(
            dimension_semantics=("arbitrary",), vmem_limit_bytes=VMEM_LIMIT
        ),
        cost_estimate=pl.CostEstimate(
            flops=4 * length * model * hidden, bytes_accessed=2 * (length * model + 2 * model * hidden), transcendentals=length * hidden
        ),
    )(normed, gate_up)


def ffn_backward_kernel(grad, weight, slopes, low, high):
    split = low.shape[1] // LANES
    grad_middle = mm(grad[...], weight[...])
    for tile in range(weight.shape[1] // LANES):
        part = grad_middle[:, tile * LANES : (tile + 1) * LANES]
        for kind in range(2):
            at = 2 * tile + kind
            target, to = (low, at) if at < split else (high, at - split)
            slope = slopes[:, at * LANES : (at + 1) * LANES].astype(f32)
            target[:, to * LANES : (to + 1) * LANES] = (part * slope).astype(bf16)


def ffn_backward(grad, down, slopes):
    length, model = grad.shape
    hidden = down.shape[1]
    block = 512
    widths = (2 * hidden - BOTH_LAST, BOTH_LAST)
    return pl.pallas_call(
        ffn_backward_kernel,
        grid=(length // block,),
        in_specs=[
            pl.BlockSpec((block, model), lambda i: (i, 0)),
            pl.BlockSpec((model, hidden), lambda i: (0, 0)),
            pl.BlockSpec((block, 2 * hidden), lambda i: (i, 0)),
        ],
        out_specs=[pl.BlockSpec((block, width), lambda i: (i, 0)) for width in widths],
        out_shape=[jax.ShapeDtypeStruct((length, width), bf16) for width in widths],
        compiler_params=pltpu.CompilerParams(
            dimension_semantics=("arbitrary",), vmem_limit_bytes=VMEM_LIMIT
        ),
        cost_estimate=pl.CostEstimate(
            flops=2 * length * model * hidden, bytes_accessed=2 * (length * model + model * hidden + 4 * length * hidden), transcendentals=0
        ),
    )(grad, down, slopes)


def finish_kernel(count, *refs):
    sources, targets, held, sems = refs[:count], refs[count : 2 * count], refs[2 * count : 3 * count], refs[-1]
    kept, outs = held[:3], refs[3 * count : 3 * count + 3]
    loads = [
        pltpu.make_async_copy(source, here, sems.at[0, at]) for at, (source, here) in enumerate(zip(sources, held))
    ]
    stores = [
        pltpu.make_async_copy(here, target, sems.at[1, at])
        for at, (here, target) in enumerate(zip((*outs, *held[3:]), targets))
    ]
    for load in loads:
        load.start()
    low, high, down = kept
    gate_out, up_out, down_out = outs
    split = low.shape[1] // LANES
    for load in loads[:3]:
        load.wait()
    for tile in range(gate_out.shape[1] // LANES):
        for kind, target in enumerate((gate_out, up_out)):
            at = 2 * tile + kind
            source, start = (low, at) if at < split else (high, at - split)
            target[:, tile * LANES : (tile + 1) * LANES] = source[:, start * LANES : (start + 1) * LANES].astype(f32)
    stores[0].start()
    stores[1].start()
    for load, store in zip(loads[3:], stores[3:]):
        load.wait()
        store.start()
    for tile in range(gate_out.shape[1] // LANES):
        lanes = slice(tile * LANES, (tile + 1) * LANES)
        down_out[lanes, :] = jnp.transpose(down[:, lanes].astype(f32))
    stores[2].start()
    for store in stores:
        store.wait()


def finish(low, high, down, arrays):
    slab, hidden = down.shape
    sources = [low, high, down, *arrays]
    count = len(sources)
    outs = [
        jax.ShapeDtypeStruct((slab, hidden), f32),
        jax.ShapeDtypeStruct((slab, hidden), f32),
        jax.ShapeDtypeStruct((hidden, slab), f32),
    ]
    return pl.pallas_call(
        functools.partial(finish_kernel, count),
        in_specs=anywhere(count),
        out_specs=anywhere(count),
        out_shape=outs + [jax.ShapeDtypeStruct(array.shape, array.dtype) for array in arrays],
        scratch_shapes=[pltpu.VMEM(array.shape, array.dtype) for array in sources]
        + [pltpu.VMEM(out.shape, f32) for out in outs]
        + [pltpu.SemaphoreType.DMA((2, count))],
        compiler_params=pltpu.CompilerParams(vmem_limit_bytes=VMEM_LIMIT),
        cost_estimate=pl.CostEstimate(flops=0, bytes_accessed=40 * slab * hidden, transcendentals=0),
    )(*sources)


def plain_ffn(normed, gate_up):
    gate, up_part = jnp.split(jnp.dot(normed, gate_up, preferred_element_type=f32), 2, axis=1)
    act, sig = silu_parts(gate)
    slopes = jnp.concatenate([up_part * sig * (1.0 + gate * (1.0 - sig)), act], axis=1)
    return (act * up_part).astype(bf16), slopes.astype(bf16)


def plain_ffn_backward(grad, down, slopes):
    grad_middle = jnp.dot(grad, down, preferred_element_type=f32)
    both = (jnp.concatenate([grad_middle, grad_middle], axis=1) * slopes.astype(f32)).astype(bf16)
    return both[:, :-BOTH_LAST], both[:, -BOTH_LAST:]


def plain_finish(low, high, down, arrays):
    gate, up_part = jnp.split(jnp.concatenate([low.astype(f32), high], axis=1), 2, axis=1)
    return gate, up_part, down.astype(f32).T, *arrays


def anywhere(count):
    return [pl.BlockSpec(memory_space=pl.ANY)] * count


def in_vmem(count):
    return [pl.BlockSpec(memory_space=pltpu.VMEM)] * count


def first_gather(w_query, w_key, w_value, w_gate_out, w_beta, w_output, inputs, cotangent, mask, gain, w_gate, w_up, w_down):
    shards = lax.axis_size("dp")
    rows, model = inputs.shape
    slab, width = w_query.shape
    hidden = w_gate.shape[1]
    inner = jax.ShapeDtypeStruct((slab, 4 * width), bf16)
    output = jax.ShapeDtypeStruct((slab, width), bf16)
    pieces = len(pieces_of([inner, output, w_beta], PIECE))
    return pl.pallas_call(
        functools.partial(first_gather_kernel, shards // 2),
        in_specs=in_vmem(10) + anywhere(3),
        out_specs=anywhere(5) + in_vmem(3),
        out_shape=[
            jax.ShapeDtypeStruct((shards, *inner.shape), bf16),
            jax.ShapeDtypeStruct((shards, *output.shape), bf16),
            jax.ShapeDtypeStruct((shards, *w_beta.shape), bf16),
            jax.ShapeDtypeStruct((4 * rows, model), bf16),
            jax.ShapeDtypeStruct((4 * rows, model), bf16),
            jax.ShapeDtypeStruct((slab, 2 * hidden), bf16),
            jax.ShapeDtypeStruct((slab, hidden), bf16),
            jax.ShapeDtypeStruct((rows, model), bf16),
        ],
        scratch_shapes=[
            pltpu.VMEM(inner.shape, bf16),
            pltpu.VMEM(output.shape, bf16),
            pltpu.VMEM((rows, model), bf16),
            pltpu.VMEM((slab, hidden), f32),
            pltpu.VMEM((slab, hidden), f32),
            pltpu.VMEM((hidden, slab), f32),
        ]
        + LineGather.scratch(shards // 2, pieces, 3)
        + [pltpu.SemaphoreType.DMA((6,)) for _ in range(4)]
        + [pltpu.SemaphoreType.DMA((5,))],
        compiler_params=pltpu.CompilerParams(
            collective_id=1, has_side_effects=True, vmem_limit_bytes=VMEM_LIMIT
        ),
        cost_estimate=pl.CostEstimate(flops=80_000_000_000, bytes_accessed=20_000_000, transcendentals=0),
    )(w_query, w_key, w_value, w_gate_out, w_beta, w_output, inputs, cotangent, mask, gain, w_gate, w_up, w_down)


def branch_kernel(z, weight, inputs, gain, resid, full, part, first, second, stage, low, s_send, s_recv, g_send, g_recv, local):
    scatter = PlaneScatter(part, first, second, stage, s_send, s_recv)
    gather = PlaneGather(low, full, g_send, g_recv)
    rows = scatter.rows
    slab = weight.shape[1]
    greet(tensor=scatter.across)
    greet(tensor=scatter.along)

    def compute(block):
        here = pl.ds(scatter.start_of(block, 0), rows)

        def column(index, carry):
            part[here, pl.ds(pl.multiple_of(index * slab, slab), slab)] = mm_nt(z[here, :], weight[index]).astype(bf16)
            return carry

        lax.fori_loop(0, weight.shape[0], column, 0)

    compute(scatter.far)
    wait_greetings(2)
    scatter.start_far()
    compute(scatter.across)
    scatter.start_near(0)
    compute(scatter.along)
    scatter.start_near(1)
    compute(scatter.me)
    scatter.relay(0)
    scatter.relay(1)
    for half in (0, 1):
        scatter.ready(half)

        def norm(index, carry):
            at = pl.multiple_of(index * TILE, TILE)
            here = pl.ds(pl.multiple_of(half * scatter.half + at, TILE), TILE)
            value = inputs[here, :].astype(f32) + scatter.tile(half, at)
            resid[here, :] = value
            scale = lax.rsqrt(jnp.mean(value * value, axis=-1, keepdims=True) + norm_epsilon)
            low[here, :] = (value * scale * gain[...]).astype(bf16)
            return carry

        lax.fori_loop(0, scatter.half // TILE, norm, 0)
        gather.start(half)
    keep = pltpu.make_async_copy(low, full.at[pl.ds(pl.multiple_of(gather.me * rows, rows), rows)], local.at[0])
    keep.start()
    gather.relay(0)
    gather.relay(1)
    scatter.finish()
    gather.finish()
    keep.wait()


def branch_and_norm(z, weight, inputs, gain):
    rows, model = inputs.shape
    return pl.pallas_call(
        branch_kernel,
        in_specs=in_vmem(4),
        out_specs=in_vmem(1) + anywhere(1),
        out_shape=[
            jax.ShapeDtypeStruct((rows, model), f32),
            jax.ShapeDtypeStruct((4 * rows, model), bf16),
        ],
        scratch_shapes=[pltpu.VMEM((4 * rows, model), bf16)]
        + plane_scatter_scratch(rows, model)[:3]
        + [pltpu.VMEM((rows, model), bf16)]
        + [pltpu.SemaphoreType.DMA((6,)) for _ in range(4)]
        + [pltpu.SemaphoreType.DMA((1,))],
        compiler_params=pltpu.CompilerParams(
            collective_id=2, has_side_effects=True, vmem_limit_bytes=VMEM_LIMIT
        ),
        cost_estimate=pl.CostEstimate(flops=50_000_000_000, bytes_accessed=20_000_000, transcendentals=0),
    )(z, weight, inputs, gain)


def norm_backward(value, grad, gain):
    scale = lax.rsqrt(jnp.mean(value * value, axis=-1, keepdims=True) + norm_epsilon)
    normed = value * scale
    inner = grad * gain
    return scale * (inner - normed * jnp.mean(inner * normed, axis=-1, keepdims=True)), grad * normed


class LineScatter:
    def __init__(self, chips, parts, stages, trades, arrived, sems):
        self.chips, self.parts, self.stages, self.trades, self.arrived = chips, parts, stages, trades, arrived
        self.pieces = pieces_of(parts, PIECE)
        self.right_send, self.right_receive, self.left_send, self.left_receive = sems[:4]
        self.core_send, self.core_receive, self.local = sems[4:]
        self.chip, self.core = chip_and_core()

    @staticmethod
    def scratch(chips, arrays):
        shapes = [array.shape[-2:] for array in arrays]
        pieces = len(pieces_of(arrays, PIECE))
        return (
            [pltpu.VMEM((chips, *shape), bf16) for shape in shapes]
            + [pltpu.VMEM((chips, *shape), bf16) for shape in shapes]
            + [pltpu.VMEM((chips + 1, *shape), bf16) for shape in shapes]
            + [pltpu.SemaphoreType.DMA((chips, pieces)) for _ in range(6)]
            + [pltpu.SemaphoreType.DMA((len(arrays), chips))]
        )

    def order(self):
        order = []
        for step in range(self.chips // 2):
            order += [self.chips - 1 - step, step]
        return order

    def trade(self, piece, dest):
        index, start, rows = self.pieces[piece]
        return remote(
            self.parts[index].at[dest * 2 + 1 - self.core, pl.ds(start, rows)],
            self.trades[index].at[dest, pl.ds(start, rows)],
            self.core_send.at[dest, piece],
            self.core_receive.at[dest, piece],
            dp=self.chip * 2 + 1 - self.core,
        )

    def load(self, index, dest):
        return pltpu.make_async_copy(
            self.parts[index].at[dest * 2 + self.core], self.stages[index].at[dest], self.local.at[index, dest]
        )

    def right(self, piece, dest):
        index, start, rows = self.pieces[piece]
        here = pl.ds(start, rows)
        return remote(
            self.stages[index].at[dest, here],
            self.arrived[index].at[dest, here],
            self.right_send.at[dest, piece],
            self.right_receive.at[dest, piece],
            dp=(self.chip + 1) * 2 + self.core,
        )

    def left_slot(self, dest, chip):
        return jnp.where(dest == chip, self.chips, dest)

    def left(self, piece, dest):
        index, start, rows = self.pieces[piece]
        here = pl.ds(start, rows)
        return remote(
            self.stages[index].at[dest, here],
            self.arrived[index].at[self.left_slot(dest, self.chip - 1), here],
            self.left_send.at[dest, piece],
            self.left_receive.at[dest, piece],
            dp=(self.chip - 1) * 2 + self.core,
        )

    def start(self):
        for dest in self.order():
            for index in range(len(self.parts)):
                self.load(index, dest).start()
            for piece in range(len(self.pieces)):
                self.trade(piece, dest).start()

    def add(self, piece, dest, slots, put=None):
        index, start, rows = self.pieces[piece]

        def tile(at, carry):
            here = pl.ds(pl.multiple_of(start + at * TILE, TILE), TILE)
            total = self.stages[index][dest, here, :].astype(f32) + self.trades[index][dest, here, :].astype(f32)
            for slot in slots:
                total = total + self.arrived[index][slot, here, :].astype(f32)
            if put is None:
                self.stages[index][dest, here, :] = total.astype(bf16)
            else:
                put[index](here, total)
            return carry

        lax.fori_loop(0, rows // TILE, tile, 0)

    def first_of(self, piece):
        return piece == 0 or self.pieces[piece - 1][0] != self.pieces[piece][0]

    def receive(self, piece, dest):
        if self.first_of(piece):
            self.load(self.pieces[piece][0], dest).wait()
        self.trade(piece, dest).wait_recv()

    def step(self, step, ends, turns=(0, 1)):
        to_right, to_left = self.chips - 1 - step, step

        def send_right(piece):
            self.receive(piece, to_right)
            if not ends:
                self.right(piece, to_right).wait_recv()
            self.add(piece, to_right, [] if ends else [to_right])
            self.right(piece, to_right).start()

        def send_left(piece):
            self.receive(piece, to_left)
            if not ends:
                self.left(piece, to_left).wait_recv()
            self.add(piece, to_left, [] if ends else [to_left])
            self.left(piece, to_left).start()

        count = len(self.pieces)
        if ends:
            when(self.chip == 0, lambda: [send_right(piece) for piece in range(count)] and None)
            when(self.chip == self.chips - 1, lambda: [send_left(piece) for piece in range(count)] and None)
            return
        inner_right = (self.chip > 0) & (to_right > self.chip)
        inner_left = (self.chip < self.chips - 1) & (to_left < self.chip)
        low = self.chip < self.chips // 2
        lead = 2
        for at in range(count + lead):
            early, late = at, at - lead
            if 0 in turns and early < count:
                when(low & inner_right, functools.partial(send_right, early))
                when(jnp.logical_not(low) & inner_left, functools.partial(send_left, early))
            if 1 in turns and late >= 0:
                when(low & inner_left, functools.partial(send_left, late))
                when(jnp.logical_not(low) & inner_right, functools.partial(send_right, late))

    def keep(self, outs, pieces):
        me = self.chip
        for piece in pieces:
            self.receive(piece, me)
            when(me > 0, lambda: self.right(piece, me).wait_recv())
            when(me < self.chips - 1, lambda: self.left(piece, me).wait_recv())
            when((me > 0) & (me < self.chips - 1), lambda: self.add(piece, me, [me, self.chips], outs))
            when(me == 0, lambda: self.add(piece, me, [self.chips], outs))
            when(me == self.chips - 1, lambda: self.add(piece, me, [me], outs))

    def finish(self):
        for piece in range(len(self.pieces)):
            for dest in range(self.chips):
                self.trade(piece, dest).wait_send()
                when(dest > self.chip, lambda: self.right(piece, dest).wait_send())
                when(dest < self.chip, lambda: self.left(piece, dest).wait_send())


def resid_kernel(
    chips, slab, low_far, high_far, weight_far, z_far, out_weight_far, resid, grad_out, gain, high_part,
    grad_resid, dgain, dz, output_grad, high_out,
    part, first, second, stage, low, full, total, s_send, s_recv, g_send, g_recv,
    grad_both, weight, z, out_weight, load_sems, *rest
):
    scatter = PlaneScatter(part, first, second, stage, s_send, s_recv)
    gather = PlaneGather(low, full, g_send, g_recv)
    line = LineScatter(chips, [high_part], rest[:1], rest[1:2], rest[2:3], rest[3:])
    rows = scatter.rows
    split = low_far.shape[1]
    slabs = weight.shape[0] // slab
    order = (scatter.far, scatter.along, scatter.across, scatter.me)
    greetings = greet_line(chips)
    greet(tensor=scatter.across)
    greet(tensor=scatter.along)

    def rows_loads(at):
        here = pl.ds(scatter.start_of(order[at], 0), rows)
        return [
            pltpu.make_async_copy(far.at[here], grad_both.at[here, lanes], load_sems.at[slabs + 2 * at + which])
            for which, (far, lanes) in enumerate(
                ((low_far, pl.ds(0, split)), (high_far, pl.ds(split, grad_both.shape[1] - split)))
            )
        ]

    def slab_load(index):
        here = pl.ds(pl.multiple_of(index * slab, slab), slab)
        return pltpu.make_async_copy(weight_far.at[here], weight.at[here], load_sems.at[index])

    late_loads = [
        pltpu.make_async_copy(z_far, z, load_sems.at[slabs + 8]),
        pltpu.make_async_copy(out_weight_far, out_weight, load_sems.at[slabs + 9]),
    ]
    for at in range(4):
        for load in rows_loads(at):
            load.start()
        if at == 1:
            for index in range(slabs):
                slab_load(index).start()
    for load in late_loads:
        load.start()

    def compute(blocks, first):
        start = pl.multiple_of(scatter.start_of(jnp.minimum(order[blocks[0]], order[blocks[1]]), 0), rows)
        here = pl.ds(start, 2 * rows)
        for at in blocks:
            for load in rows_loads(at):
                load.wait()

        def column(index, carry):
            lanes = pl.ds(pl.multiple_of(index * slab, slab), slab)
            if first:
                slab_load(index).wait()
            part[here, lanes] = mm_nt(grad_both[here, :], weight[lanes, :]).astype(bf16)
            return carry

        lax.fori_loop(0, slabs, column, 0)

    compute((0, 1), True)
    wait_greetings(2 + greetings)
    scatter.start_far()
    scatter.start_near(1)
    line.start()
    compute((2, 3), False)
    scatter.start_near(0)
    line.step(0, True)
    dgain[...] = jnp.zeros_like(dgain)
    scatter.relay(0)
    scatter.relay(1)
    for step in range(1, chips - 1):
        line.step(step, True)
    for half in (0, 1):
        scatter.ready(half)

        def norm(index, carry):
            at = pl.multiple_of(index * TILE, TILE)
            here = pl.ds(pl.multiple_of(half * scatter.half + at, TILE), TILE)
            back, gain_part = norm_backward(resid[here, :], scatter.tile(half, at), gain[...])
            value = grad_out[here, :].astype(f32) + back
            grad_resid[here, :] = value
            low[here, :] = value.astype(bf16)
            dgain[...] += jnp.sum(gain_part, axis=0, keepdims=True)
            return carry

        lax.fori_loop(0, scatter.half // TILE, norm, 0)
        gather.start(half)
        if half == 0:
            line.step(0, False, (0,))
    for load in late_loads:
        load.wait()

    def use(block, left, fresh=False):
        here = pl.ds(pl.multiple_of(block * rows, rows), rows)
        dz[here, :] = mm(left[...], out_weight[...]).astype(bf16)

        def column(index, carry):
            lanes = pl.ds(pl.multiple_of(index * slab, slab), slab)
            product = mm_tn(left[:, lanes], z[here, :])
            total[lanes, :] = product if fresh else total[lanes, :] + product
            return carry

        lax.fori_loop(0, slabs, column, 0)

    def block_of(block):
        return full.at[pl.ds(pl.multiple_of(block * rows, rows), rows)]

    gather.relay(0)
    gather.relay(1)
    line.step(0, False, (1,))
    for step in range(1, chips - 1):
        line.step(step, False)
    use(scatter.me, low, True)
    gather.near(0)
    use(scatter.across, block_of(scatter.across))
    gather.near(1)
    use(scatter.along, block_of(scatter.along))

    def put(here, total):
        high_out[here, :] = total

    line.keep([put], range(len(line.pieces)))
    gather.diagonal()
    use(scatter.far, block_of(scatter.far))
    output_grad[...] = total[...].astype(bf16)
    gather.sent()
    scatter.finish()
    line.finish()


def resid_backward(grad_low, grad_high, weight, z, out_weight, resid, grad_out, gain, high_part):
    chips = lax.axis_size("dp") // 2
    rows, model = resid.shape
    width = z.shape[1]
    slab, columns = high_part.shape[1:]
    return pl.pallas_call(
        functools.partial(resid_kernel, chips, 256),
        in_specs=anywhere(5) + in_vmem(3) + anywhere(1),
        out_specs=in_vmem(5),
        out_shape=[
            jax.ShapeDtypeStruct((rows, model), f32),
            jax.ShapeDtypeStruct((1, model), f32),
            jax.ShapeDtypeStruct((4 * rows, width), bf16),
            jax.ShapeDtypeStruct((model, width), bf16),
            jax.ShapeDtypeStruct((slab, columns), f32),
        ],
        scratch_shapes=[pltpu.VMEM((4 * rows, model), bf16)]
        + plane_scatter_scratch(rows, model)[:3]
        + [
            pltpu.VMEM((rows, model), bf16),
            pltpu.VMEM((4 * rows, model), bf16),
            pltpu.VMEM((model, width), f32),
        ]
        + [pltpu.SemaphoreType.DMA((6,)) for _ in range(4)]
        + [
            pltpu.VMEM((4 * rows, weight.shape[1]), bf16),
            pltpu.VMEM(weight.shape, bf16),
            pltpu.VMEM(z.shape, bf16),
            pltpu.VMEM(out_weight.shape, bf16),
            pltpu.SemaphoreType.DMA((model // 256 + 10,)),
        ]
        + LineScatter.scratch(chips, [high_part]),
        compiler_params=pltpu.CompilerParams(
            collective_id=3, has_side_effects=True, vmem_limit_bytes=LARGE_LIMIT
        ),
        cost_estimate=pl.CostEstimate(flops=1_000_000, bytes_accessed=1_000_000, transcendentals=0),
    )(grad_low, grad_high, weight, z, out_weight, resid, grad_out, gain, high_part)


SMALL = 512


def last_kernel(chips, *refs):
    inner_part, output_part, weight, inner, dpre_far, middle_far, inputs_far, grad_resid_far, resid_far = refs[:9]
    mask, first_gain, ffn_dgain, head_dgain, dtaps, dbeta, beta, beta_part = refs[9:17]
    refs = refs[3:]
    query_out, key_out, value_out, gate_out, beta_out, output_out, input_grad, out = refs[14:22]
    first_out, ffn_out, head_out, taps_out = refs[22:26]
    refs = refs[26:]
    line = LineScatter(chips, [inner_part, output_part], refs[:2], refs[2:4], refs[4:6], refs[6:13])
    grad = PlaneScatter(*refs[13:19])
    ffn = PlaneScatter(*refs[19:25])
    turned, small, near, lined, dgain, small_send, small_receive, inner_slabs, down_slabs, slab_sems = refs[25:35]
    dpre, middle, inputs, grad_resid, resid, load_sems = refs[35:41]
    chip, core = line.chip, line.core
    slab = inner_part.shape[1]
    shards = 2 * chips
    sibling = chip * 2 + 1 - core
    greet(tensor=grad.across)
    greet(tensor=grad.along)
    greet(dp=sibling)
    for other in range(1, chips):
        greet(dp=lax.rem(chip + other, chips) * 2 + core)

    def stream(at, source, buffers, kind):
        return pltpu.make_async_copy(source.at[at], buffers.at[lax.rem(at, 2)], slab_sems.at[kind, lax.rem(at, 2)])

    rows = inputs.shape[0]

    def product(left, source, buffers, each, kind, mine, extra=None):
        pair = each.me // 2
        here = pl.ds(pl.multiple_of((pair if mine else 1 - pair) * 2 * rows, 2 * rows), 2 * rows)

        def column(index, carry):
            def following():
                stream(lax.rem(index + 1, shards), source, buffers, kind).start()

            when(index < (shards - 1 if mine else shards), following)
            stream(index, source, buffers, kind).wait()
            total = mm_nt(left[here, :], buffers[lax.rem(index, 2)])
            if extra is not None:
                total = total + mm(extra[0][here, :], extra[1][index])
            each.part[here, pl.ds(pl.multiple_of(index * slab, slab), slab)] = total.astype(bf16)
            return carry

        lax.fori_loop(0, shards, column, 0)

    loads = [
        pltpu.make_async_copy(source, target, load_sems.at[at])
        for at, (source, target) in enumerate(
            (
                (dpre_far, dpre),
                (middle_far, middle),
                (inputs_far, inputs),
                (grad_resid_far, grad_resid),
                (resid_far, resid),
            )
        )
    ]
    wait_greetings(2 + chips)
    line.start()
    for load in loads[:2]:
        load.start()
    stream(0, inner, inner_slabs, 0).start()
    stream(0, weight, down_slabs, 1).start()
    for load in loads[2:]:
        load.start()
    dgain[...] = jnp.zeros_like(dgain)
    small[...] = jnp.zeros_like(small)
    line.step(0, True)
    loads[0].wait()
    product(dpre, inner, inner_slabs, grad, 0, False, (dbeta, beta))
    grad.start_far()
    grad.start_near(1)
    line.step(1, True)
    product(dpre, inner, inner_slabs, grad, 0, True, (dbeta, beta))
    grad.start_near(0)
    line.step(0, False, (0,))
    loads[1].wait()
    product(middle, weight, down_slabs, ffn, 1, False)
    for step in range(2, chips - 1):
        line.step(step, True)
    grad.relay(0)
    grad.relay(1)
    ffn.start_far()
    ffn.start_near(1)
    product(middle, weight, down_slabs, ffn, 1, True)
    ffn.start_near(0)
    line.step(0, False, (1,))
    for step in range(1, chips - 1):
        line.step(step, False)
    for load in loads[2:]:
        load.wait()
    for half in (0, 1):
        grad.ready(half)

        def norm(index, carry):
            at = pl.multiple_of(index * TILE, TILE)
            here = pl.ds(pl.multiple_of(half * grad.half + at, TILE), TILE)
            back, gain_part = norm_backward(inputs[here, :].astype(f32), grad.tile(half, at), first_gain[...])
            input_grad[here, :] = grad_resid[here, :] + back
            dgain[...] += jnp.sum(gain_part, axis=0, keepdims=True)
            return carry

        lax.fori_loop(0, grad.half // TILE, norm, 0)
    model = dgain.shape[1]
    count = model // SMALL
    for row in range(count):
        lanes = slice(row * SMALL, (row + 1) * SMALL)
        small[0, row : row + 1, :] = dgain[:, lanes]
        small[0, count + row : count + row + 1, :] = ffn_dgain[:, lanes]
    small[0, 2 * count : 2 * count + 1, 0:HEAD] = head_dgain[...]
    small[0, 16 : 16 + 3 * TAPS, :] = dtaps[...]
    heads = beta_out.shape[0]
    for head in range(heads):
        for row in range(count):
            at = 32 + head * count + row
            small[0, at : at + 1, :] = beta_part[head : head + 1, row * SMALL : (row + 1) * SMALL]

    def hop(at):
        where = (dict(tensor=grad.across), dict(tensor=grad.along), dict(dp=sibling))[at]
        return remote(small.at[at], near.at[at], small_send.at[at], small_receive.at[at], **where)

    def hopped(at):
        hop(at).wait()
        if at < 2:
            small[at + 1, 0:16, :] = small[at, 0:16, :] + near[at, 0:16, :]
            small[at + 1, 16:, :] = small[at, 16:, :]
        else:
            small[3] = small[2] + near[2]

    def tell(other):
        to = lax.rem(chip + other, chips)
        return remote(
            small.at[3], lined.at[chip], small_send.at[2 + other], small_receive.at[2 + other], dp=to * 2 + core
        )

    def put_inner(here, total):
        width = query_out.shape[1]
        for kind, target in enumerate((query_out, key_out, value_out, gate_out)):
            target[here, :] = total[:, kind * width : (kind + 1) * width]

    def put_output(here, total):
        turned[here, :] = total

    puts = [put_inner, put_output]
    hop(0).start()
    ffn.relay(0)
    ffn.relay(1)
    hopped(0)
    hop(1).start()
    pieces = len(line.pieces)
    line.keep(puts, range(0, pieces - 3))
    hopped(1)
    hop(2).start()
    for half in (0, 1):
        ffn.ready(half)

        def finish_rows(index, carry):
            at = pl.multiple_of(index * TILE, TILE)
            here = pl.ds(pl.multiple_of(half * ffn.half + at, TILE), TILE)
            out[here, :] = ((resid[here, :] + ffn.tile(half, at)) * mask[here, :]).astype(bf16)
            return carry

        lax.fori_loop(0, ffn.half // TILE, finish_rows, 0)
    hopped(2)
    lined[chip] = small[3]
    for other in range(1, chips):
        tell(other).start()
    line.keep(puts, range(pieces - 3, pieces))
    output_out[...] = jnp.transpose(turned[...])
    for other in range(1, chips):
        tell(other).wait()
    total = lined[0]
    for other in range(1, chips):
        total = total + lined[other]
    for row in range(count):
        lanes = slice(row * SMALL, (row + 1) * SMALL)
        first_out[:, lanes] = total[row : row + 1, :]
        ffn_out[:, lanes] = total[count + row : count + row + 1, :]
    head_out[...] = total[2 * count : 2 * count + 1, 0:HEAD]
    summed = small.at[0]
    summed[...] = total
    mine = (chip * 2 + core) * slab
    lanes = pl.ds(pl.multiple_of(lax.rem(mine, SMALL), slab), slab)
    for head in range(heads):
        beta_out[head : head + 1, :] = summed[pl.ds(32 + head * count + mine // SMALL, 1), lanes]
    for kind in range(3):
        taps_out[kind] = total[16 + kind * TAPS : 16 + (kind + 1) * TAPS, :]
    grad.finish()
    ffn.finish()
    line.finish()


def last_scatter(
    inner_part, output_part, weight, inner, dpre, middle, inputs, grad_resid, resid, mask, gain, ffn_dgain, head_dgain, dtaps,
    dbeta, beta, beta_part
):
    chips = lax.axis_size("dp") // 2
    rows, model = inputs.shape
    slab, width = output_part.shape[1:]
    arrays = [inner_part, output_part]
    shape = jax.ShapeDtypeStruct
    return pl.pallas_call(
        functools.partial(last_kernel, chips),
        in_specs=anywhere(9) + in_vmem(8),
        out_specs=in_vmem(12),
        out_shape=[shape((slab, width), f32)] * 4
        + [
            shape((width // HEAD, slab), f32),
            shape((width, slab), f32),
            shape((rows, model), f32),
            shape((rows, model), bf16),
            shape((1, model), f32),
            shape((1, model), f32),
            shape((1, HEAD), f32),
            shape((3, TAPS, dtaps.shape[1]), f32),
        ],
        scratch_shapes=LineScatter.scratch(chips, arrays)
        + [pltpu.VMEM((4 * rows, model), bf16)]
        + plane_scatter_scratch(rows, model)
        + [pltpu.VMEM((4 * rows, model), bf16)]
        + plane_scatter_scratch(rows, model)
        + [
            pltpu.VMEM((slab, width), f32),
            pltpu.VMEM((4, 48, SMALL), f32),
            pltpu.VMEM((3, 48, SMALL), f32),
            pltpu.VMEM((chips, 48, SMALL), f32),
            pltpu.VMEM((1, model), f32),
            pltpu.SemaphoreType.DMA((2 + chips,)),
            pltpu.SemaphoreType.DMA((2 + chips,)),
            pltpu.VMEM((2, *inner.shape[1:]), bf16),
            pltpu.VMEM((2, *weight.shape[1:]), bf16),
            pltpu.SemaphoreType.DMA((2, 2)),
            pltpu.VMEM(dpre.shape, bf16),
            pltpu.VMEM(middle.shape, bf16),
            pltpu.VMEM((rows, model), bf16),
            pltpu.VMEM((rows, model), f32),
            pltpu.VMEM((rows, model), f32),
            pltpu.SemaphoreType.DMA((5,)),
        ],
        compiler_params=pltpu.CompilerParams(
            collective_id=4, has_side_effects=True, vmem_limit_bytes=LARGE_LIMIT
        ),
        cost_estimate=pl.CostEstimate(flops=1_000_000, bytes_accessed=1_000_000, transcendentals=0),
    )(inner_part, output_part, weight, inner, dpre, middle, inputs, grad_resid, resid, mask, gain, ffn_dgain, head_dgain, dtaps, dbeta, beta, beta_part)


def rms_norm(values, gain):
    return (
        values * lax.rsqrt(jnp.mean(values * values, axis=-1, keepdims=True) + norm_epsilon) * gain
    )


def gather(values, axis):
    return lax.all_gather(values, axis, axis=0, tiled=True)


def scatter(values, axis):
    return lax.psum_scatter(values, axis, scatter_dimension=0, tiled=True)


def plain_first_gather(
    w_query, w_key, w_value, w_gate_out, w_beta, w_output, inputs, cotangent, mask, gain, w_gate, w_up, w_down
):
    shards = lax.axis_size("dp")
    inner = jnp.concatenate([w_query, w_key, w_value, w_gate_out], axis=1).astype(bf16)
    output = w_output.T.astype(bf16)
    grad = (cotangent.astype(f32) * mask).astype(bf16)
    return (
        gather(inner, "dp").reshape(shards, *inner.shape),
        gather(output, "dp").reshape(shards, *output.shape),
        gather(w_beta, "dp").reshape(shards, *w_beta.shape),
        gather(rms_norm(inputs.astype(f32), gain[0]).astype(bf16), "tensor"),
        gather(grad, "tensor"),
        jnp.concatenate([w_gate, w_up], axis=1).astype(bf16),
        w_down.T.astype(bf16),
        grad,
    )


def plain_branch_and_norm(z, weight, inputs, gain):
    branch = mm_nt(z, weight.reshape(-1, z.shape[1])).astype(bf16)
    resid = inputs.astype(f32) + scatter(branch, "tensor").astype(f32)
    return resid, gather(rms_norm(resid, gain[0]).astype(bf16), "tensor")


def plain_resid_backward(grad_low, grad_high, weight, z, out_weight, resid, grad_out, gain, high_part):
    part = mm_nt(jnp.concatenate([grad_low, grad_high], axis=1), weight).astype(bf16)
    back, gain_part = norm_backward(resid, scatter(part, "tensor").astype(f32), gain)
    value = grad_out.astype(f32) + back
    full = gather(value.astype(bf16), "tensor")
    high = scatter(high_part.reshape(-1, high_part.shape[2]), "dp").astype(f32)
    dgain = jnp.sum(gain_part, axis=0, keepdims=True)
    return value, dgain, mm(full, out_weight).astype(bf16), mm_tn(full, z).astype(bf16), high


def plain_last_scatter(
    inner_part, output_part, weight, inner, dpre, middle, inputs, grad_resid, resid, mask, gain, ffn_dgain, head_dgain, dtaps,
    dbeta, beta, beta_part
):
    beta = beta.transpose(1, 0, 2).reshape(BETA_PAD, -1)
    grad_part = (mm_nt(dpre, inner.reshape(-1, inner.shape[2])) + mm(dbeta, beta)).astype(bf16)
    slab = inner_part.shape[1]
    beta_total = lax.psum(beta_part[: output_part.shape[2] // HEAD], "dp")
    beta_total = lax.dynamic_slice_in_dim(beta_total, lax.axis_index("dp") * slab, slab, axis=1)
    inner, output = (
        scatter(part.reshape(-1, part.shape[-1]), "dp").astype(f32) for part in (inner_part, output_part)
    )
    width = output.shape[1]
    back, gain_part = norm_backward(inputs.astype(f32), scatter(grad_part, "tensor").astype(f32), gain)
    ffn_part = mm_nt(middle, weight.reshape(-1, weight.shape[2])).astype(bf16)
    out = ((resid + scatter(ffn_part, "tensor").astype(f32)) * mask).astype(bf16)
    gains = (jnp.sum(gain_part, axis=0, keepdims=True), ffn_dgain, head_dgain)
    return (
        *(inner[:, kind * width : (kind + 1) * width] for kind in range(4)),
        beta_total,
        output.T,
        grad_resid + back,
        out,
        *lax.psum(gains, ("dp", "tensor")),
        lax.psum(dtaps, "dp").reshape(3, TAPS, -1),
    )


def body(
    inputs,
    cotangent,
    lengths,
    norm_gain,
    w_query,
    w_key,
    w_value,
    w_gate_out,
    w_beta,
    conv_weight,
    out_norm_gain,
    w_output,
    ffn_norm_gain,
    w_gate,
    w_up,
    w_down,
):
    tensor_count = lax.axis_size("tensor")
    shards = lax.axis_size("dp")
    kernels = tensor_count == 4 and shards == 8
    rows, model = inputs.shape
    length = rows * tensor_count
    width = w_query.shape[1]
    heads = width // HEAD
    hidden = w_gate.shape[1]
    slab = w_query.shape[0]
    taps = conv_weight.reshape(3 * TAPS, width)
    first_gain, head_gain = norm_gain.reshape(1, model), out_norm_gain.reshape(1, HEAD)
    ffn_gain = ffn_norm_gain.reshape(1, model)

    positions = lax.axis_index("tensor") * rows + jnp.arange(rows, dtype=jnp.int32)
    mask = (positions < lengths[0]).astype(f32)[:, None]
    beta_rows = jnp.pad(w_beta.T, ((0, BETA_PAD - w_beta.shape[1]), (0, 0))).astype(bf16)
    inner, full_output, full_beta, normed, grad_full, gate_up, down, grad_out = (
        first_gather if kernels else plain_first_gather
    )(w_query, w_key, w_value, w_gate_out, beta_rows, w_output, inputs, cotangent, mask, first_gain, w_gate, w_up, w_down)
    gate_up = gather(gate_up, "dp")
    down = gather(down, "dp")

    pre = jnp.dot(normed, inner.reshape(model, -1), preferred_element_type=f32).astype(bf16)
    beta_pre = mm_nt(normed, full_beta.transpose(1, 0, 2).reshape(BETA_PAD, model))
    z, conv, mixed, inverse, states = mixer_forward(pre, beta_pre, taps, head_gain, heads)
    resid, normed2 = (branch_and_norm if kernels else plain_branch_and_norm)(z, full_output, inputs, ffn_gain)
    middle, slopes = (ffn if kernels else plain_ffn)(normed2, gate_up)
    down_part = mm_tn(grad_full, middle).astype(bf16)
    down, down_part = lax.optimization_barrier((down, down_part))
    down_total = scatter(down_part, "dp")
    grad_low, grad_high = (ffn_backward if kernels else plain_ffn_backward)(grad_full, down, slopes)
    low_part, high_part = mm_tn(normed2, grad_low).astype(bf16), mm_tn(normed2, grad_high).astype(bf16)
    grad_low, grad_high, low_part = lax.optimization_barrier((grad_low, grad_high, low_part))
    low_total = scatter(low_part, "dp")
    grad_resid, ffn_dgain, dz, output_grad, high_total = (resid_backward if kernels else plain_resid_backward)(
        grad_low,
        grad_high,
        gate_up,
        z,
        full_output.reshape(model, width),
        resid,
        grad_out,
        ffn_gain,
        high_part.reshape(shards, slab, -1),
    )
    dpre, dbeta, beta_part, dtaps, head_dgain = mixer_backward(
        pre, beta_pre, normed, conv, mixed, dz, inverse, states, taps, head_gain, heads
    )
    output_grad = output_grad.reshape(shards, slab, width)
    inner_grad = mm_tn(normed, dpre).astype(bf16).reshape(shards, slab, -1)
    results = (last_scatter if kernels else plain_last_scatter)(
        inner_grad,
        output_grad,
        down.reshape(shards, slab, hidden),
        inner,
        dpre,
        middle,
        inputs,
        grad_resid,
        resid,
        mask,
        first_gain,
        ffn_dgain,
        head_dgain,
        dtaps,
        dbeta,
        full_beta,
        beta_part,
    )
    gate_total, up_total, down_total, *results = (finish if kernels else plain_finish)(
        low_total, high_total, down_total, results
    )
    query_total, key_total, value_total, gate_out_total, beta_total, output_total, input_grad, output = results[:8]
    first_total, ffn_total, head_total, taps_total = results[8:]
    return (
        output,
        input_grad,
        first_total[0],
        query_total,
        key_total,
        value_total,
        gate_out_total,
        beta_total.T,
        taps_total,
        head_total[0],
        output_total,
        ffn_total[0],
        gate_total,
        up_total,
        down_total,
    )


def solution(mesh):
    rows = P(("dp", "tensor"), None)
    split = P("dp", "tensor")
    turned = P("tensor", "dp")
    taps = P(None, None, "tensor")
    return jax.shard_map(
        body,
        mesh=mesh,
        in_specs=(rows, rows, P("dp"), P(), split, split, split, split, split, taps, P(), turned, P(), split, split, turned),
        out_specs=(rows, rows, P(), split, split, split, split, split, taps, P(), turned, P(), split, split, turned),
        check_vma=False,
    )
```

```python
import functools
import jax
import jax.numpy as jnp
from jax import lax
from jax.experimental import pallas as pl
from jax.experimental.pallas import tpu as pltpu
from jax.sharding import PartitionSpec as P

norm_epsilon = 1e-06
head_epsilon = 1e-05
HEAD = 128
CHUNK = 128
STEP = 256
TAPS = 4
BETA_PAD = 16
VMEM_LIMIT = 56 * 1024 * 1024
f32 = jnp.float32
bf16 = jnp.bfloat16


def mm(a, b):
    return lax.dot_general(a, b, (((1,), (0,)), ((), ())), preferred_element_type=f32)


def mm_nt(a, b):
    return lax.dot_general(a, b, (((1,), (1,)), ((), ())), preferred_element_type=f32)


def mm_tn(a, b):
    return lax.dot_general(a, b, (((0,), (0,)), ((), ())), preferred_element_type=f32)


def chunk_indices():
    row = lax.broadcasted_iota(jnp.int32, (CHUNK, CHUNK), 0)
    col = lax.broadcasted_iota(jnp.int32, (CHUNK, CHUNK), 1)
    return row, col


def unit_lower_inverses(stricts, row, col):
    apart = row ^ col
    inverses = [jnp.where(row == col, 1.0, jnp.where(apart == 1, -strict, 0.0)) for strict in stricts]
    span = 2
    while span < CHUNK:
        here = (apart >= span) & (apart < 2 * span)
        lows = [inverse.astype(bf16) for inverse in inverses]
        firsts = [mm(low, jnp.where(here, strict, 0.0).astype(bf16)).astype(bf16) for low, strict in zip(lows, stricts)]
        inverses = [inverse - mm(first, low) for inverse, first, low in zip(inverses, firsts, lows)]
        span *= 2
    return [inverse.astype(bf16) for inverse in inverses]


def silu_parts(conv):
    sig = jax.nn.sigmoid(conv)
    return conv * sig, sig


def forward_kernel(
    heads, pre_ref, beta_ref, taps_ref, gain_ref, z_ref, conv_ref, mixed_ref, inv_ref, state_ref, hist, state
):
    step = pl.program_id(0)
    width = heads * HEAD
    rows = pre_ref.shape[0]

    @pl.when(step == 0)
    def _():
        hist[0:8, :] = jnp.zeros((8, 3 * width), f32)
        state[...] = jnp.zeros_like(state)

    @pl.when(step > 0)
    def _():
        hist[0:8, :] = hist[rows : rows + 8, :]

    hist[8 : 8 + rows, :] = pre_ref[:, 0 : 3 * width].astype(f32)
    row, col = chunk_indices()
    beta_all = jax.nn.sigmoid(beta_ref[...])
    work = []
    for head in range(heads):
        parts = []
        for kind in range(3):
            lanes = slice(kind * width + head * HEAD, kind * width + (head + 1) * HEAD)
            total = taps_ref[kind * TAPS : kind * TAPS + 1, head * HEAD : (head + 1) * HEAD] * hist[5 : 5 + rows, lanes]
            for tap in range(1, TAPS):
                total = total + taps_ref[
                    kind * TAPS + tap : kind * TAPS + tap + 1, head * HEAD : (head + 1) * HEAD
                ] * hist[5 + tap : 5 + tap + rows, lanes]
            conv_ref[:, lanes] = total
            act, _ = silu_parts(total)
            if kind < 2:
                act = act * lax.rsqrt(jnp.sum(act * act, axis=-1, keepdims=True) + norm_epsilon)
            if kind == 0:
                act = act * HEAD ** (-0.5)
            parts.append(act)
        beta = beta_all[:, head : head + 1]
        for part in range(rows // CHUNK):
            here = slice(part * CHUNK, (part + 1) * CHUNK)
            query, key, value = (p[here] for p in parts)
            query_low, key_low = query.astype(bf16), key.astype(bf16)
            b = beta[here]
            stacked = jnp.concatenate([(b * key).astype(bf16), (b * value).astype(bf16)], axis=1)
            strict = jnp.where(row > col, b * mm_nt(key_low, key_low), 0.0)
            scores = jnp.where(row >= col, mm_nt(query_low, key_low), 0.0).astype(bf16)
            work.append((head, part, query_low, key_low, stacked, scores, strict))
    inverses = unit_lower_inverses([item[-1] for item in work], row, col)
    solved_all = {}
    for (head, part, query_low, key_low, stacked, scores, _), inverse in zip(work, inverses):
        inv_ref[head, part] = inverse
        solved_all[part, head] = (query_low, key_low, scores, mm(inverse, stacked))
    states = [state[head] for head in range(heads)]
    for part in range(rows // CHUNK):
        here = slice(part * CHUNK, (part + 1) * CHUNK)
        enters = [enter.astype(bf16) for enter in states]
        items = [solved_all[part, head] for head in range(heads)]
        freshes = [
            (solved[:, HEAD:] - mm(solved[:, :HEAD].astype(bf16), enter)).astype(bf16)
            for (_, _, _, solved), enter in zip(items, enters)
        ]
        states = [old + mm_tn(key_low, fresh) for old, (_, key_low, _, _), fresh in zip(states, items, freshes)]
        for head in range(heads):
            lanes = slice(head * HEAD, (head + 1) * HEAD)
            query_low, _, scores, _ = items[head]
            state_ref[head, part] = enters[head]
            mixed = mm(query_low, enters[head]) + mm(scores, freshes[head])
            mixed_ref[here, lanes] = mixed
            gate = pre_ref[here, 3 * width + head * HEAD : 3 * width + (head + 1) * HEAD].astype(f32)
            gate_act, _ = silu_parts(gate)
            normed = mixed * lax.rsqrt(jnp.mean(mixed * mixed, axis=-1, keepdims=True) + head_epsilon)
            z_ref[here, lanes] = (normed * gain_ref[...] * gate_act).astype(bf16)
    for head in range(heads):
        state[head] = states[head]


def mixer_forward(pre, beta, taps, gain, heads):
    length, total = pre.shape
    width = heads * HEAD
    steps, parts = length // STEP, STEP // CHUNK
    return pl.pallas_call(
        functools.partial(forward_kernel, heads),
        grid=(steps,),
        in_specs=[
            pl.BlockSpec((STEP, total), lambda i: (i, 0)),
            pl.BlockSpec((STEP, BETA_PAD), lambda i: (i, 0)),
            pl.BlockSpec((3 * TAPS, width), lambda i: (0, 0)),
            pl.BlockSpec((1, HEAD), lambda i: (0, 0)),
        ],
        out_specs=[
            pl.BlockSpec((STEP, width), lambda i: (i, 0)),
            pl.BlockSpec((STEP, 3 * width), lambda i: (i, 0)),
            pl.BlockSpec((STEP, width), lambda i: (i, 0)),
            pl.BlockSpec((heads, parts, CHUNK, CHUNK), lambda i: (0, i, 0, 0)),
            pl.BlockSpec((heads, parts, HEAD, HEAD), lambda i: (0, i, 0, 0)),
        ],
        out_shape=[
            jax.ShapeDtypeStruct((length, width), bf16),
            jax.ShapeDtypeStruct((length, 3 * width), f32),
            jax.ShapeDtypeStruct((length, width), f32),
            jax.ShapeDtypeStruct((heads, steps * parts, CHUNK, CHUNK), bf16),
            jax.ShapeDtypeStruct((heads, steps * parts, HEAD, HEAD), bf16),
        ],
        scratch_shapes=[
            pltpu.VMEM((STEP + 8, 3 * width), f32),
            pltpu.VMEM((heads, HEAD, HEAD), f32),
        ],
        compiler_params=pltpu.CompilerParams(
            dimension_semantics=("arbitrary",), vmem_limit_bytes=VMEM_LIMIT
        ),
        cost_estimate=pl.CostEstimate(
            flops=2 * length * width * HEAD * 60, bytes_accessed=length * (total * 4 + width * 24), transcendentals=length * width * 8
        ),
    )(pre, beta, taps, gain)


def backward_kernel(
    heads,
    pre_ref,
    beta_ref,
    source_ref,
    conv_ref,
    mixed_ref,
    dz_ref,
    inv_ref,
    state_ref,
    taps_ref,
    gain_ref,
    dpre_ref,
    dbeta_ref,
    dsource_ref,
    dtaps_ref,
    dgain_ref,
    later,
    dstate,
):
    step = pl.program_id(0)
    width = heads * HEAD
    rows = pre_ref.shape[0]
    count = rows // CHUNK

    @pl.when(step == 0)
    def _():
        later[rows : rows + 8, :] = jnp.zeros((8, 3 * width), f32)
        dstate[...] = jnp.zeros_like(dstate)
        dtaps_ref[...] = jnp.zeros_like(dtaps_ref)
        dgain_ref[...] = jnp.zeros_like(dgain_ref)
        dsource_ref[...] = jnp.zeros_like(dsource_ref)

    @pl.when(step > 0)
    def _():
        later[rows : rows + 8, :] = later[0:8, :]

    row, col = chunk_indices()
    beta_all = jax.nn.sigmoid(beta_ref[...])
    beta_lane = lax.broadcasted_iota(jnp.int32, (CHUNK, BETA_PAD), 1)
    dbeta_all = [jnp.zeros((CHUNK, BETA_PAD), f32) for _ in range(count)]
    dgain = jnp.zeros((1, HEAD), f32)
    gain = gain_ref[...]
    every = [(part, head) for part in reversed(range(count)) for head in range(heads)]

    def of(ref, kind, at):
        part, head = at
        lanes = slice(kind * width + head * HEAD, kind * width + (head + 1) * HEAD)
        return ref[part * CHUNK : (part + 1) * CHUNK, lanes].astype(f32)

    betas = {(part, head): beta_all[part * CHUNK : (part + 1) * CHUNK, head : head + 1] for part, head in every}
    unit_queries, keys, query_lows, key_lows, scales, stacks = {}, {}, {}, {}, {}, {}
    for at in every:
        acts = [silu_parts(of(conv_ref, kind, at))[0] for kind in range(3)]
        scales[at] = [lax.rsqrt(jnp.sum(act * act, axis=-1, keepdims=True) + norm_epsilon) for act in acts[:2]]
        unit_queries[at], keys[at] = acts[0] * scales[at][0], acts[1] * scales[at][1]
        query_lows[at] = (unit_queries[at] * HEAD ** (-0.5)).astype(bf16)
        key_lows[at] = keys[at].astype(bf16)
        stacks[at] = jnp.concatenate([(betas[at] * keys[at]).astype(bf16), (betas[at] * acts[2]).astype(bf16)], axis=1)
    solved = {at: mm(inv_ref[at[1], at[0]], stacks[at]) for at in every}
    scores = {at: jnp.where(row >= col, mm_nt(query_lows[at], key_lows[at]), 0.0).astype(bf16) for at in every}
    weights = {at: solved[at][:, :HEAD].astype(bf16) for at in every}
    outs = {}
    for at in every:
        part, head = at
        here = slice(part * CHUNK, (part + 1) * CHUNK)
        gate = of(pre_ref, 3, at)
        gate_act, gate_sig = silu_parts(gate)
        mixed, dz = of(mixed_ref, 0, at), of(dz_ref, 0, at)
        root = lax.rsqrt(jnp.mean(mixed * mixed, axis=-1, keepdims=True) + head_epsilon)
        normed = mixed * root
        dgate = dz * normed * gain * (gate_sig * (1.0 + gate * (1.0 - gate_sig)))
        dpre_ref[here, 3 * width + head * HEAD : 3 * width + (head + 1) * HEAD] = dgate.astype(bf16)
        dgained = dz * gate_act
        dgain = dgain + jnp.sum(dgained * normed, axis=0, keepdims=True)
        dnormed = dgained * gain
        dmixed = root * (dnormed - normed * jnp.mean(dnormed * normed, axis=-1, keepdims=True))
        outs[at] = dmixed.astype(bf16)
    enters = {(part, head): state_ref[head, part] for part, head in every}
    fresh = {at: (solved[at][:, HEAD:] - mm(weights[at], enters[at])).astype(bf16) for at in every}
    within = {at: mm_tn(scores[at], outs[at]) for at in every}
    across = {at: mm_tn(query_lows[at], outs[at]) for at in every}
    leavings, dfresh = {}, {}
    states = [dstate[head] for head in range(heads)]
    for part in reversed(range(count)):
        for head in range(heads):
            leavings[part, head] = states[head].astype(bf16)
        for head in range(heads):
            at = (part, head)
            dfresh[at] = (within[at] + mm(key_lows[at], leavings[at])).astype(bf16)
        for head in range(heads):
            at = (part, head)
            states[head] = states[head] + across[at] - mm_tn(weights[at], dfresh[at])
    for head in range(heads):
        dstate[head] = states[head]
    dscores = {at: jnp.where(row >= col, mm_nt(outs[at], fresh[at]), 0.0).astype(bf16) for at in every}
    dweights = {at: (-mm_nt(dfresh[at], enters[at])).astype(bf16) for at in every}
    dxys = {
        at: mm_tn(inv_ref[at[1], at[0]], jnp.concatenate([dweights[at], dfresh[at]], axis=1)) for at in every
    }
    dqueries = {at: mm_nt(outs[at], enters[at]) + mm(dscores[at], key_lows[at]) for at in every}
    dkeys = {at: mm_tn(dscores[at], query_lows[at]) + mm_nt(fresh[at], leavings[at]) for at in every}
    dsystems = {
        at: jnp.where(row > col, -mm_nt(dxys[at].astype(bf16), solved[at].astype(bf16)), 0.0) for at in every
    }
    dsystem_lows = {at: dsystems[at].astype(bf16) for at in every}
    firsts = {at: mm(dsystem_lows[at], key_lows[at]) for at in every}
    seconds = {at: mm_tn(dsystem_lows[at], stacks[at][:, :HEAD]) for at in every}
    grams = {at: mm_nt(key_lows[at], key_lows[at]) for at in every}
    for at in every:
        part, head = at
        beta, dx, dy, key = betas[at], dxys[at][:, :HEAD], dxys[at][:, HEAD:], keys[at]
        dkey = dkeys[at] + beta * (firsts[at] + dx) + seconds[at]
        convs = [of(conv_ref, kind, at) for kind in range(3)]
        sigs = [jax.nn.sigmoid(conv) for conv in convs]
        dbeta = jnp.sum(dsystems[at] * grams[at] + dx * key + dy * (convs[2] * sigs[2]), axis=-1, keepdims=True)
        dbeta = dbeta * beta * (1.0 - beta)
        dbeta_all[part] = jnp.where(beta_lane == head, dbeta, dbeta_all[part])
        unit_query, dquery = unit_queries[at], dqueries[at] * HEAD ** (-0.5)
        dquery = scales[at][0] * (dquery - unit_query * jnp.sum(unit_query * dquery, axis=-1, keepdims=True))
        dkey = scales[at][1] * (dkey - key * jnp.sum(key * dkey, axis=-1, keepdims=True))
        for kind, grad in enumerate((dquery, dkey, beta * dy)):
            dconv = grad * (sigs[kind] * (1.0 + convs[kind] * (1.0 - sigs[kind])))
            lanes = slice(kind * width + head * HEAD, kind * width + (head + 1) * HEAD)
            later[part * CHUNK : (part + 1) * CHUNK, lanes] = dconv
    for part in range(count):
        here = slice(part * CHUNK, (part + 1) * CHUNK)
        dbeta_low = dbeta_all[part].astype(bf16)
        dbeta_ref[here, :] = dbeta_low
        dsource_ref[...] += mm_tn(dbeta_low, source_ref[here, :])
    dgain_ref[...] += dgain
    for kind in range(3):
        for head in range(heads):
            lanes = slice(kind * width + head * HEAD, kind * width + (head + 1) * HEAD)
            source = pre_ref[:, lanes].astype(f32)
            total = jnp.zeros((rows, HEAD), f32)
            for tap in range(TAPS):
                at = kind * TAPS + tap
                shifted = later[TAPS - 1 - tap : TAPS - 1 - tap + rows, lanes]
                total = total + taps_ref[at : at + 1, head * HEAD : (head + 1) * HEAD] * shifted
                dtaps_ref[at : at + 1, head * HEAD : (head + 1) * HEAD] += jnp.sum(
                    source * shifted, axis=0, keepdims=True
                )
            dpre_ref[:, lanes] = total.astype(bf16)


def mixer_backward(pre, beta, source, conv, mixed, dz, inverse, states, taps, gain, heads):
    length, total = pre.shape
    model = source.shape[1]
    width = heads * HEAD
    steps, parts = length // STEP, STEP // CHUNK
    return pl.pallas_call(
        functools.partial(backward_kernel, heads),
        grid=(steps,),
        in_specs=[
            pl.BlockSpec((STEP, total), lambda i: (steps - 1 - i, 0)),
            pl.BlockSpec((STEP, BETA_PAD), lambda i: (steps - 1 - i, 0)),
            pl.BlockSpec((STEP, model), lambda i: (steps - 1 - i, 0)),
            pl.BlockSpec((STEP, 3 * width), lambda i: (steps - 1 - i, 0)),
            pl.BlockSpec((STEP, width), lambda i: (steps - 1 - i, 0)),
            pl.BlockSpec((STEP, width), lambda i: (steps - 1 - i, 0)),
            pl.BlockSpec((heads, parts, CHUNK, CHUNK), lambda i: (0, steps - 1 - i, 0, 0)),
            pl.BlockSpec((heads, parts, HEAD, HEAD), lambda i: (0, steps - 1 - i, 0, 0)),
            pl.BlockSpec((3 * TAPS, width), lambda i: (0, 0)),
            pl.BlockSpec((1, HEAD), lambda i: (0, 0)),
        ],
        out_specs=[
            pl.BlockSpec((STEP, total), lambda i: (steps - 1 - i, 0)),
            pl.BlockSpec((STEP, BETA_PAD), lambda i: (steps - 1 - i, 0)),
            pl.BlockSpec((BETA_PAD, model), lambda i: (0, 0)),
            pl.BlockSpec((3 * TAPS, width), lambda i: (0, 0)),
            pl.BlockSpec((1, HEAD), lambda i: (0, 0)),
        ],
        out_shape=[
            jax.ShapeDtypeStruct((length, total), bf16),
            jax.ShapeDtypeStruct((length, BETA_PAD), bf16),
            jax.ShapeDtypeStruct((BETA_PAD, model), f32),
            jax.ShapeDtypeStruct((3 * TAPS, width), f32),
            jax.ShapeDtypeStruct((1, HEAD), f32),
        ],
        scratch_shapes=[
            pltpu.VMEM((STEP + 8, 3 * width), f32),
            pltpu.VMEM((heads, HEAD, HEAD), f32),
        ],
        compiler_params=pltpu.CompilerParams(
            dimension_semantics=("arbitrary",), vmem_limit_bytes=VMEM_LIMIT
        ),
        cost_estimate=pl.CostEstimate(
            flops=1_000_000, bytes_accessed=1_000_000, transcendentals=0
        ),
    )(pre, beta, source, conv, mixed, dz, inverse, states, taps, gain)


MESH = pl.DeviceIdType.MESH
TILE = 16
BOTH_LAST = 512
LANES = 128
LARGE_LIMIT = 60 * 1024 * 1024


def remote(source, target, send, receive, **where):
    return pltpu.make_async_remote_copy(
        src_ref=source,
        dst_ref=target,
        send_sem=send,
        recv_sem=receive,
        device_id=where,
        device_id_type=MESH,
    )


def when(condition, action):
    pl.when(condition)(action)


def greet(**where):
    pl.semaphore_signal(
        pltpu.get_barrier_semaphore(), inc=1, device_id=where, device_id_type=MESH
    )


def wait_greetings(count):
    pl.semaphore_wait(pltpu.get_barrier_semaphore(), count)


def plane():
    me = lax.axis_index("tensor")
    across = me + 1 - 2 * lax.rem(me, 2)
    along = lax.rem(me + 2, 4)
    return me, across, along


def chip_and_core():
    index = lax.axis_index("dp")
    return index // 2, lax.rem(index, 2)


def greet_line(chips):
    chip, core = chip_and_core()
    greet(dp=chip * 2 + 1 - core)
    when(chip > 0, lambda: greet(dp=(chip - 1) * 2 + core))
    when(chip < chips - 1, lambda: greet(dp=(chip + 1) * 2 + core))
    return 1 + jnp.where(chip > 0, 1, 0) + jnp.where(chip < chips - 1, 1, 0)


class PlaneGather:
    def __init__(self, own, full, send, receive):
        self.own, self.full, self.send, self.receive = own, full, send, receive
        self.me, self.across, self.along = plane()
        self.far = lax.rem(self.across + 2, 4)
        self.rows = own.shape[0]
        self.half = self.rows // 2

    def slot(self, block, half):
        start = pl.multiple_of(block * self.rows + half * self.half, self.half)
        return self.full.at[pl.ds(start, self.half)]

    def mine(self, half):
        return self.own.at[pl.ds(half * self.half, self.half)]

    def out(self, half, kind):
        where = self.across if kind == 0 else self.along
        at = 2 * kind + half
        return remote(
            self.mine(half), self.slot(self.me, half), self.send.at[at], self.receive.at[at], tensor=where
        )

    def arriving(self, half, kind):
        block = self.across if kind == 0 else self.along
        at = 2 * kind + half
        view = self.slot(block, half)
        return remote(view, view, self.send.at[at], self.receive.at[at], tensor=block)

    def passing(self, kind):
        view = self.slot(self.across if kind == 0 else self.along, kind)
        where = self.along if kind == 0 else self.across
        return remote(view, view, self.send.at[4 + kind], self.receive.at[4 + kind], tensor=where)

    def passed(self, kind):
        view = self.slot(self.far, kind)
        where = self.along if kind == 0 else self.across
        return remote(view, view, self.send.at[4 + kind], self.receive.at[4 + kind], tensor=where)

    def start(self, half):
        for kind in (half, 1 - half):
            self.out(half, kind).start()

    def relay(self, kind):
        self.arriving(kind, kind).wait_recv()
        self.passing(kind).start()

    def near(self, kind):
        self.arriving(1 - kind, kind).wait_recv()

    def diagonal(self):
        self.passed(0).wait_recv()
        self.passed(1).wait_recv()

    def finish(self):
        self.near(0)
        self.near(1)
        self.diagonal()
        self.sent()

    def sent(self):
        for kind in (0, 1):
            self.passing(kind).wait_send()
            for half in (0, 1):
                self.out(half, kind).wait_send()


class PlaneScatter:
    def __init__(self, part, first, second, stage, send, receive):
        self.part, self.first, self.second, self.stage = part, first, second, stage
        self.send, self.receive = send, receive
        self.me, self.across, self.along = plane()
        self.far = lax.rem(self.across + 2, 4)
        self.rows = part.shape[0] // 4
        self.half = self.rows // 2

    def start_of(self, block, half):
        return pl.multiple_of(block * self.rows + half * self.half, self.half)

    def view(self, block, half):
        return self.part.at[pl.ds(self.start_of(block, half), self.half)]

    def out(self, kind, order):
        where = self.across if kind == 0 else self.along
        at = 2 * kind + order
        return remote(
            self.view(self.far if order == 0 else where, kind),
            self.first.at[at],
            self.send.at[at],
            self.receive.at[at],
            tensor=where,
        )

    def over(self, kind):
        where = self.along if kind == 0 else self.across
        return remote(
            self.stage.at[kind], self.second.at[kind], self.send.at[4 + kind], self.receive.at[4 + kind], tensor=where
        )

    def start_far(self):
        for kind in (0, 1):
            self.out(kind, 0).start()

    def start_near(self, kind):
        self.out(kind, 1).start()

    def relay(self, kind):
        self.out(kind, 0).wait_recv()
        block = self.along if kind == 0 else self.across
        start = self.start_of(block, kind)

        def add(index, carry):
            at = pl.multiple_of(index * TILE, TILE)
            mine = self.part[pl.ds(pl.multiple_of(start + at, TILE), TILE), :].astype(f32)
            other = self.first[2 * kind, pl.ds(at, TILE), :].astype(f32)
            self.stage[kind, pl.ds(at, TILE), :] = (mine + other).astype(bf16)
            return carry

        lax.fori_loop(0, self.half // TILE, add, 0)
        self.over(kind).start()

    def ready(self, kind):
        self.out(kind, 1).wait_recv()
        self.over(kind).wait_recv()

    def tile(self, kind, at):
        start = self.start_of(self.me, kind)
        mine = self.part[pl.ds(pl.multiple_of(start + at, TILE), TILE), :].astype(f32)
        near = self.first[2 * kind + 1, pl.ds(at, TILE), :].astype(f32)
        return mine + near + self.second[kind, pl.ds(at, TILE), :].astype(f32)

    def finish(self):
        for kind in (0, 1):
            for order in (0, 1):
                self.out(kind, order).wait_send()
            self.over(kind).wait_send()


def plane_scatter_scratch(rows, columns):
    half = rows // 2
    return [
        pltpu.VMEM((4, half, columns), bf16),
        pltpu.VMEM((2, half, columns), bf16),
        pltpu.VMEM((2, half, columns), bf16),
        pltpu.SemaphoreType.DMA((6,)),
        pltpu.SemaphoreType.DMA((6,)),
    ]


def pieces_of(arrays, size):
    found = []
    for index, array in enumerate(arrays):
        rows, columns = array.shape[-2:]
        count = max(1, min(rows // 64, round(rows * columns / size)))
        while rows % count or (rows // count) % 16:
            count -= 1
        for piece in range(count):
            found.append((index, piece * (rows // count), rows // count))
    return found


PIECE = 64 * 2176


class LineGather:
    def __init__(self, chips, owns, fulls, sems):
        self.chips, self.owns, self.fulls = chips, owns, fulls
        self.pieces = pieces_of(owns, PIECE)
        self.right_send, self.right_receive, self.left_send, self.left_receive = sems[:4]
        self.core_send, self.core_receive, self.local = sems[4:]
        self.chip, self.core = chip_and_core()

    @staticmethod
    def scratch(chips, pieces, arrays):
        return [pltpu.SemaphoreType.DMA((chips, pieces)) for _ in range(6)] + [pltpu.SemaphoreType.DMA((arrays,))]

    def slot(self, piece, chip, core):
        index, start, rows = self.pieces[piece]
        return self.fulls[index].at[chip * 2 + core, pl.ds(start, rows)]

    def source(self, piece, away):
        index, start, rows = self.pieces[piece]
        return self.owns[index].at[pl.ds(start, rows)]

    def right(self, piece, away, chip):
        slot = self.slot(piece, chip, self.core)
        source = self.source(piece, 0) if away == 0 else slot
        to = (self.chip + 1) * 2 + self.core
        return remote(source, slot, self.right_send.at[away, piece], self.right_receive.at[away, piece], dp=to)

    def left(self, piece, away, chip):
        slot = self.slot(piece, chip, self.core)
        source = self.source(piece, 0) if away == 0 else slot
        to = (self.chip - 1) * 2 + self.core
        return remote(source, slot, self.left_send.at[away, piece], self.left_receive.at[away, piece], dp=to)

    def trade(self, piece, chip, own):
        slot = self.slot(piece, chip, self.core)
        source = self.source(piece, 0) if own else slot
        to = self.chip * 2 + 1 - self.core
        return remote(source, slot, self.core_send.at[chip, piece], self.core_receive.at[chip, piece], dp=to)

    def keep(self, index):
        return pltpu.make_async_copy(
            self.owns[index], self.fulls[index].at[self.chip * 2 + self.core], self.local.at[index]
        )

    def start(self):
        for piece in range(len(self.pieces)):
            when(self.chip < self.chips - 1, lambda: self.right(piece, 0, self.chip).start())
            when(self.chip > 0, lambda: self.left(piece, 0, self.chip).start())
        for piece in range(len(self.pieces)):
            self.trade(piece, self.chip, True).start()
        for index in range(len(self.owns)):
            self.keep(index).start()

    def step(self, away):
        for piece in range(len(self.pieces)):

            def from_left():
                chip = self.chip - away
                self.right(piece, away - 1, chip).wait_recv()
                if away < self.chips - 1:
                    when(self.chip < self.chips - 1, lambda: self.right(piece, away, chip).start())
                self.trade(piece, chip, False).start()

            def from_right():
                chip = self.chip + away
                self.left(piece, away - 1, chip).wait_recv()
                if away < self.chips - 1:
                    when(self.chip > 0, lambda: self.left(piece, away, chip).start())
                self.trade(piece, chip, False).start()

            when(self.chip >= away, from_left)
            when(self.chip + away < self.chips, from_right)

    def finish(self):
        for index in range(len(self.owns)):
            self.keep(index).wait()
        for piece in range(len(self.pieces)):
            for away in range(self.chips - 1):
                when(
                    (self.chip < self.chips - 1) & (self.chip >= away),
                    lambda: self.right(piece, away, self.chip - away).wait_send(),
                )
                when(
                    (self.chip > 0) & (self.chip + away < self.chips),
                    lambda: self.left(piece, away, self.chip + away).wait_send(),
                )
            for chip in range(self.chips):
                trade = remote(
                    self.slot(piece, chip, self.core),
                    self.slot(piece, chip, 1 - self.core),
                    self.core_send.at[chip, piece],
                    self.core_receive.at[chip, piece],
                    dp=self.chip * 2 + 1 - self.core,
                )
                trade.wait_send()
                trade.wait_recv()


def first_gather_kernel(chips, *refs):
    w_query, w_key, w_value, w_gate_out, w_beta, w_output, inputs, cotangent, mask, gain = refs[:10]
    w_gate, w_up, w_down = refs[10:13]
    inner_full, output_full, beta_full, normed_full, grad_full, gate_up, down, grad = refs[13:21]
    inner, output, normed, gate_wide, up_wide, down_wide = refs[21:27]
    sems = refs[27:]
    width, hidden = w_query.shape[1], w_gate.shape[1]
    line = LineGather(chips, [inner, output, w_beta], [inner_full, output_full, beta_full], sems[:7])
    rows = [PlaneGather(normed, normed_full, *sems[7:9]), PlaneGather(grad, grad_full, *sems[9:11])]
    local = sems[11]
    keeps = [
        pltpu.make_async_copy(
            own, full.at[pl.ds(pl.multiple_of(each.me * each.rows, each.rows), each.rows)], local.at[at]
        )
        for at, (own, full, each) in enumerate(((normed, normed_full, rows[0]), (grad, grad_full, rows[1])))
    ]
    loads = [
        pltpu.make_async_copy(source, target, local.at[2 + at])
        for at, (source, target) in enumerate(((w_gate, gate_wide), (w_up, up_wide), (w_down, down_wide)))
    ]
    greetings = greet_line(chips)
    greet(tensor=rows[0].across)
    greet(tensor=rows[0].along)
    for kind, weight in enumerate((w_query, w_key, w_value, w_gate_out)):
        inner[:, kind * width : (kind + 1) * width] = weight[...].astype(bf16)
    output[...] = jnp.transpose(w_output[...]).astype(bf16)
    wait_greetings(2 + greetings)
    line.start()
    for load in loads:
        load.start()

    def norm(index, carry):
        here = pl.ds(pl.multiple_of(index * TILE, TILE), TILE)
        value = inputs[here, :].astype(f32)
        scale = lax.rsqrt(jnp.mean(value * value, axis=-1, keepdims=True) + norm_epsilon)
        normed[here, :] = (value * scale * gain[...]).astype(bf16)
        grad[here, :] = (cotangent[here, :].astype(f32) * mask[here, :]).astype(bf16)
        return carry

    lax.fori_loop(0, inputs.shape[0] // TILE, norm, 0)
    for each in rows:
        each.start(0)
        each.start(1)
    for keep in keeps:
        keep.start()
    for load in loads:
        load.wait()
    for kind, wide in enumerate((gate_wide, up_wide)):
        for tile in range(hidden // LANES):
            to = (2 * tile + kind) * LANES
            gate_up[:, to : to + LANES] = wide[:, tile * LANES : (tile + 1) * LANES].astype(bf16)
    down[...] = jnp.transpose(down_wide[...]).astype(bf16)
    rows[0].relay(0)
    rows[0].relay(1)
    line.step(1)
    rows[1].relay(0)
    rows[1].relay(1)
    for away in range(2, chips):
        line.step(away)
    for each in rows:
        each.finish()
    for keep in keeps:
        keep.wait()
    line.finish()


def ffn_kernel(normed, weight, middle, slopes):
    def block(index, carry):
        here = pl.ds(pl.multiple_of(index * 512, 512), 512)
        both = mm(normed[here, :], weight[...])
        gate, up_part = both[:, :LANES], both[:, LANES:]
        act, sig = silu_parts(gate)
        middle[here, :] = (act * up_part).astype(bf16)
        slopes[here, :LANES] = (up_part * sig * (1.0 + gate * (1.0 - sig))).astype(bf16)
        slopes[here, LANES:] = act.astype(bf16)
        return carry

    lax.fori_loop(0, normed.shape[0] // 512, block, 0, unroll=True)


def ffn(normed, gate_up):
    length, model = normed.shape
    hidden = gate_up.shape[1] // 2
    return pl.pallas_call(
        ffn_kernel,
        grid=(hidden // LANES,),
        in_specs=[
            pl.BlockSpec((length, model), lambda i: (0, 0)),
            pl.BlockSpec((model, 2 * LANES), lambda i: (0, i)),
        ],
        out_specs=[
            pl.BlockSpec((length, LANES), lambda i: (0, i)),
            pl.BlockSpec((length, 2 * LANES), lambda i: (0, i)),
        ],
        out_shape=[
            jax.ShapeDtypeStruct((length, hidden), bf16),
            jax.ShapeDtypeStruct((length, 2 * hidden), bf16),
        ],
        compiler_params=pltpu.CompilerParams(
            dimension_semantics=("arbitrary",), vmem_limit_bytes=VMEM_LIMIT
        ),
        cost_estimate=pl.CostEstimate(
            flops=4 * length * model * hidden, bytes_accessed=2 * (length * model + 2 * model * hidden), transcendentals=length * hidden
        ),
    )(normed, gate_up)


def ffn_backward_kernel(grad, weight, slopes, low, high):
    split = low.shape[1] // LANES
    grad_middle = mm(grad[...], weight[...])
    for tile in range(weight.shape[1] // LANES):
        part = grad_middle[:, tile * LANES : (tile + 1) * LANES]
        for kind in range(2):
            at = 2 * tile + kind
            target, to = (low, at) if at < split else (high, at - split)
            slope = slopes[:, at * LANES : (at + 1) * LANES].astype(f32)
            target[:, to * LANES : (to + 1) * LANES] = (part * slope).astype(bf16)


def ffn_backward(grad, down, slopes):
    length, model = grad.shape
    hidden = down.shape[1]
    block = 512
    widths = (2 * hidden - BOTH_LAST, BOTH_LAST)
    return pl.pallas_call(
        ffn_backward_kernel,
        grid=(length // block,),
        in_specs=[
            pl.BlockSpec((block, model), lambda i: (i, 0)),
            pl.BlockSpec((model, hidden), lambda i: (0, 0)),
            pl.BlockSpec((block, 2 * hidden), lambda i: (i, 0)),
        ],
        out_specs=[pl.BlockSpec((block, width), lambda i: (i, 0)) for width in widths],
        out_shape=[jax.ShapeDtypeStruct((length, width), bf16) for width in widths],
        compiler_params=pltpu.CompilerParams(
            dimension_semantics=("arbitrary",), vmem_limit_bytes=VMEM_LIMIT
        ),
        cost_estimate=pl.CostEstimate(
            flops=2 * length * model * hidden, bytes_accessed=2 * (length * model + model * hidden + 4 * length * hidden), transcendentals=0
        ),
    )(grad, down, slopes)


def finish_kernel(count, *refs):
    sources, targets, held, sems = refs[:count], refs[count : 2 * count], refs[2 * count : 3 * count], refs[-1]
    kept, outs = held[:3], refs[3 * count : 3 * count + 3]
    loads = [
        pltpu.make_async_copy(source, here, sems.at[0, at]) for at, (source, here) in enumerate(zip(sources, held))
    ]
    stores = [
        pltpu.make_async_copy(here, target, sems.at[1, at])
        for at, (here, target) in enumerate(zip((*outs, *held[3:]), targets))
    ]
    for load in loads:
        load.start()
    low, high, down = kept
    gate_out, up_out, down_out = outs
    split = low.shape[1] // LANES
    for load in loads[:3]:
        load.wait()
    for tile in range(gate_out.shape[1] // LANES):
        for kind, target in enumerate((gate_out, up_out)):
            at = 2 * tile + kind
            source, start = (low, at) if at < split else (high, at - split)
            target[:, tile * LANES : (tile + 1) * LANES] = source[:, start * LANES : (start + 1) * LANES].astype(f32)
    stores[0].start()
    stores[1].start()
    for load, store in zip(loads[3:], stores[3:]):
        load.wait()
        store.start()
    for tile in range(gate_out.shape[1] // LANES):
        lanes = slice(tile * LANES, (tile + 1) * LANES)
        down_out[lanes, :] = jnp.transpose(down[:, lanes].astype(f32))
    stores[2].start()
    for store in stores:
        store.wait()


def finish(low, high, down, arrays):
    slab, hidden = down.shape
    sources = [low, high, down, *arrays]
    count = len(sources)
    outs = [
        jax.ShapeDtypeStruct((slab, hidden), f32),
        jax.ShapeDtypeStruct((slab, hidden), f32),
        jax.ShapeDtypeStruct((hidden, slab), f32),
    ]
    return pl.pallas_call(
        functools.partial(finish_kernel, count),
        in_specs=anywhere(count),
        out_specs=anywhere(count),
        out_shape=outs + [jax.ShapeDtypeStruct(array.shape, array.dtype) for array in arrays],
        scratch_shapes=[pltpu.VMEM(array.shape, array.dtype) for array in sources]
        + [pltpu.VMEM(out.shape, f32) for out in outs]
        + [pltpu.SemaphoreType.DMA((2, count))],
        compiler_params=pltpu.CompilerParams(vmem_limit_bytes=VMEM_LIMIT),
        cost_estimate=pl.CostEstimate(flops=0, bytes_accessed=40 * slab * hidden, transcendentals=0),
    )(*sources)


def plain_ffn(normed, gate_up):
    gate, up_part = jnp.split(jnp.dot(normed, gate_up, preferred_element_type=f32), 2, axis=1)
    act, sig = silu_parts(gate)
    slopes = jnp.concatenate([up_part * sig * (1.0 + gate * (1.0 - sig)), act], axis=1)
    return (act * up_part).astype(bf16), slopes.astype(bf16)


def plain_ffn_backward(grad, down, slopes):
    grad_middle = jnp.dot(grad, down, preferred_element_type=f32)
    both = (jnp.concatenate([grad_middle, grad_middle], axis=1) * slopes.astype(f32)).astype(bf16)
    return both[:, :-BOTH_LAST], both[:, -BOTH_LAST:]


def plain_finish(low, high, down, arrays):
    gate, up_part = jnp.split(jnp.concatenate([low.astype(f32), high], axis=1), 2, axis=1)
    return gate, up_part, down.astype(f32).T, *arrays


def anywhere(count):
    return [pl.BlockSpec(memory_space=pl.ANY)] * count


def in_vmem(count):
    return [pl.BlockSpec(memory_space=pltpu.VMEM)] * count


def first_gather(w_query, w_key, w_value, w_gate_out, w_beta, w_output, inputs, cotangent, mask, gain, w_gate, w_up, w_down):
    shards = lax.axis_size("dp")
    rows, model = inputs.shape
    slab, width = w_query.shape
    hidden = w_gate.shape[1]
    inner = jax.ShapeDtypeStruct((slab, 4 * width), bf16)
    output = jax.ShapeDtypeStruct((slab, width), bf16)
    pieces = len(pieces_of([inner, output, w_beta], PIECE))
    return pl.pallas_call(
        functools.partial(first_gather_kernel, shards // 2),
        in_specs=in_vmem(10) + anywhere(3),
        out_specs=anywhere(5) + in_vmem(3),
        out_shape=[
            jax.ShapeDtypeStruct((shards, *inner.shape), bf16),
            jax.ShapeDtypeStruct((shards, *output.shape), bf16),
            jax.ShapeDtypeStruct((shards, *w_beta.shape), bf16),
            jax.ShapeDtypeStruct((4 * rows, model), bf16),
            jax.ShapeDtypeStruct((4 * rows, model), bf16),
            jax.ShapeDtypeStruct((slab, 2 * hidden), bf16),
            jax.ShapeDtypeStruct((slab, hidden), bf16),
            jax.ShapeDtypeStruct((rows, model), bf16),
        ],
        scratch_shapes=[
            pltpu.VMEM(inner.shape, bf16),
            pltpu.VMEM(output.shape, bf16),
            pltpu.VMEM((rows, model), bf16),
            pltpu.VMEM((slab, hidden), f32),
            pltpu.VMEM((slab, hidden), f32),
            pltpu.VMEM((hidden, slab), f32),
        ]
        + LineGather.scratch(shards // 2, pieces, 3)
        + [pltpu.SemaphoreType.DMA((6,)) for _ in range(4)]
        + [pltpu.SemaphoreType.DMA((5,))],
        compiler_params=pltpu.CompilerParams(
            collective_id=1, has_side_effects=True, vmem_limit_bytes=VMEM_LIMIT
        ),
        cost_estimate=pl.CostEstimate(flops=80_000_000_000, bytes_accessed=20_000_000, transcendentals=0),
    )(w_query, w_key, w_value, w_gate_out, w_beta, w_output, inputs, cotangent, mask, gain, w_gate, w_up, w_down)


def branch_kernel(z, weight, inputs, gain, resid, full, part, first, second, stage, low, s_send, s_recv, g_send, g_recv, local):
    scatter = PlaneScatter(part, first, second, stage, s_send, s_recv)
    gather = PlaneGather(low, full, g_send, g_recv)
    rows = scatter.rows
    slab = weight.shape[1]
    greet(tensor=scatter.across)
    greet(tensor=scatter.along)

    def compute(block):
        here = pl.ds(scatter.start_of(block, 0), rows)

        def column(index, carry):
            part[here, pl.ds(pl.multiple_of(index * slab, slab), slab)] = mm_nt(z[here, :], weight[index]).astype(bf16)
            return carry

        lax.fori_loop(0, weight.shape[0], column, 0)

    compute(scatter.far)
    wait_greetings(2)
    scatter.start_far()
    compute(scatter.across)
    scatter.start_near(0)
    compute(scatter.along)
    scatter.start_near(1)
    compute(scatter.me)
    scatter.relay(0)
    scatter.relay(1)
    for half in (0, 1):
        scatter.ready(half)

        def norm(index, carry):
            at = pl.multiple_of(index * TILE, TILE)
            here = pl.ds(pl.multiple_of(half * scatter.half + at, TILE), TILE)
            value = inputs[here, :].astype(f32) + scatter.tile(half, at)
            resid[here, :] = value
            scale = lax.rsqrt(jnp.mean(value * value, axis=-1, keepdims=True) + norm_epsilon)
            low[here, :] = (value * scale * gain[...]).astype(bf16)
            return carry

        lax.fori_loop(0, scatter.half // TILE, norm, 0)
        gather.start(half)
    keep = pltpu.make_async_copy(low, full.at[pl.ds(pl.multiple_of(gather.me * rows, rows), rows)], local.at[0])
    keep.start()
    gather.relay(0)
    gather.relay(1)
    scatter.finish()
    gather.finish()
    keep.wait()


def branch_and_norm(z, weight, inputs, gain):
    rows, model = inputs.shape
    return pl.pallas_call(
        branch_kernel,
        in_specs=in_vmem(4),
        out_specs=in_vmem(1) + anywhere(1),
        out_shape=[
            jax.ShapeDtypeStruct((rows, model), f32),
            jax.ShapeDtypeStruct((4 * rows, model), bf16),
        ],
        scratch_shapes=[pltpu.VMEM((4 * rows, model), bf16)]
        + plane_scatter_scratch(rows, model)[:3]
        + [pltpu.VMEM((rows, model), bf16)]
        + [pltpu.SemaphoreType.DMA((6,)) for _ in range(4)]
        + [pltpu.SemaphoreType.DMA((1,))],
        compiler_params=pltpu.CompilerParams(
            collective_id=2, has_side_effects=True, vmem_limit_bytes=VMEM_LIMIT
        ),
        cost_estimate=pl.CostEstimate(flops=50_000_000_000, bytes_accessed=20_000_000, transcendentals=0),
    )(z, weight, inputs, gain)


def norm_backward(value, grad, gain):
    scale = lax.rsqrt(jnp.mean(value * value, axis=-1, keepdims=True) + norm_epsilon)
    normed = value * scale
    inner = grad * gain
    return scale * (inner - normed * jnp.mean(inner * normed, axis=-1, keepdims=True)), grad * normed


class LineScatter:
    def __init__(self, chips, parts, stages, trades, arrived, sems):
        self.chips, self.parts, self.stages, self.trades, self.arrived = chips, parts, stages, trades, arrived
        self.pieces = pieces_of(parts, PIECE)
        self.right_send, self.right_receive, self.left_send, self.left_receive = sems[:4]
        self.core_send, self.core_receive, self.local = sems[4:]
        self.chip, self.core = chip_and_core()

    @staticmethod
    def scratch(chips, arrays):
        shapes = [array.shape[-2:] for array in arrays]
        pieces = len(pieces_of(arrays, PIECE))
        return (
            [pltpu.VMEM((chips, *shape), bf16) for shape in shapes]
            + [pltpu.VMEM((chips, *shape), bf16) for shape in shapes]
            + [pltpu.VMEM((chips + 1, *shape), bf16) for shape in shapes]
            + [pltpu.SemaphoreType.DMA((chips, pieces)) for _ in range(6)]
            + [pltpu.SemaphoreType.DMA((len(arrays), chips))]
        )

    def order(self):
        order = []
        for step in range(self.chips // 2):
            order += [self.chips - 1 - step, step]
        return order

    def trade(self, piece, dest):
        index, start, rows = self.pieces[piece]
        return remote(
            self.parts[index].at[dest * 2 + 1 - self.core, pl.ds(start, rows)],
            self.trades[index].at[dest, pl.ds(start, rows)],
            self.core_send.at[dest, piece],
            self.core_receive.at[dest, piece],
            dp=self.chip * 2 + 1 - self.core,
        )

    def load(self, index, dest):
        return pltpu.make_async_copy(
            self.parts[index].at[dest * 2 + self.core], self.stages[index].at[dest], self.local.at[index, dest]
        )

    def right(self, piece, dest):
        index, start, rows = self.pieces[piece]
        here = pl.ds(start, rows)
        return remote(
            self.stages[index].at[dest, here],
            self.arrived[index].at[dest, here],
            self.right_send.at[dest, piece],
            self.right_receive.at[dest, piece],
            dp=(self.chip + 1) * 2 + self.core,
        )

    def left_slot(self, dest, chip):
        return jnp.where(dest == chip, self.chips, dest)

    def left(self, piece, dest):
        index, start, rows = self.pieces[piece]
        here = pl.ds(start, rows)
        return remote(
            self.stages[index].at[dest, here],
            self.arrived[index].at[self.left_slot(dest, self.chip - 1), here],
            self.left_send.at[dest, piece],
            self.left_receive.at[dest, piece],
            dp=(self.chip - 1) * 2 + self.core,
        )

    def start(self):
        for dest in self.order():
            for index in range(len(self.parts)):
                self.load(index, dest).start()
            for piece in range(len(self.pieces)):
                self.trade(piece, dest).start()

    def add(self, piece, dest, slots, put=None):
        index, start, rows = self.pieces[piece]

        def tile(at, carry):
            here = pl.ds(pl.multiple_of(start + at * TILE, TILE), TILE)
            total = self.stages[index][dest, here, :].astype(f32) + self.trades[index][dest, here, :].astype(f32)
            for slot in slots:
                total = total + self.arrived[index][slot, here, :].astype(f32)
            if put is None:
                self.stages[index][dest, here, :] = total.astype(bf16)
            else:
                put[index](here, total)
            return carry

        lax.fori_loop(0, rows // TILE, tile, 0)

    def first_of(self, piece):
        return piece == 0 or self.pieces[piece - 1][0] != self.pieces[piece][0]

    def receive(self, piece, dest):
        if self.first_of(piece):
            self.load(self.pieces[piece][0], dest).wait()
        self.trade(piece, dest).wait_recv()

    def step(self, step, ends, turns=(0, 1)):
        to_right, to_left = self.chips - 1 - step, step

        def send_right(piece):
            self.receive(piece, to_right)
            if not ends:
                self.right(piece, to_right).wait_recv()
            self.add(piece, to_right, [] if ends else [to_right])
            self.right(piece, to_right).start()

        def send_left(piece):
            self.receive(piece, to_left)
            if not ends:
                self.left(piece, to_left).wait_recv()
            self.add(piece, to_left, [] if ends else [to_left])
            self.left(piece, to_left).start()

        count = len(self.pieces)
        if ends:
            when(self.chip == 0, lambda: [send_right(piece) for piece in range(count)] and None)
            when(self.chip == self.chips - 1, lambda: [send_left(piece) for piece in range(count)] and None)
            return
        inner_right = (self.chip > 0) & (to_right > self.chip)
        inner_left = (self.chip < self.chips - 1) & (to_left < self.chip)
        low = self.chip < self.chips // 2
        lead = 2
        for at in range(count + lead):
            early, late = at, at - lead
            if 0 in turns and early < count:
                when(low & inner_right, functools.partial(send_right, early))
                when(jnp.logical_not(low) & inner_left, functools.partial(send_left, early))
            if 1 in turns and late >= 0:
                when(low & inner_left, functools.partial(send_left, late))
                when(jnp.logical_not(low) & inner_right, functools.partial(send_right, late))

    def keep(self, outs, pieces):
        me = self.chip
        for piece in pieces:
            self.receive(piece, me)
            when(me > 0, lambda: self.right(piece, me).wait_recv())
            when(me < self.chips - 1, lambda: self.left(piece, me).wait_recv())
            when((me > 0) & (me < self.chips - 1), lambda: self.add(piece, me, [me, self.chips], outs))
            when(me == 0, lambda: self.add(piece, me, [self.chips], outs))
            when(me == self.chips - 1, lambda: self.add(piece, me, [me], outs))

    def finish(self):
        for piece in range(len(self.pieces)):
            for dest in range(self.chips):
                self.trade(piece, dest).wait_send()
                when(dest > self.chip, lambda: self.right(piece, dest).wait_send())
                when(dest < self.chip, lambda: self.left(piece, dest).wait_send())


def resid_kernel(
    chips, slab, low_far, high_far, weight_far, z_far, out_weight_far, resid, grad_out, gain, high_part,
    grad_resid, dgain, dz, output_grad, high_out,
    part, first, second, stage, low, full, total, s_send, s_recv, g_send, g_recv,
    grad_both, weight, z, out_weight, load_sems, *rest
):
    scatter = PlaneScatter(part, first, second, stage, s_send, s_recv)
    gather = PlaneGather(low, full, g_send, g_recv)
    line = LineScatter(chips, [high_part], rest[:1], rest[1:2], rest[2:3], rest[3:])
    rows = scatter.rows
    split = low_far.shape[1]
    slabs = weight.shape[0] // slab
    order = (scatter.far, scatter.across, scatter.along, scatter.me)
    greetings = greet_line(chips)
    greet(tensor=scatter.across)
    greet(tensor=scatter.along)

    def rows_loads(at):
        here = pl.ds(scatter.start_of(order[at], 0), rows)
        return [
            pltpu.make_async_copy(far.at[here], grad_both.at[here, lanes], load_sems.at[slabs + 2 * at + which])
            for which, (far, lanes) in enumerate(
                ((low_far, pl.ds(0, split)), (high_far, pl.ds(split, grad_both.shape[1] - split)))
            )
        ]

    def slab_load(index):
        here = pl.ds(pl.multiple_of(index * slab, slab), slab)
        return pltpu.make_async_copy(weight_far.at[here], weight.at[here], load_sems.at[index])

    late_loads = [
        pltpu.make_async_copy(z_far, z, load_sems.at[slabs + 8]),
        pltpu.make_async_copy(out_weight_far, out_weight, load_sems.at[slabs + 9]),
    ]
    for at in range(4):
        for load in rows_loads(at):
            load.start()
        if at == 0:
            for index in range(slabs):
                slab_load(index).start()
    for load in late_loads:
        load.start()

    def compute(at):
        here = pl.ds(scatter.start_of(order[at], 0), rows)
        for load in rows_loads(at):
            load.wait()

        def column(index, carry):
            lanes = pl.ds(pl.multiple_of(index * slab, slab), slab)
            if at == 0:
                slab_load(index).wait()
            part[here, lanes] = mm_nt(grad_both[here, :], weight[lanes, :]).astype(bf16)
            return carry

        lax.fori_loop(0, slabs, column, 0)

    compute(0)
    wait_greetings(2 + greetings)
    scatter.start_far()
    line.start()
    compute(1)
    scatter.start_near(0)
    compute(2)
    scatter.start_near(1)
    line.step(0, True)
    compute(3)
    dgain[...] = jnp.zeros_like(dgain)
    scatter.relay(0)
    scatter.relay(1)
    for step in range(1, chips - 1):
        line.step(step, True)
    for half in (0, 1):
        scatter.ready(half)

        def norm(index, carry):
            at = pl.multiple_of(index * TILE, TILE)
            here = pl.ds(pl.multiple_of(half * scatter.half + at, TILE), TILE)
            back, gain_part = norm_backward(resid[here, :], scatter.tile(half, at), gain[...])
            value = grad_out[here, :].astype(f32) + back
            grad_resid[here, :] = value
            low[here, :] = value.astype(bf16)
            dgain[...] += jnp.sum(gain_part, axis=0, keepdims=True)
            return carry

        lax.fori_loop(0, scatter.half // TILE, norm, 0)
        gather.start(half)
        if half == 0:
            line.step(0, False, (0,))
    for load in late_loads:
        load.wait()

    def use(block, left, fresh=False):
        here = pl.ds(pl.multiple_of(block * rows, rows), rows)
        dz[here, :] = mm(left[...], out_weight[...]).astype(bf16)

        def column(index, carry):
            lanes = pl.ds(pl.multiple_of(index * slab, slab), slab)
            product = mm_tn(left[:, lanes], z[here, :])
            total[lanes, :] = product if fresh else total[lanes, :] + product
            return carry

        lax.fori_loop(0, slabs, column, 0)

    def block_of(block):
        return full.at[pl.ds(pl.multiple_of(block * rows, rows), rows)]

    gather.relay(0)
    gather.relay(1)
    line.step(0, False, (1,))
    for step in range(1, chips - 1):
        line.step(step, False)
    use(scatter.me, low, True)
    gather.near(0)
    use(scatter.across, block_of(scatter.across))
    gather.near(1)
    use(scatter.along, block_of(scatter.along))

    def put(here, total):
        high_out[here, :] = total

    line.keep([put], range(len(line.pieces)))
    gather.diagonal()
    use(scatter.far, block_of(scatter.far))
    output_grad[...] = total[...].astype(bf16)
    gather.sent()
    scatter.finish()
    line.finish()


def resid_backward(grad_low, grad_high, weight, z, out_weight, resid, grad_out, gain, high_part):
    chips = lax.axis_size("dp") // 2
    rows, model = resid.shape
    width = z.shape[1]
    slab, columns = high_part.shape[1:]
    return pl.pallas_call(
        functools.partial(resid_kernel, chips, 256),
        in_specs=anywhere(5) + in_vmem(3) + anywhere(1),
        out_specs=in_vmem(5),
        out_shape=[
            jax.ShapeDtypeStruct((rows, model), f32),
            jax.ShapeDtypeStruct((1, model), f32),
            jax.ShapeDtypeStruct((4 * rows, width), bf16),
            jax.ShapeDtypeStruct((model, width), bf16),
            jax.ShapeDtypeStruct((slab, columns), f32),
        ],
        scratch_shapes=[pltpu.VMEM((4 * rows, model), bf16)]
        + plane_scatter_scratch(rows, model)[:3]
        + [
            pltpu.VMEM((rows, model), bf16),
            pltpu.VMEM((4 * rows, model), bf16),
            pltpu.VMEM((model, width), f32),
        ]
        + [pltpu.SemaphoreType.DMA((6,)) for _ in range(4)]
        + [
            pltpu.VMEM((4 * rows, weight.shape[1]), bf16),
            pltpu.VMEM(weight.shape, bf16),
            pltpu.VMEM(z.shape, bf16),
            pltpu.VMEM(out_weight.shape, bf16),
            pltpu.SemaphoreType.DMA((model // 256 + 10,)),
        ]
        + LineScatter.scratch(chips, [high_part]),
        compiler_params=pltpu.CompilerParams(
            collective_id=3, has_side_effects=True, vmem_limit_bytes=LARGE_LIMIT
        ),
        cost_estimate=pl.CostEstimate(flops=1_000_000, bytes_accessed=1_000_000, transcendentals=0),
    )(grad_low, grad_high, weight, z, out_weight, resid, grad_out, gain, high_part)


SMALL = 512


def last_kernel(chips, *refs):
    inner_part, output_part, weight, inner, dpre_far, middle_far, inputs_far, grad_resid_far, resid_far = refs[:9]
    mask, first_gain, ffn_dgain, head_dgain, dtaps, dbeta, beta, beta_part = refs[9:17]
    refs = refs[3:]
    query_out, key_out, value_out, gate_out, beta_out, output_out, input_grad, out = refs[14:22]
    first_out, ffn_out, head_out, taps_out = refs[22:26]
    refs = refs[26:]
    line = LineScatter(chips, [inner_part, output_part], refs[:2], refs[2:4], refs[4:6], refs[6:13])
    grad = PlaneScatter(*refs[13:19])
    ffn = PlaneScatter(*refs[19:25])
    turned, small, near, lined, dgain, small_send, small_receive, inner_slabs, down_slabs, slab_sems = refs[25:35]
    dpre, middle, inputs, grad_resid, resid, load_sems = refs[35:41]
    chip, core = line.chip, line.core
    slab = inner_part.shape[1]
    shards = 2 * chips
    sibling = chip * 2 + 1 - core
    greet(tensor=grad.across)
    greet(tensor=grad.along)
    greet(dp=sibling)
    for other in range(1, chips):
        greet(dp=lax.rem(chip + other, chips) * 2 + core)

    def stream(at, source, buffers, kind):
        return pltpu.make_async_copy(source.at[at], buffers.at[lax.rem(at, 2)], slab_sems.at[kind, lax.rem(at, 2)])

    rows = inputs.shape[0]

    def product(left, source, buffers, each, kind, mine, extra=None):
        pair = each.me // 2
        here = pl.ds(pl.multiple_of((pair if mine else 1 - pair) * 2 * rows, 2 * rows), 2 * rows)

        def column(index, carry):
            def following():
                stream(lax.rem(index + 1, shards), source, buffers, kind).start()

            when(index < (shards - 1 if mine else shards), following)
            stream(index, source, buffers, kind).wait()
            total = mm_nt(left[here, :], buffers[lax.rem(index, 2)])
            if extra is not None:
                total = total + mm(extra[0][here, :], extra[1][index])
            each.part[here, pl.ds(pl.multiple_of(index * slab, slab), slab)] = total.astype(bf16)
            return carry

        lax.fori_loop(0, shards, column, 0)

    loads = [
        pltpu.make_async_copy(source, target, load_sems.at[at])
        for at, (source, target) in enumerate(
            (
                (dpre_far, dpre),
                (middle_far, middle),
                (inputs_far, inputs),
                (grad_resid_far, grad_resid),
                (resid_far, resid),
            )
        )
    ]
    wait_greetings(2 + chips)
    line.start()
    for load in loads[:2]:
        load.start()
    stream(0, inner, inner_slabs, 0).start()
    stream(0, weight, down_slabs, 1).start()
    for load in loads[2:]:
        load.start()
    dgain[...] = jnp.zeros_like(dgain)
    small[...] = jnp.zeros_like(small)
    line.step(0, True)
    loads[0].wait()
    product(dpre, inner, inner_slabs, grad, 0, False, (dbeta, beta))
    grad.start_far()
    grad.start_near(1)
    line.step(1, True)
    product(dpre, inner, inner_slabs, grad, 0, True, (dbeta, beta))
    grad.start_near(0)
    line.step(0, False, (0,))
    loads[1].wait()
    product(middle, weight, down_slabs, ffn, 1, False)
    for step in range(2, chips - 1):
        line.step(step, True)
    grad.relay(0)
    grad.relay(1)
    ffn.start_far()
    ffn.start_near(1)
    product(middle, weight, down_slabs, ffn, 1, True)
    ffn.start_near(0)
    line.step(0, False, (1,))
    for step in range(1, chips - 1):
        line.step(step, False)
    for load in loads[2:]:
        load.wait()
    for half in (0, 1):
        grad.ready(half)

        def norm(index, carry):
            at = pl.multiple_of(index * TILE, TILE)
            here = pl.ds(pl.multiple_of(half * grad.half + at, TILE), TILE)
            back, gain_part = norm_backward(inputs[here, :].astype(f32), grad.tile(half, at), first_gain[...])
            input_grad[here, :] = grad_resid[here, :] + back
            dgain[...] += jnp.sum(gain_part, axis=0, keepdims=True)
            return carry

        lax.fori_loop(0, grad.half // TILE, norm, 0)
    model = dgain.shape[1]
    count = model // SMALL
    for row in range(count):
        lanes = slice(row * SMALL, (row + 1) * SMALL)
        small[0, row : row + 1, :] = dgain[:, lanes]
        small[0, count + row : count + row + 1, :] = ffn_dgain[:, lanes]
    small[0, 2 * count : 2 * count + 1, 0:HEAD] = head_dgain[...]
    small[0, 16 : 16 + 3 * TAPS, :] = dtaps[...]
    heads = beta_out.shape[0]
    for head in range(heads):
        for row in range(count):
            at = 32 + head * count + row
            small[0, at : at + 1, :] = beta_part[head : head + 1, row * SMALL : (row + 1) * SMALL]

    def hop(at):
        where = (dict(tensor=grad.across), dict(tensor=grad.along), dict(dp=sibling))[at]
        return remote(small.at[at], near.at[at], small_send.at[at], small_receive.at[at], **where)

    def hopped(at):
        hop(at).wait()
        if at < 2:
            small[at + 1, 0:16, :] = small[at, 0:16, :] + near[at, 0:16, :]
            small[at + 1, 16:, :] = small[at, 16:, :]
        else:
            small[3] = small[2] + near[2]

    def tell(other):
        to = lax.rem(chip + other, chips)
        return remote(
            small.at[3], lined.at[chip], small_send.at[2 + other], small_receive.at[2 + other], dp=to * 2 + core
        )

    def put_inner(here, total):
        width = query_out.shape[1]
        for kind, target in enumerate((query_out, key_out, value_out, gate_out)):
            target[here, :] = total[:, kind * width : (kind + 1) * width]

    def put_output(here, total):
        turned[here, :] = total

    puts = [put_inner, put_output]
    hop(0).start()
    ffn.relay(0)
    ffn.relay(1)
    hopped(0)
    hop(1).start()
    pieces = len(line.pieces)
    line.keep(puts, range(0, pieces - 3))
    hopped(1)
    hop(2).start()
    for half in (0, 1):
        ffn.ready(half)

        def finish_rows(index, carry):
            at = pl.multiple_of(index * TILE, TILE)
            here = pl.ds(pl.multiple_of(half * ffn.half + at, TILE), TILE)
            out[here, :] = ((resid[here, :] + ffn.tile(half, at)) * mask[here, :]).astype(bf16)
            return carry

        lax.fori_loop(0, ffn.half // TILE, finish_rows, 0)
    hopped(2)
    lined[chip] = small[3]
    for other in range(1, chips):
        tell(other).start()
    line.keep(puts, range(pieces - 3, pieces))
    output_out[...] = jnp.transpose(turned[...])
    for other in range(1, chips):
        tell(other).wait()
    total = lined[0]
    for other in range(1, chips):
        total = total + lined[other]
    for row in range(count):
        lanes = slice(row * SMALL, (row + 1) * SMALL)
        first_out[:, lanes] = total[row : row + 1, :]
        ffn_out[:, lanes] = total[count + row : count + row + 1, :]
    head_out[...] = total[2 * count : 2 * count + 1, 0:HEAD]
    summed = small.at[0]
    summed[...] = total
    mine = (chip * 2 + core) * slab
    lanes = pl.ds(pl.multiple_of(lax.rem(mine, SMALL), slab), slab)
    for head in range(heads):
        beta_out[head : head + 1, :] = summed[pl.ds(32 + head * count + mine // SMALL, 1), lanes]
    for kind in range(3):
        taps_out[kind] = total[16 + kind * TAPS : 16 + (kind + 1) * TAPS, :]
    grad.finish()
    ffn.finish()
    line.finish()


def last_scatter(
    inner_part, output_part, weight, inner, dpre, middle, inputs, grad_resid, resid, mask, gain, ffn_dgain, head_dgain, dtaps,
    dbeta, beta, beta_part
):
    chips = lax.axis_size("dp") // 2
    rows, model = inputs.shape
    slab, width = output_part.shape[1:]
    arrays = [inner_part, output_part]
    shape = jax.ShapeDtypeStruct
    return pl.pallas_call(
        functools.partial(last_kernel, chips),
        in_specs=anywhere(9) + in_vmem(8),
        out_specs=in_vmem(12),
        out_shape=[shape((slab, width), f32)] * 4
        + [
            shape((width // HEAD, slab), f32),
            shape((width, slab), f32),
            shape((rows, model), f32),
            shape((rows, model), bf16),
            shape((1, model), f32),
            shape((1, model), f32),
            shape((1, HEAD), f32),
            shape((3, TAPS, dtaps.shape[1]), f32),
        ],
        scratch_shapes=LineScatter.scratch(chips, arrays)
        + [pltpu.VMEM((4 * rows, model), bf16)]
        + plane_scatter_scratch(rows, model)
        + [pltpu.VMEM((4 * rows, model), bf16)]
        + plane_scatter_scratch(rows, model)
        + [
            pltpu.VMEM((slab, width), f32),
            pltpu.VMEM((4, 48, SMALL), f32),
            pltpu.VMEM((3, 48, SMALL), f32),
            pltpu.VMEM((chips, 48, SMALL), f32),
            pltpu.VMEM((1, model), f32),
            pltpu.SemaphoreType.DMA((2 + chips,)),
            pltpu.SemaphoreType.DMA((2 + chips,)),
            pltpu.VMEM((2, *inner.shape[1:]), bf16),
            pltpu.VMEM((2, *weight.shape[1:]), bf16),
            pltpu.SemaphoreType.DMA((2, 2)),
            pltpu.VMEM(dpre.shape, bf16),
            pltpu.VMEM(middle.shape, bf16),
            pltpu.VMEM((rows, model), bf16),
            pltpu.VMEM((rows, model), f32),
            pltpu.VMEM((rows, model), f32),
            pltpu.SemaphoreType.DMA((5,)),
        ],
        compiler_params=pltpu.CompilerParams(
            collective_id=4, has_side_effects=True, vmem_limit_bytes=LARGE_LIMIT
        ),
        cost_estimate=pl.CostEstimate(flops=1_000_000, bytes_accessed=1_000_000, transcendentals=0),
    )(inner_part, output_part, weight, inner, dpre, middle, inputs, grad_resid, resid, mask, gain, ffn_dgain, head_dgain, dtaps, dbeta, beta, beta_part)


def rms_norm(values, gain):
    return (
        values * lax.rsqrt(jnp.mean(values * values, axis=-1, keepdims=True) + norm_epsilon) * gain
    )


def gather(values, axis):
    return lax.all_gather(values, axis, axis=0, tiled=True)


def scatter(values, axis):
    return lax.psum_scatter(values, axis, scatter_dimension=0, tiled=True)


def plain_first_gather(
    w_query, w_key, w_value, w_gate_out, w_beta, w_output, inputs, cotangent, mask, gain, w_gate, w_up, w_down
):
    shards = lax.axis_size("dp")
    inner = jnp.concatenate([w_query, w_key, w_value, w_gate_out], axis=1).astype(bf16)
    output = w_output.T.astype(bf16)
    grad = (cotangent.astype(f32) * mask).astype(bf16)
    return (
        gather(inner, "dp").reshape(shards, *inner.shape),
        gather(output, "dp").reshape(shards, *output.shape),
        gather(w_beta, "dp").reshape(shards, *w_beta.shape),
        gather(rms_norm(inputs.astype(f32), gain[0]).astype(bf16), "tensor"),
        gather(grad, "tensor"),
        jnp.concatenate([w_gate, w_up], axis=1).astype(bf16),
        w_down.T.astype(bf16),
        grad,
    )


def plain_branch_and_norm(z, weight, inputs, gain):
    branch = mm_nt(z, weight.reshape(-1, z.shape[1])).astype(bf16)
    resid = inputs.astype(f32) + scatter(branch, "tensor").astype(f32)
    return resid, gather(rms_norm(resid, gain[0]).astype(bf16), "tensor")


def plain_resid_backward(grad_low, grad_high, weight, z, out_weight, resid, grad_out, gain, high_part):
    part = mm_nt(jnp.concatenate([grad_low, grad_high], axis=1), weight).astype(bf16)
    back, gain_part = norm_backward(resid, scatter(part, "tensor").astype(f32), gain)
    value = grad_out.astype(f32) + back
    full = gather(value.astype(bf16), "tensor")
    high = scatter(high_part.reshape(-1, high_part.shape[2]), "dp").astype(f32)
    dgain = jnp.sum(gain_part, axis=0, keepdims=True)
    return value, dgain, mm(full, out_weight).astype(bf16), mm_tn(full, z).astype(bf16), high


def plain_last_scatter(
    inner_part, output_part, weight, inner, dpre, middle, inputs, grad_resid, resid, mask, gain, ffn_dgain, head_dgain, dtaps,
    dbeta, beta, beta_part
):
    beta = beta.transpose(1, 0, 2).reshape(BETA_PAD, -1)
    grad_part = (mm_nt(dpre, inner.reshape(-1, inner.shape[2])) + mm(dbeta, beta)).astype(bf16)
    slab = inner_part.shape[1]
    beta_total = lax.psum(beta_part[: output_part.shape[2] // HEAD], "dp")
    beta_total = lax.dynamic_slice_in_dim(beta_total, lax.axis_index("dp") * slab, slab, axis=1)
    inner, output = (
        scatter(part.reshape(-1, part.shape[-1]), "dp").astype(f32) for part in (inner_part, output_part)
    )
    width = output.shape[1]
    back, gain_part = norm_backward(inputs.astype(f32), scatter(grad_part, "tensor").astype(f32), gain)
    ffn_part = mm_nt(middle, weight.reshape(-1, weight.shape[2])).astype(bf16)
    out = ((resid + scatter(ffn_part, "tensor").astype(f32)) * mask).astype(bf16)
    gains = (jnp.sum(gain_part, axis=0, keepdims=True), ffn_dgain, head_dgain)
    return (
        *(inner[:, kind * width : (kind + 1) * width] for kind in range(4)),
        beta_total,
        output.T,
        grad_resid + back,
        out,
        *lax.psum(gains, ("dp", "tensor")),
        lax.psum(dtaps, "dp").reshape(3, TAPS, -1),
    )


def body(
    inputs,
    cotangent,
    lengths,
    norm_gain,
    w_query,
    w_key,
    w_value,
    w_gate_out,
    w_beta,
    conv_weight,
    out_norm_gain,
    w_output,
    ffn_norm_gain,
    w_gate,
    w_up,
    w_down,
):
    tensor_count = lax.axis_size("tensor")
    shards = lax.axis_size("dp")
    kernels = tensor_count == 4 and shards == 8
    rows, model = inputs.shape
    length = rows * tensor_count
    width = w_query.shape[1]
    heads = width // HEAD
    hidden = w_gate.shape[1]
    slab = w_query.shape[0]
    taps = conv_weight.reshape(3 * TAPS, width)
    first_gain, head_gain = norm_gain.reshape(1, model), out_norm_gain.reshape(1, HEAD)
    ffn_gain = ffn_norm_gain.reshape(1, model)

    positions = lax.axis_index("tensor") * rows + jnp.arange(rows, dtype=jnp.int32)
    mask = (positions < lengths[0]).astype(f32)[:, None]
    beta_rows = jnp.pad(w_beta.T, ((0, BETA_PAD - w_beta.shape[1]), (0, 0))).astype(bf16)
    inner, full_output, full_beta, normed, grad_full, gate_up, down, grad_out = (
        first_gather if kernels else plain_first_gather
    )(w_query, w_key, w_value, w_gate_out, beta_rows, w_output, inputs, cotangent, mask, first_gain, w_gate, w_up, w_down)
    gate_up = gather(gate_up, "dp")
    down = gather(down, "dp")

    pre = jnp.dot(normed, inner.reshape(model, -1), preferred_element_type=f32).astype(bf16)
    beta_pre = mm_nt(normed, full_beta.transpose(1, 0, 2).reshape(BETA_PAD, model))
    z, conv, mixed, inverse, states = mixer_forward(pre, beta_pre, taps, head_gain, heads)
    resid, normed2 = (branch_and_norm if kernels else plain_branch_and_norm)(z, full_output, inputs, ffn_gain)
    middle, slopes = (ffn if kernels else plain_ffn)(normed2, gate_up)
    down_part = mm_tn(grad_full, middle).astype(bf16)
    down, down_part = lax.optimization_barrier((down, down_part))
    down_total = scatter(down_part, "dp")
    grad_low, grad_high = (ffn_backward if kernels else plain_ffn_backward)(grad_full, down, slopes)
    low_part, high_part = mm_tn(normed2, grad_low).astype(bf16), mm_tn(normed2, grad_high).astype(bf16)
    grad_low, grad_high, low_part = lax.optimization_barrier((grad_low, grad_high, low_part))
    low_total = scatter(low_part, "dp")
    grad_resid, ffn_dgain, dz, output_grad, high_total = (resid_backward if kernels else plain_resid_backward)(
        grad_low,
        grad_high,
        gate_up,
        z,
        full_output.reshape(model, width),
        resid,
        grad_out,
        ffn_gain,
        high_part.reshape(shards, slab, -1),
    )
    dpre, dbeta, beta_part, dtaps, head_dgain = mixer_backward(
        pre, beta_pre, normed, conv, mixed, dz, inverse, states, taps, head_gain, heads
    )
    output_grad = output_grad.reshape(shards, slab, width)
    inner_grad = mm_tn(normed, dpre).astype(bf16).reshape(shards, slab, -1)
    results = (last_scatter if kernels else plain_last_scatter)(
        inner_grad,
        output_grad,
        down.reshape(shards, slab, hidden),
        inner,
        dpre,
        middle,
        inputs,
        grad_resid,
        resid,
        mask,
        first_gain,
        ffn_dgain,
        head_dgain,
        dtaps,
        dbeta,
        full_beta,
        beta_part,
    )
    gate_total, up_total, down_total, *results = (finish if kernels else plain_finish)(
        low_total, high_total, down_total, results
    )
    query_total, key_total, value_total, gate_out_total, beta_total, output_total, input_grad, output = results[:8]
    first_total, ffn_total, head_total, taps_total = results[8:]
    return (
        output,
        input_grad,
        first_total[0],
        query_total,
        key_total,
        value_total,
        gate_out_total,
        beta_total.T,
        taps_total,
        head_total[0],
        output_total,
        ffn_total[0],
        gate_total,
        up_total,
        down_total,
    )


def solution(mesh):
    rows = P(("dp", "tensor"), None)
    split = P("dp", "tensor")
    turned = P("tensor", "dp")
    taps = P(None, None, "tensor")
    return jax.shard_map(
        body,
        mesh=mesh,
        in_specs=(rows, rows, P("dp"), P(), split, split, split, split, split, taps, P(), turned, P(), split, split, turned),
        out_specs=(rows, rows, P(), split, split, split, split, split, taps, P(), turned, P(), split, split, turned),
        check_vma=False,
    )
```
